32 devices in a mesh: section: 4 (over y, x), tm: 2 (over core), mp: 4 (over z).
Axes of the slice: x: 2, y: 2, z: 4, core: 2. Of those that a mesh axis runs over, the one named last changes fastest.
Arguments:
- audio: bfloat16 [4096, 1536], P(('section', 'tm')), may hold values from -16 to 16
- lengths: int32 [4, 4], P('section'), may hold values from 1 to 512, 1024 in all within a row
- conv_kernel: float32 [31, 1536], replicated, may hold values from -1 to 1
- w_qkv: bfloat16 [1536, 3, 1536], P(None, None, 'mp'), may hold values from -6 to 6
- w_out: bfloat16 [1536, 1536], P('mp'), may hold values from -0.15625 to 0.15625
- place: int32 [1024, 1], P(('section', 'tm')), may hold values from 0 to 7; in each aligned block of 128 rows (0 to 127, 128 to 255, ...) at most 32 rows name the same one
- w_adapt: bfloat16 [1536, 5120], P(None, 'mp'), may hold values from -0.15625 to 0.15625
Outputs:
- dec_in: bfloat16 [2048, 5120], P(('section', 'tm'), 'mp')
The draws below stay inside these ranges and needn't reach their ends.
Inputs may be any that keep to these rules, and one draw needn't show every extreme that they name: `lengths`: each row sums to 1024; its largest entry is exactly 512. `place`: among the 128 rows of one device no value appears more than 32 times, and some value appears exactly 32 times.
All inputs are finite; a program needn't handle non-finite values.
Results may differ from the reference program's by a relative error of at most 0.011.
Values may be sent and summed in bfloat16 or wider, within the bound.
No kernel may reach another device: no remote copies, remote signals or barrier semaphores. Data moves between devices by JAX's collectives and lax.ppermute only.
A program may use at most 128 MiB of HBM per device.

```python
import math
import jax
import jax.numpy as jnp
import numpy as np
from jax import lax

DE = 1536
HE = 16
HDE = 96
D = 5120
KER = 31
STRIDE = 4
RECS = 4
FR_DEV = 512
FRAMES = 1024
ALL_FRAMES = 4096
POOL_DEV = 128
POOLED = 1024
CAP = 32
SLOTS = 2048
N_SECTION = 4
N_TM = 2


def draw_audio(key, part):
    key = jax.random.fold_in(key, 11)
    subkeys = jax.random.split(key, 1)
    return jnp.clip(jax.random.normal(subkeys[0], (ALL_FRAMES, DE), jnp.float32), -6.0, 6.0).astype(jnp.bfloat16)


def draw_w_qkv(key, part):
    key = jax.random.fold_in(key, 23)
    subkeys = jax.random.split(key, 1)
    width = HE * HDE
    return (jnp.clip(jax.random.normal(subkeys[0], (DE, 3, width), jnp.float32), -6.0, 6.0) * DE ** (-0.5)).astype(jnp.bfloat16)


def block_levels(stream_key, extent, pieces, low, high):
    loudness, own = 1.0, jax.random.fold_in(stream_key, 6)
    for dim, parts in pieces:
        heights = jnp.exp(jax.random.uniform(jax.random.fold_in(own, dim), (parts,), jnp.float32, low / len(pieces), high / len(pieces)))
        loudness = loudness * jnp.repeat(heights, extent[dim] // parts).reshape([-1 if axis == dim else 1 for axis in range(len(extent))])
    return loudness


def split_up(count, total, bound, slope):
    weights = [(1 << 20) // math.isqrt(standing ** slope) + 1 for standing in range(2, count + 1)]
    spare, given = total - bound - (count - 1), [1] * (count - 1)
    while spare > 0:
        movable = [i for i in range(count - 1) if given[i] < bound]
        pool, remaining = sum([weights[i] for i in movable]), spare
        for i in movable:
            addition = min(bound - given[i], max(1, remaining * weights[i] // pool), spare)
            given[i] = given[i] + addition
            spare = spare - addition
    return np.array([bound] + given)


def uneven(stream_key, count, total, limit, lean):
    if count == 2:
        one = jax.random.randint(stream_key, (), max(1, total - limit), min(limit, total - 1) + 1)
        return jnp.stack([one, total - one])
    sizes = jnp.asarray(split_up(count, total, limit, lean), jnp.int32)
    twos = (count - 1) // 2
    source_of, receiver = sizes[1:1 + 2 * twos:2], sizes[2:2 + 2 * twos:2]
    slack = jnp.minimum(source_of - 1, limit - receiver)
    shifted = jax.random.randint(jax.random.fold_in(stream_key, 1), (twos,), 0, 1 << 20) % (slack + 1)
    sizes = sizes.at[1:1 + 2 * twos:2].set(source_of - shifted).at[2:2 + 2 * twos:2].set(receiver + shifted)
    return sizes[jax.random.permutation(jax.random.fold_in(stream_key, 2), count)]


def deal_out(stream_key, own, number, rows, count, top, bound, slope):
    ranking = jax.random.permutation(stream_key, count)
    heavy_load, usual = portions_of(count, rows * top, bound, slope, True), portions_of(count, rows * top, bound, slope, False)
    places = jnp.arange(count)

    def named(sizes, turn):
        used = int((sizes > 0).sum())
        fixed = max(1, used // 4)
        passed = fixed + (places - fixed + turn * (used - fixed)) % max(1, count - fixed)
        return jnp.zeros((count,), jnp.int32).at[ranking[jnp.where(places < fixed, places, passed)]].set(jnp.asarray(sizes, jnp.int32))

    sizes = jnp.where(number % 4 == 0, named(heavy_load, number // 4), named(usual, number - number // 4 - 1))
    mixed = jax.random.permutation(jax.random.fold_in(own, 3), count)
    donor, taker = mixed[0:count // 2 * 2:2], mixed[1:count // 2 * 2:2]
    margin = jnp.minimum(sizes[donor] - 1, bound - sizes[taker]) // 2
    margin = jnp.where((donor == ranking[0]) | (taker == ranking[0]) | (sizes[taker] == 0), 0, jnp.maximum(margin, 0))
    passed = jax.random.randint(jax.random.fold_in(own, 4), (count // 2,), 0, 1 << 20) % (margin + 1)
    sizes = sizes.at[donor].add(-passed).at[taker].add(passed)
    labels = jnp.searchsorted(jnp.cumsum(sizes), jnp.arange(rows * top), side="right").astype(jnp.int32)
    grid = labels.reshape(top, rows).T
    grid = grid[jax.random.permutation(jax.random.fold_in(own, 1), rows)]
    turn = jax.random.randint(jax.random.fold_in(own, 2), (rows, 1), 0, top)
    return jnp.take_along_axis(grid, (jnp.arange(top)[None, :] + turn) % top, axis=1)


def portions_of(amount, total, limit, skew, full):
    loads = [(1 << 20) // math.isqrt(rank ** skew) + 1 for rank in range(1, amount + 1)]
    largest = limit if full else min(limit, max(-(-total // amount), total * loads[0] // sum(loads)))
    least = 1 if total - largest >= amount - 1 else 0
    given, rest = [largest] + [least] * (amount - 1), total - largest - least * (amount - 1)
    while rest > 0:
        candidates = [i for i in range(1, amount) if given[i] < largest] or [i for i in range(1, amount) if given[i] < limit]
        pool, budget = sum([loads[i] for i in candidates]), rest
        for i in candidates:
            extra = min(limit - given[i], max(1, budget * loads[i] // pool), rest)
            given[i] = given[i] + extra
            rest = rest - extra
    return np.array(given)


def gaussian(own_key, shape, scale, reach, shards=(), kind=jnp.bfloat16):
    drawn = scale * jax.random.normal(own_key, shape, jnp.float32)
    if shards:
        drawn = drawn * block_levels(own_key, shape, shards, -0.22, 0.18)
    return jnp.clip(drawn, -reach, reach).astype(kind)


def setup_inputs(seed: int = 0) -> dict:
    splits = jax.random.split(jax.random.key(seed), 8)
    audio = draw_audio(jax.random.fold_in(splits[7], 71), 0)
    lengths = jax.vmap(lambda own: uneven(own, RECS, FRAMES, FRAMES // 2, 2))(jax.random.split(splits[1], N_SECTION)).reshape((N_SECTION, RECS)).astype(jnp.int32)
    conv_kernel = gaussian(splits[2], (KER, DE), KER ** -0.5, 1.0, (), jnp.float32)
    w_qkv = draw_w_qkv(jax.random.fold_in(splits[7], 71), 0)
    w_out = gaussian(splits[4], (HE * HDE, DE), (HE * HDE) ** -0.5, 0.15625, ((0, 4),))
    place_keys = jax.random.split(jax.random.fold_in(splits[5], 1), POOLED // POOL_DEV)
    place_turns = jax.random.permutation(jax.random.fold_in(splits[5], 3), POOLED // POOL_DEV)
    place = jax.vmap(lambda own, number: deal_out(jax.random.fold_in(splits[5], 2), own, number, POOL_DEV, N_SECTION * N_TM, 1, CAP, 2))(place_keys, place_turns).reshape((POOLED, 1))
    w_adapt = gaussian(splits[6], (DE, D), DE ** -0.5, 0.15625, ((1, 4),))
    return dict(audio=audio, lengths=lengths, conv_kernel=conv_kernel, w_qkv=w_qkv, w_out=w_out, place=place, w_adapt=w_adapt)


def layer_normed(input_rows):
    values = input_rows.astype(jnp.float32)
    centre = lax.optimization_barrier(jnp.mean(values, -1, keepdims=True))
    centred = values - centre
    spread = lax.optimization_barrier(jnp.mean(centred * centred, -1, keepdims=True))
    return (centred * lax.rsqrt(spread + 1e-05)).astype(jnp.bfloat16)

def recording_of(lengths_row, positions):
    bounds = jnp.cumsum(lengths_row).astype(jnp.int32)
    inside = (positions >= 0) & (positions < FRAMES)
    counted = lax.optimization_barrier(jnp.sum((positions[:, None] >= bounds[None, :]).astype(jnp.int32), axis=1))
    return jnp.where(inside, counted, -1)

def attend_group(queries, key_rows, value_rows, own_ids):
    score_scale = HDE ** (-0.5)
    query_blocks = queries.reshape(N_TM, FR_DEV, HE, HDE)
    id_blocks = own_ids.reshape(N_TM, FR_DEV)
    key_heads = key_rows.reshape(FRAMES, HE, HDE).astype(jnp.float32)
    value_heads = value_rows.reshape(FRAMES, HE, HDE).astype(jnp.float32)

    def one_block(block_item):
        query_block, query_ids = block_item
        scores = jnp.einsum('qhd,khd->hqk', query_block.astype(jnp.float32), key_heads, precision=lax.Precision.HIGHEST) * score_scale
        allowed = query_ids[:, None] == own_ids[None, :]
        scores = jnp.where(allowed[None], scores, -1e+30)
        score_peak = lax.optimization_barrier(jnp.max(scores, axis=-1, keepdims=True))
        weights = jnp.exp(scores - score_peak)
        weight_sum = lax.optimization_barrier(jnp.sum(weights, axis=-1))
        low_weights = weights.astype(jnp.bfloat16).astype(jnp.float32)
        gathered = jnp.einsum('hqk,khd->hqd', low_weights, value_heads, precision=lax.Precision.HIGHEST)
        return jnp.transpose(gathered / weight_sum[:, :, None], (1, 0, 2))
    return lax.map(one_block, (query_blocks, id_blocks)).reshape(FRAMES, HE * HDE)

def reference(audio, lengths, conv_kernel, w_qkv, w_out, place, w_adapt):
    conv_reach = KER // 2
    positions = jnp.arange(-conv_reach, FRAMES + conv_reach, dtype=jnp.int32)
    encoded = []
    for group_index in range(N_SECTION):
        frames = audio[group_index * FRAMES:(group_index + 1) * FRAMES]
        window_ids = recording_of(lengths[group_index], positions)
        own_ids = window_ids[conv_reach:conv_reach + FRAMES]
        widened = jnp.pad(frames.astype(jnp.float32), ((conv_reach, conv_reach), (0, 0)))
        depthwise = jnp.zeros((FRAMES, DE), jnp.float32)
        for tap_index in range(KER):
            keep_mask = (window_ids[tap_index:tap_index + FRAMES] == own_ids).astype(jnp.float32)
            depthwise = depthwise + conv_kernel[tap_index] * widened[tap_index:tap_index + FRAMES] * keep_mask[:, None]
        mixed_rows = (frames.astype(jnp.float32) + jax.nn.silu(depthwise)).astype(jnp.bfloat16)
        normed = layer_normed(mixed_rows)
        queries = jnp.dot(normed, w_qkv[:, 0, :], preferred_element_type=jnp.float32).astype(jnp.bfloat16)
        key_rows = jnp.dot(normed, w_qkv[:, 1, :], preferred_element_type=jnp.float32).astype(jnp.bfloat16)
        value_rows = jnp.dot(normed, w_qkv[:, 2, :], preferred_element_type=jnp.float32).astype(jnp.bfloat16)
        attended = attend_group(queries, key_rows, value_rows, own_ids).astype(jnp.bfloat16)
        projected_heads = jnp.dot(attended, w_out, preferred_element_type=jnp.float32)
        encoded.append((projected_heads + mixed_rows.astype(jnp.float32)).astype(jnp.bfloat16))
    encoded = jnp.concatenate(encoded, 0)
    pooled = lax.optimization_barrier(jnp.mean(encoded.astype(jnp.float32).reshape(POOLED, STRIDE, DE), axis=1)).astype(jnp.bfloat16)
    device_count = N_SECTION * N_TM
    targets = place[:, 0].reshape(device_count, POOL_DEV)
    matches = targets[:, :, None] == targets[:, None, :]
    row_order = jnp.arange(POOL_DEV, dtype=jnp.int32)
    before = row_order[None, :] < row_order[:, None]
    slot_ranks = lax.optimization_barrier(jnp.sum((matches & before[None]).astype(jnp.int32), axis=2))
    sources = jnp.arange(device_count, dtype=jnp.int32)[:, None]
    slot_index = (targets * (device_count * CAP) + sources * CAP + slot_ranks).reshape(-1).astype(jnp.int32)
    routed = jnp.zeros((SLOTS, DE), jnp.bfloat16).at[slot_index].set(pooled)
    projected = jnp.dot(routed, w_adapt, preferred_element_type=jnp.float32)
    squares = lax.optimization_barrier(jnp.mean(projected * projected, axis=-1, keepdims=True))
    return (projected * lax.rsqrt(squares + 1e-05)).astype(jnp.bfloat16)
```

```python
import math

import jax
import jax.numpy as jnp
from jax import lax
from jax.sharding import PartitionSpec as P

HDE = 96
D = 5120
STRIDE = 4


def with_halo(shard, sides, width):
    for axis, dim in sides:
        devices, length = (lax.axis_size(axis), shard.shape[dim])
        up = [(i, (i + 1) % devices) for i in range(devices - 1)]
        down = [(j, i) for i, j in up]
        last = lax.slice_in_dim(shard, length - width, length, axis=dim)
        initial = lax.slice_in_dim(shard, 0, width, axis=dim)
        before = lax.ppermute(last, axis, up)
        after = lax.ppermute(initial, axis, down)
        shard = jnp.concatenate([before, shard, after], axis=dim)
    return shard


def layer_normed(input_rows):
    values = input_rows.astype(jnp.float32)
    centre = jnp.mean(values, -1, keepdims=True)
    centred = values - centre
    spread = jnp.mean(centred * centred, -1, keepdims=True)
    return (centred * lax.rsqrt(spread + 1e-05)).astype(jnp.bfloat16)


def local(audio, lengths, conv_kernel, w_qkv, w_out, place, w_adapt):
    frame_count, channels = audio.shape
    conv_reach = conv_kernel.shape[0] // 2
    seq_devices = lax.axis_size("tm")
    group_frames = frame_count * seq_devices
    offset = lax.axis_index("tm") * frame_count
    bounds = jnp.cumsum(lengths[0])

    def recording_of(positions):
        inside = (positions >= 0) & (positions < group_frames)
        counted = jnp.sum((positions[:, None] >= bounds[None, :]).astype(jnp.int32), axis=1)
        return jnp.where(inside, counted, -1)

    window_ids = recording_of(
        offset + jnp.arange(-conv_reach, frame_count + conv_reach, dtype=jnp.int32)
    )
    own_ids = window_ids[conv_reach : conv_reach + frame_count]
    widened = with_halo(audio, (("tm", 0),), conv_reach).astype(jnp.float32)
    depthwise = jnp.zeros((frame_count, channels), jnp.float32)
    for tap_index in range(conv_kernel.shape[0]):
        keep_mask = (window_ids[tap_index : tap_index + frame_count] == own_ids).astype(jnp.float32)
        depthwise = (
            depthwise
            + conv_kernel[tap_index]
            * widened[tap_index : tap_index + frame_count]
            * keep_mask[:, None]
        )
    mixed_rows = (audio.astype(jnp.float32) + jax.nn.silu(depthwise)).astype(jnp.bfloat16)
    normed = layer_normed(mixed_rows)
    queries = jnp.dot(normed, w_qkv[:, 0, :], preferred_element_type=jnp.float32).astype(
        jnp.bfloat16
    )
    key_rows = jnp.dot(normed, w_qkv[:, 1, :], preferred_element_type=jnp.float32).astype(
        jnp.bfloat16
    )
    value_rows = jnp.dot(normed, w_qkv[:, 2, :], preferred_element_type=jnp.float32).astype(
        jnp.bfloat16
    )
    head_count = queries.shape[1] // HDE
    query_heads = queries.reshape(frame_count, head_count, HDE)
    score_scale = HDE ** (-0.5)
    start_state = (
        jnp.full((head_count, frame_count), -1e30, jnp.float32),
        jnp.zeros((head_count, frame_count), jnp.float32),
        jnp.zeros((head_count, frame_count, HDE), jnp.float32),
    )

    def update(state_now, key_block, value_block, key_ids):
        running_max, running_sum, running_out = state_now
        scores = (
            jnp.einsum("qhd,khd->hqk", query_heads, key_block, preferred_element_type=jnp.float32)
            * score_scale
        )
        allowed = own_ids[:, None] == key_ids[None, :]
        scores = jnp.where(allowed[None], scores, -1e30)
        new_max = jnp.maximum(running_max, jnp.max(scores, axis=-1))
        rescale = jnp.exp(running_max - new_max)
        weights = jnp.exp(scores - new_max[:, :, None])
        new_sum = running_sum * rescale + jnp.sum(weights, axis=-1)
        low_weights = weights.astype(jnp.bfloat16)
        new_out = running_out * rescale[:, :, None] + jnp.einsum(
            "hqk,khd->hqd", low_weights, value_block, preferred_element_type=jnp.float32
        )
        return (new_max, new_sum, new_out)

    key_piece = lax.all_gather(
        key_rows.reshape(frame_count, head_count, HDE), "tm", axis=0, tiled=True
    )
    value_piece = lax.all_gather(
        value_rows.reshape(frame_count, head_count, HDE), "tm", axis=0, tiled=True
    )
    piece_rows = key_piece.shape[0]
    block_rows = math.gcd(piece_rows, 512)
    block_count = piece_rows // block_rows
    key_blocks = key_piece.reshape(block_count, block_rows, head_count, HDE)
    value_blocks = value_piece.reshape(block_count, block_rows, head_count, HDE)
    block_ids = recording_of(jnp.arange(piece_rows, dtype=jnp.int32)).reshape(
        block_count, block_rows
    )

    def advance(state_held, block_item):
        key_block, value_block, key_ids = block_item
        state_next = update(state_held, key_block, value_block, key_ids)
        return (state_next, None)

    state_out, unused = lax.scan(advance, start_state, (key_blocks, value_blocks, block_ids))
    final_max, final_sum, final_out = state_out
    attended = (
        jnp.transpose(final_out / final_sum[:, :, None], (1, 0, 2))
        .reshape(frame_count, head_count * HDE)
        .astype(jnp.bfloat16)
    )
    pooled_rows = frame_count // STRIDE
    mp_devices = lax.axis_size("mp")
    width = channels // mp_devices
    att_pooled = jnp.mean(
        attended.astype(jnp.float32).reshape(pooled_rows, STRIDE, attended.shape[1]), axis=1
    ).astype(jnp.bfloat16)
    mixed_pooled = jnp.mean(
        mixed_rows.astype(jnp.float32).reshape(pooled_rows, STRIDE, channels), axis=1
    )
    partial_out = jnp.dot(att_pooled, w_out, preferred_element_type=jnp.float32)
    parts = jnp.transpose(
        partial_out.astype(jnp.bfloat16).reshape(pooled_rows, mp_devices, width), (1, 0, 2)
    )
    parts = lax.all_to_all(parts, "mp", split_axis=0, concat_axis=0, tiled=True)
    own_columns = lax.dynamic_slice_in_dim(
        mixed_pooled, lax.axis_index("mp") * width, width, axis=1
    )
    pooled_part = (jnp.sum(parts.astype(jnp.float32), axis=0) + own_columns).astype(jnp.bfloat16)
    pooled = lax.all_gather(pooled_part, "mp", axis=0)
    projected = sum(
        jnp.dot(
            pooled[i], w_adapt[i * width : (i + 1) * width], preferred_element_type=jnp.float32
        )
        for i in range(mp_devices)
    )
    squares = lax.psum(jnp.sum(projected * projected, axis=-1), "mp")
    row_scale = lax.rsqrt(squares / D + 1e-05)
    normal_rows = (projected * row_scale[:, None]).astype(jnp.bfloat16)
    device_count = lax.axis_size("section") * seq_devices
    destination = place[:, 0]
    slot_cap = max(2, (2 * pooled_rows + device_count - 1) // device_count)
    row_order = jnp.arange(pooled_rows, dtype=jnp.int32)
    matches = destination[:, None] == destination[None, :]
    before = row_order[None, :] < row_order[:, None]
    slot_ranks = jnp.sum((matches & before).astype(jnp.int32), axis=1)
    slot_target = destination * slot_cap + slot_ranks
    one_hot = (
        jnp.arange(device_count * slot_cap, dtype=jnp.int32)[:, None] == slot_target[None, :]
    ).astype(jnp.bfloat16)
    outgoing = (
        jnp.dot(one_hot, normal_rows, preferred_element_type=jnp.float32)
        .astype(jnp.bfloat16)
        .reshape(device_count, slot_cap, normal_rows.shape[1])
    )
    arrived = lax.all_to_all(outgoing, ("section", "tm"), split_axis=0, concat_axis=0, tiled=True)
    return arrived.reshape(device_count * slot_cap, arrived.shape[2])


def solution(mesh):
    placed = (
        P(("section", "tm"), None),
        P("section", None),
        P(),
        P(None, None, "mp"),
        P("mp", None),
        P(("section", "tm"), None),
        P(None, "mp"),
    )
    return jax.shard_map(
        local, mesh=mesh, in_specs=placed, out_specs=P(("section", "tm"), "mp"), check_vma=False
    )
```

```python
import functools
import math

import jax
import jax.numpy as jnp
from jax import lax
from jax.experimental import pallas as pl
from jax.experimental.pallas import tpu as pltpu
from jax.sharding import PartitionSpec as P

HDE = 96
D = 5120
STRIDE = 4
LANES = 128
SUBLANES = 8
HALO = 16
MIB = 1 << 20
HIDDEN = -1e30


def recording_rows(bounds_ref, count, start, rows):
    position = start + lax.broadcasted_iota(jnp.int32, (rows, LANES), 0)
    found = jnp.zeros((rows, LANES), jnp.int32)
    for r in range(count):
        found += (position >= bounds_ref[r]).astype(jnp.int32)
    return found


def conv_qkv_kernel(
    recs,
    group_frames,
    bounds_ref,
    where_ref,
    audio_ref,
    before_ref,
    after_ref,
    taps_ref,
    w_ref,
    q_ref,
    kv_ref,
    pooled_ref,
    wide,
    mixed,
    normed,
    w_vmem,
    sem,
):
    frames, channels = audio_ref.shape
    taps = taps_ref.shape[0]
    reach = taps // 2
    blocks = channels // LANES
    offset = where_ref[0]
    load_w = pltpu.make_async_copy(w_ref, w_vmem, sem)
    load_w.start()
    for b in range(blocks):
        lanes = slice(b * LANES, (b + 1) * LANES)
        wide[b, :HALO, :] = before_ref[:, lanes].astype(jnp.float32)
        wide[b, HALO + frames :, :] = after_ref[:, lanes].astype(jnp.float32)
        wide[b, HALO : HALO + frames, :] = audio_ref[:, lanes].astype(jnp.float32)

    rows = 64
    shift = HALO - reach

    def chunk(i, carry):
        base = pl.multiple_of(i * rows, rows)

        def convolve(masked):
            if masked:
                position = offset + base + lax.broadcasted_iota(jnp.int32, (rows, LANES), 0)
                low = jnp.zeros((rows, LANES), jnp.int32)
                high = jnp.full((rows, LANES), group_frames, jnp.int32)
                for r in range(recs):
                    low = jnp.where(position >= bounds_ref[r], bounds_ref[r], low)
                for r in reversed(range(recs)):
                    high = jnp.where(position < bounds_ref[r], bounds_ref[r], high)
                low, high = low - position, high - position

            def block(b, carry):
                lanes = pl.ds(pl.multiple_of(b * LANES, LANES), LANES)
                total = jnp.zeros((rows, LANES), jnp.float32)
                for residue in range(SUBLANES):
                    steps = [
                        q
                        for q in range(taps // SUBLANES + 2)
                        if 0 <= q * SUBLANES + residue - shift < taps
                    ]
                    first, last = steps[0], steps[-1]
                    part = wide[
                        b,
                        pl.ds(
                            base + first * SUBLANES + residue, rows + (last - first) * SUBLANES
                        ),
                        :,
                    ]
                    for q in steps:
                        tap = q * SUBLANES + residue - shift
                        at = (q - first) * SUBLANES
                        term = part[at : at + rows]
                        if masked and tap < reach:
                            term = jnp.where(low <= tap - reach, term, 0.0)
                        if masked and tap > reach:
                            term = jnp.where(high > tap - reach, term, 0.0)
                        total = total + taps_ref[tap : tap + 1, lanes] * term
                own = wide[b, pl.ds(base + HALO, rows), :]
                half = 0.5 * total
                value = own + half * (1.0 + jnp.tanh(half))
                mixed[pl.ds(base, rows), lanes] = value.astype(jnp.bfloat16)
                return carry

            lax.fori_loop(0, blocks, block, 0)

        touched = jnp.zeros((), jnp.bool_)
        for r in range(recs - 1):
            at = bounds_ref[r] - offset - base
            touched = touched | ((at > -reach) & (at < rows + reach))

        @pl.when(touched)
        def _():
            convolve(True)

        @pl.when(jnp.logical_not(touched))
        def _():
            convolve(False)

        for sub in range(rows // 16):
            at = pl.ds(pl.multiple_of(base + sub * 16, 16), 16)
            values = mixed[at, :].astype(jnp.float32)
            centred = values - jnp.mean(values, -1, keepdims=True)
            spread = jnp.mean(centred * centred, -1, keepdims=True)
            normed[at, :] = (centred * lax.rsqrt(spread + 1e-05)).astype(jnp.bfloat16)
        return carry

    lax.fori_loop(0, frames // rows, chunk, 0)

    width = pooled_ref.shape[1]
    own_columns = pl.ds(pl.multiple_of(where_ref[1] * width, LANES), width)
    pooled_rows = frames // STRIDE
    pool = (
        lax.broadcasted_iota(jnp.int32, (pooled_rows, frames), 1) // STRIDE
        == lax.broadcasted_iota(jnp.int32, (pooled_rows, frames), 0)
    ).astype(jnp.bfloat16) * (1.0 / STRIDE)
    pooled_ref[...] = jnp.dot(
        pool.astype(jnp.bfloat16), mixed[:, own_columns], preferred_element_type=jnp.float32
    )

    load_w.wait()
    heads = w_ref.shape[2] // HDE
    part_rows = 256
    score_scale = HDE ** (-0.5) * math.log2(math.e)
    for part in range(frames // part_rows):
        at = slice(part * part_rows, (part + 1) * part_rows)
        lane = lax.broadcasted_iota(jnp.int32, (part_rows, LANES), 1)
        mine = recording_rows(bounds_ref, recs, offset + part * part_rows, part_rows)
        same = lane - HDE == mine
        extra_q = jnp.where(same | (lane >= HDE + recs), 0.0, HIDDEN)
        extra_k = jnp.where(same, 1.0, 0.0)
        extra_v = jnp.where(lane == HDE, 1.0, 0.0)
        for kind, extra in enumerate((extra_q, extra_k, extra_v)):
            result = jnp.dot(normed[at, :], w_vmem[kind], preferred_element_type=jnp.float32)
            if kind == 0:
                result = result * score_scale
            for h in range(heads):
                tile, start = divmod(h * HDE, LANES)
                tiles = 1 if start + HDE <= LANES else 2
                head = result[:, tile * LANES : (tile + tiles) * LANES]
                if start:
                    head = pltpu.roll(head, tiles * LANES - start, 1)
                head = jnp.where(lane < HDE, head[:, :LANES], extra).astype(jnp.bfloat16)
                if kind == 0:
                    q_ref[at, h * LANES : (h + 1) * LANES] = head
                else:
                    first = ((kind - 1) * heads + h) * LANES
                    kv_ref[at, first : first + LANES] = head


def attend_kernel(q_ref, *refs):
    *kv_refs, w_ref, out_ref = refs
    frames = q_ref.shape[0]
    heads = q_ref.shape[1] // LANES
    parts, _, width = out_ref.shape
    rows = 128 if len(kv_refs) <= 2 else 32
    few = rows // STRIDE
    pool = (
        lax.broadcasted_iota(jnp.int32, (few, rows), 1) // STRIDE
        == lax.broadcasted_iota(jnp.int32, (few, rows), 0)
    ).astype(jnp.float32) * (1.0 / STRIDE)
    pool = pool.astype(jnp.bfloat16)

    def step(i, carry):
        at = pl.ds(pl.multiple_of(i * rows, rows), rows)
        pooled = []
        for h in range(heads):
            query = q_ref[at, h * LANES : (h + 1) * LANES]
            scores = [
                lax.dot_general(
                    query,
                    kv[:, h * LANES : (h + 1) * LANES],
                    (((1,), (1,)), ((), ())),
                    preferred_element_type=jnp.float32,
                )
                for kv in kv_refs
            ]
            peak = functools.reduce(
                jnp.maximum, [jnp.max(s, axis=1, keepdims=True) for s in scores]
            )
            out = jnp.zeros((rows, LANES), jnp.float32)
            for s, kv in zip(scores, kv_refs):
                weights = jnp.exp2(s - peak).astype(jnp.bfloat16)
                values = kv[:, (heads + h) * LANES : (heads + h + 1) * LANES]
                out += jnp.dot(weights, values, preferred_element_type=jnp.float32)
            attended = (out * (1.0 / out[:, HDE : HDE + 1])).astype(jnp.bfloat16)
            pooled.append(
                jnp.dot(pool, attended, preferred_element_type=jnp.float32).astype(jnp.bfloat16)
            )
        for part in range(parts):
            total = jnp.zeros((few, width), jnp.float32)
            for h in range(heads):
                total += jnp.dot(
                    pooled[h][:, :HDE],
                    w_ref[h * HDE : (h + 1) * HDE, part * width : (part + 1) * width],
                    preferred_element_type=jnp.float32,
                )
            out_ref[part, pl.ds(pl.multiple_of(i * few, few), few), :] = total.astype(
                jnp.bfloat16
            )
        return carry

    lax.fori_loop(0, frames // rows, step, 0)


def local(audio, lengths, conv_kernel, w_qkv, w_out, place, w_adapt):
    frame_count, channels = audio.shape
    seq_devices = lax.axis_size("tm")
    mp_devices = lax.axis_size("mp")
    recs = lengths.shape[1]
    group_frames = frame_count * seq_devices
    width = channels // mp_devices
    pooled_rows = frame_count // STRIDE
    heads = w_qkv.shape[2] // HDE
    bounds = jnp.cumsum(lengths[0])
    where = jnp.stack([lax.axis_index("tm") * frame_count, lax.axis_index("mp")])

    up = [(i, i + 1) for i in range(seq_devices - 1)]
    down = [(j, i) for i, j in up]
    before = lax.ppermute(audio[frame_count - HALO :], "tm", up)
    after = lax.ppermute(audio[:HALO], "tm", down)

    smem = pl.BlockSpec(memory_space=pltpu.SMEM)
    vmem = pl.BlockSpec(memory_space=pltpu.VMEM)
    w_three = jnp.transpose(w_qkv, (1, 0, 2))
    queries, own_kv, mixed_pooled = pl.pallas_call(
        functools.partial(conv_qkv_kernel, recs, group_frames),
        out_shape=(
            jax.ShapeDtypeStruct((frame_count, heads * LANES), jnp.bfloat16),
            jax.ShapeDtypeStruct((frame_count, 2 * heads * LANES), jnp.bfloat16),
            jax.ShapeDtypeStruct((pooled_rows, width), jnp.float32),
        ),
        in_specs=[smem, smem, vmem, vmem, vmem, vmem, pl.BlockSpec(memory_space=pl.ANY)],
        out_specs=(vmem, vmem, vmem),
        scratch_shapes=[
            pltpu.VMEM((channels // LANES, frame_count + 2 * HALO, LANES), jnp.float32),
            pltpu.VMEM((frame_count, channels), jnp.bfloat16),
            pltpu.VMEM((frame_count, channels), jnp.bfloat16),
            pltpu.VMEM(w_three.shape, jnp.bfloat16),
            pltpu.SemaphoreType.DMA,
        ],
        compiler_params=pltpu.CompilerParams(vmem_limit_bytes=24 * MIB),
        name="conv_qkv",
    )(bounds, where, audio, before, after, conv_kernel, w_three)

    kv_blocks = [own_kv] + [
        lax.ppermute(own_kv, "tm", [(i, (i + k) % seq_devices) for i in range(seq_devices)])
        for k in range(1, seq_devices)
    ]
    parts = pl.pallas_call(
        attend_kernel,
        out_shape=jax.ShapeDtypeStruct((mp_devices, pooled_rows, width), jnp.bfloat16),
        in_specs=[vmem] * (seq_devices + 2),
        out_specs=vmem,
        compiler_params=pltpu.CompilerParams(vmem_limit_bytes=32 * MIB),
        name="attend",
    )(queries, *kv_blocks, w_out)

    parts = lax.all_to_all(parts, "mp", split_axis=0, concat_axis=0, tiled=True)
    pooled_part = (jnp.sum(parts.astype(jnp.float32), axis=0) + mixed_pooled).astype(jnp.bfloat16)
    pooled = lax.all_gather(pooled_part, "mp", axis=0)
    projected = sum(
        jnp.dot(
            pooled[i], w_adapt[i * width : (i + 1) * width], preferred_element_type=jnp.float32
        )
        for i in range(mp_devices)
    )
    squares = lax.psum(jnp.sum(projected * projected, axis=-1), "mp")
    row_scale = lax.rsqrt(squares / D + 1e-05)
    normal_rows = (projected * row_scale[:, None]).astype(jnp.bfloat16)
    device_count = lax.axis_size("section") * seq_devices
    destination = place[:, 0]
    slot_cap = max(2, (2 * pooled_rows + device_count - 1) // device_count)
    row_order = jnp.arange(pooled_rows, dtype=jnp.int32)
    matches = destination[:, None] == destination[None, :]
    earlier = row_order[None, :] < row_order[:, None]
    slot_ranks = jnp.sum((matches & earlier).astype(jnp.int32), axis=1)
    slot_target = destination * slot_cap + slot_ranks
    one_hot = (
        jnp.arange(device_count * slot_cap, dtype=jnp.int32)[:, None] == slot_target[None, :]
    ).astype(jnp.bfloat16)
    outgoing = (
        jnp.dot(one_hot, normal_rows, preferred_element_type=jnp.float32)
        .astype(jnp.bfloat16)
        .reshape(device_count, slot_cap, normal_rows.shape[1])
    )
    arrived = lax.all_to_all(outgoing, ("section", "tm"), split_axis=0, concat_axis=0, tiled=True)
    return arrived.reshape(device_count * slot_cap, arrived.shape[2])


def solution(mesh):
    placed = (
        P(("section", "tm"), None),
        P("section", None),
        P(),
        P(None, None, "mp"),
        P("mp", None),
        P(("section", "tm"), None),
        P(None, "mp"),
    )
    return jax.shard_map(
        local, mesh=mesh, in_specs=placed, out_specs=P(("section", "tm"), "mp"), check_vma=False
    )
```

```python
import functools
import math

import jax
import jax.numpy as jnp
from jax import lax
from jax.experimental import pallas as pl
from jax.experimental.pallas import tpu as pltpu
from jax.sharding import PartitionSpec as P

HDE = 96
D = 5120
STRIDE = 4
LANES = 128
SUBLANES = 8
HALO = 16
MIB = 1 << 20
HIDDEN = -1e30


def recording_rows(bounds_ref, count, start, rows):
    position = start + lax.broadcasted_iota(jnp.int32, (rows, LANES), 0)
    found = jnp.zeros((rows, LANES), jnp.int32)
    for r in range(count):
        found += (position >= bounds_ref[r]).astype(jnp.int32)
    return found


def conv_qkv_kernel(
    recs,
    group_frames,
    bounds_ref,
    where_ref,
    audio_ref,
    before_ref,
    after_ref,
    taps_ref,
    w_ref,
    q_ref,
    kv_ref,
    pooled_ref,
    wide,
    mixed,
    normed,
    w_vmem,
    sem,
):
    frames, channels = audio_ref.shape
    taps = taps_ref.shape[0]
    reach = taps // 2
    blocks = channels // LANES
    offset = where_ref[0]
    load_w = pltpu.make_async_copy(w_ref, w_vmem, sem)
    load_w.start()
    for b in range(blocks):
        lanes = slice(b * LANES, (b + 1) * LANES)
        wide[b, :HALO, :] = before_ref[:, lanes].astype(jnp.float32)
        wide[b, HALO + frames :, :] = after_ref[:, lanes].astype(jnp.float32)
        wide[b, HALO : HALO + frames, :] = audio_ref[:, lanes].astype(jnp.float32)

    rows = 64
    shift = HALO - reach

    def chunk(i, carry):
        base = pl.multiple_of(i * rows, rows)

        def convolve(masked):
            if masked:
                position = offset + base + lax.broadcasted_iota(jnp.int32, (rows, LANES), 0)
                low = jnp.zeros((rows, LANES), jnp.int32)
                high = jnp.full((rows, LANES), group_frames, jnp.int32)
                for r in range(recs):
                    low = jnp.where(position >= bounds_ref[r], bounds_ref[r], low)
                for r in reversed(range(recs)):
                    high = jnp.where(position < bounds_ref[r], bounds_ref[r], high)
                low, high = low - position, high - position

            def block(b, carry):
                lanes = pl.ds(pl.multiple_of(b * LANES, LANES), LANES)
                total = jnp.zeros((rows, LANES), jnp.float32)
                for residue in range(SUBLANES):
                    steps = [
                        q
                        for q in range(taps // SUBLANES + 2)
                        if 0 <= q * SUBLANES + residue - shift < taps
                    ]
                    first, last = steps[0], steps[-1]
                    part = wide[
                        b,
                        pl.ds(
                            base + first * SUBLANES + residue, rows + (last - first) * SUBLANES
                        ),
                        :,
                    ]
                    for q in steps:
                        tap = q * SUBLANES + residue - shift
                        at = (q - first) * SUBLANES
                        term = part[at : at + rows]
                        if masked and tap < reach:
                            term = jnp.where(low <= tap - reach, term, 0.0)
                        if masked and tap > reach:
                            term = jnp.where(high > tap - reach, term, 0.0)
                        total = total + taps_ref[tap : tap + 1, lanes] * term
                own = wide[b, pl.ds(base + HALO, rows), :]
                half = 0.5 * total
                value = own + half * (1.0 + jnp.tanh(half))
                mixed[pl.ds(base, rows), lanes] = value.astype(jnp.bfloat16)
                return carry

            lax.fori_loop(0, blocks, block, 0)

        touched = jnp.zeros((), jnp.bool_)
        for r in range(recs - 1):
            at = bounds_ref[r] - offset - base
            touched = touched | ((at > -reach) & (at < rows + reach))

        @pl.when(touched)
        def _():
            convolve(True)

        @pl.when(jnp.logical_not(touched))
        def _():
            convolve(False)

        for sub in range(rows // 16):
            at = pl.ds(pl.multiple_of(base + sub * 16, 16), 16)
            values = mixed[at, :].astype(jnp.float32)
            centred = values - jnp.mean(values, -1, keepdims=True)
            spread = jnp.mean(centred * centred, -1, keepdims=True)
            normed[at, :] = (centred * lax.rsqrt(spread + 1e-05)).astype(jnp.bfloat16)
        return carry

    lax.fori_loop(0, frames // rows, chunk, 0)

    width = pooled_ref.shape[1]
    own_columns = pl.ds(pl.multiple_of(where_ref[1] * width, LANES), width)
    pooled_rows = frames // STRIDE
    pool = (
        lax.broadcasted_iota(jnp.int32, (pooled_rows, frames), 1) // STRIDE
        == lax.broadcasted_iota(jnp.int32, (pooled_rows, frames), 0)
    ).astype(jnp.bfloat16) * (1.0 / STRIDE)
    pooled_ref[...] = jnp.dot(
        pool.astype(jnp.bfloat16), mixed[:, own_columns], preferred_element_type=jnp.float32
    )

    load_w.wait()
    heads = w_ref.shape[2] // HDE
    part_rows = 256
    score_scale = HDE ** (-0.5) * math.log2(math.e)
    for part in range(frames // part_rows):
        at = slice(part * part_rows, (part + 1) * part_rows)
        lane = lax.broadcasted_iota(jnp.int32, (part_rows, LANES), 1)
        mine = recording_rows(bounds_ref, recs, offset + part * part_rows, part_rows)
        same = lane - HDE == mine
        extra_q = jnp.where(same | (lane >= HDE + recs), 0.0, HIDDEN)
        extra_k = jnp.where(same, 1.0, 0.0)
        extra_v = jnp.where(lane == HDE, 1.0, 0.0)
        for kind, extra in enumerate((extra_q, extra_k, extra_v)):
            result = jnp.dot(normed[at, :], w_vmem[kind], preferred_element_type=jnp.float32)
            if kind == 0:
                result = result * score_scale
            for h in range(heads):
                tile, start = divmod(h * HDE, LANES)
                tiles = 1 if start + HDE <= LANES else 2
                head = result[:, tile * LANES : (tile + tiles) * LANES]
                if start:
                    head = pltpu.roll(head, tiles * LANES - start, 1)
                head = jnp.where(lane < HDE, head[:, :LANES], extra).astype(jnp.bfloat16)
                if kind == 0:
                    q_ref[at, h * LANES : (h + 1) * LANES] = head
                else:
                    first = ((kind - 1) * heads + h) * LANES
                    kv_ref[at, first : first + LANES] = head


def attend_kernel(targets_ref, q_ref, mixed_ref, w_ref, *refs):
    kv_refs, out_refs = refs[: -targets_ref.shape[0]], refs[-targets_ref.shape[0] :]
    frames = q_ref.shape[0]
    heads = q_ref.shape[1] // LANES
    width = mixed_ref.shape[1]
    rows = 128 if len(kv_refs) <= 2 else 32
    few = rows // STRIDE
    pool = (
        lax.broadcasted_iota(jnp.int32, (few, rows), 1) // STRIDE
        == lax.broadcasted_iota(jnp.int32, (few, rows), 0)
    ).astype(jnp.float32) * (1.0 / STRIDE)
    pool = pool.astype(jnp.bfloat16)

    def step(i, carry):
        at = pl.ds(pl.multiple_of(i * rows, rows), rows)
        pooled = []
        for h in range(heads):
            query = q_ref[at, h * LANES : (h + 1) * LANES]
            scores = [
                lax.dot_general(
                    query,
                    kv[:, h * LANES : (h + 1) * LANES],
                    (((1,), (1,)), ((), ())),
                    preferred_element_type=jnp.float32,
                )
                for kv in kv_refs
            ]
            peak = functools.reduce(
                jnp.maximum, [jnp.max(s, axis=1, keepdims=True) for s in scores]
            )
            out = jnp.zeros((rows, LANES), jnp.float32)
            for s, kv in zip(scores, kv_refs):
                weights = jnp.exp2(s - peak).astype(jnp.bfloat16)
                values = kv[:, (heads + h) * LANES : (heads + h + 1) * LANES]
                out += jnp.dot(weights, values, preferred_element_type=jnp.float32)
            attended = (out * (1.0 / out[:, HDE : HDE + 1])).astype(jnp.bfloat16)
            pooled.append(
                jnp.dot(pool, attended, preferred_element_type=jnp.float32).astype(jnp.bfloat16)
            )
        few_at = pl.ds(pl.multiple_of(i * few, few), few)
        for k, out_ref in enumerate(out_refs):
            columns = pl.ds(pl.multiple_of(targets_ref[k] * width, LANES), width)
            total = mixed_ref[few_at, :] if k == 0 else jnp.zeros((few, width), jnp.float32)
            for h in range(heads):
                total += jnp.dot(
                    pooled[h][:, :HDE],
                    w_ref[h * HDE : (h + 1) * HDE, columns],
                    preferred_element_type=jnp.float32,
                )
            out_ref[few_at, :] = total.astype(out_ref.dtype)
        return carry

    lax.fori_loop(0, frames // rows, step, 0)


def project_kernel(targets_ref, *refs):
    *part_refs, w_ref, out_ref, squares_ref = refs
    width = part_refs[0].shape[1]
    total = jnp.zeros(out_ref.shape, jnp.float32)
    for k, part_ref in enumerate(part_refs):
        at = pl.ds(pl.multiple_of(targets_ref[k] * width, LANES), width)
        total += jnp.dot(part_ref[...], w_ref[at, :], preferred_element_type=jnp.float32)
    out_ref[...] = total
    rows = total.shape[0]
    squares = jnp.sum(total * total, axis=1, keepdims=True)
    squares_ref[...] = jnp.transpose(jnp.broadcast_to(squares, (rows, rows)))[:SUBLANES]


def route_kernel(cap, firsts_ref, place_ref, rows_ref, *refs):
    square_refs, out_refs = refs[: -firsts_ref.shape[0]], refs[-firsts_ref.shape[0] :]
    rows = rows_ref.shape[0]
    devices = sum(ref.shape[0] for ref in out_refs) // cap
    squares = square_refs[0][...]
    for ref in square_refs[1:]:
        squares += ref[...]
    scale = lax.rsqrt(squares[:1] / D + 1e-05)
    scale = jnp.transpose(jnp.broadcast_to(scale, (rows, rows)))[:, :1]
    normal_rows = (rows_ref[...] * scale).astype(jnp.bfloat16)
    destination = place_ref[...]
    named = lax.broadcasted_iota(jnp.int32, (devices, rows), 0) == destination
    earlier = lax.broadcasted_iota(jnp.int32, (rows, rows), 0) < lax.broadcasted_iota(
        jnp.int32, (rows, rows), 1
    )
    counts = jnp.dot(
        named.astype(jnp.float32).astype(jnp.bfloat16),
        earlier.astype(jnp.float32).astype(jnp.bfloat16),
        preferred_element_type=jnp.float32,
    )
    rank = jnp.sum(jnp.where(named, counts, 0.0), axis=0, keepdims=True).astype(jnp.int32)
    target = destination * cap + rank
    for k, out_ref in enumerate(out_refs):
        slots = out_ref.shape[0]
        slot = firsts_ref[k] + lax.broadcasted_iota(jnp.int32, (slots, rows), 0)
        one_hot = (slot == target).astype(jnp.float32).astype(jnp.bfloat16)
        out_ref[...] = jnp.dot(
            one_hot, normal_rows, preferred_element_type=jnp.float32
        ).astype(jnp.bfloat16)


def collect_kernel(firsts_ref, *refs):
    *block_refs, out_ref = refs
    for k, block_ref in enumerate(block_refs):
        slots = block_ref.shape[0]
        at = pl.ds(pl.multiple_of(firsts_ref[k], slots), slots)
        out_ref[at, :] = block_ref[...]


def partner(index, k, devices):
    if devices & (devices - 1) == 0:
        return index ^ k
    return (index + k) % devices


def sender(index, k, devices):
    if devices & (devices - 1) == 0:
        return index ^ k
    return (index - k) % devices


def exchange(value, axes, k, devices):
    return lax.ppermute(value, axes, [(i, partner(i, k, devices)) for i in range(devices)])


def local(audio, lengths, conv_kernel, w_qkv, w_out, place, w_adapt):
    frame_count, channels = audio.shape
    seq_devices = lax.axis_size("tm")
    mp_devices = lax.axis_size("mp")
    recs = lengths.shape[1]
    group_frames = frame_count * seq_devices
    width = channels // mp_devices
    pooled_rows = frame_count // STRIDE
    heads = w_qkv.shape[2] // HDE
    bounds = jnp.cumsum(lengths[0])
    where = jnp.stack([lax.axis_index("tm") * frame_count, lax.axis_index("mp")])

    up = [(i, i + 1) for i in range(seq_devices - 1)]
    down = [(j, i) for i, j in up]
    before = lax.ppermute(audio[frame_count - HALO :], "tm", up)
    after = lax.ppermute(audio[:HALO], "tm", down)

    smem = pl.BlockSpec(memory_space=pltpu.SMEM)
    vmem = pl.BlockSpec(memory_space=pltpu.VMEM)
    w_three = jnp.transpose(w_qkv, (1, 0, 2))
    queries, own_kv, mixed_pooled = pl.pallas_call(
        functools.partial(conv_qkv_kernel, recs, group_frames),
        out_shape=(
            jax.ShapeDtypeStruct((frame_count, heads * LANES), jnp.bfloat16),
            jax.ShapeDtypeStruct((frame_count, 2 * heads * LANES), jnp.bfloat16),
            jax.ShapeDtypeStruct((pooled_rows, width), jnp.float32),
        ),
        in_specs=[smem, smem, vmem, vmem, vmem, vmem, pl.BlockSpec(memory_space=pl.ANY)],
        out_specs=(vmem, vmem, vmem),
        scratch_shapes=[
            pltpu.VMEM((channels // LANES, frame_count + 2 * HALO, LANES), jnp.float32),
            pltpu.VMEM((frame_count, channels), jnp.bfloat16),
            pltpu.VMEM((frame_count, channels), jnp.bfloat16),
            pltpu.VMEM(w_three.shape, jnp.bfloat16),
            pltpu.SemaphoreType.DMA,
        ],
        compiler_params=pltpu.CompilerParams(vmem_limit_bytes=24 * MIB),
        name="conv_qkv",
    )(bounds, where, audio, before, after, conv_kernel, w_three)

    kv_blocks = [own_kv] + [
        lax.ppermute(own_kv, "tm", [(i, (i + k) % seq_devices) for i in range(seq_devices)])
        for k in range(1, seq_devices)
    ]
    mp_index = lax.axis_index("mp")
    mp_targets = jnp.stack([partner(mp_index, k, mp_devices) for k in range(mp_devices)])
    mp_senders = jnp.stack([sender(mp_index, k, mp_devices) for k in range(mp_devices)])
    part = (pooled_rows, width)
    own_part, *parts = pl.pallas_call(
        attend_kernel,
        out_shape=[jax.ShapeDtypeStruct(part, jnp.float32)]
        + [jax.ShapeDtypeStruct(part, jnp.bfloat16)] * (mp_devices - 1),
        in_specs=[smem] + [vmem] * (seq_devices + 3),
        out_specs=[vmem] * mp_devices,
        compiler_params=pltpu.CompilerParams(vmem_limit_bytes=32 * MIB),
        name="attend",
    )(mp_targets, queries, mixed_pooled, w_out, *kv_blocks)
    others = range(1, mp_devices)
    for k in others:
        own_part += exchange(parts[k - 1], "mp", k, mp_devices).astype(jnp.float32)
    own_part = own_part.astype(jnp.bfloat16)
    pooled = [own_part] + [exchange(own_part, "mp", k, mp_devices) for k in others]

    columns = w_adapt.shape[1]
    projected, squares = pl.pallas_call(
        project_kernel,
        out_shape=[
            jax.ShapeDtypeStruct((pooled_rows, columns), jnp.float32),
            jax.ShapeDtypeStruct((SUBLANES, pooled_rows), jnp.float32),
        ],
        in_specs=[smem] + [vmem] * (mp_devices + 1),
        out_specs=[vmem] * 2,
        compiler_params=pltpu.CompilerParams(vmem_limit_bytes=16 * MIB),
        name="project",
    )(mp_senders, *pooled, w_adapt)
    squares = [squares] + [exchange(squares, "mp", k, mp_devices) for k in others]

    axes = ("section", "tm")
    device_count = lax.axis_size("section") * seq_devices
    me = lax.axis_index(axes)
    cap = max(2, (2 * pooled_rows + device_count - 1) // device_count)
    direct = device_count <= 8
    if direct:
        firsts = jnp.stack([partner(me, k, device_count) * cap for k in range(device_count)])
        blocks = [jax.ShapeDtypeStruct((cap, columns), jnp.bfloat16)] * device_count
    else:
        firsts = jnp.zeros((1,), jnp.int32)
        blocks = [jax.ShapeDtypeStruct((device_count * cap, columns), jnp.bfloat16)]
    blocks = pl.pallas_call(
        functools.partial(route_kernel, cap),
        out_shape=blocks,
        in_specs=[smem] + [vmem] * (mp_devices + 2),
        out_specs=[vmem] * len(blocks),
        compiler_params=pltpu.CompilerParams(vmem_limit_bytes=16 * MIB),
        name="route",
    )(firsts, place.T, projected, *squares)
    if not direct:
        return lax.all_to_all(blocks[0], axes, split_axis=0, concat_axis=0, tiled=True)
    arrived = [blocks[0]] + [
        exchange(blocks[k], axes, k, device_count) for k in range(1, device_count)
    ]
    firsts = jnp.stack([sender(me, k, device_count) * cap for k in range(device_count)])
    return pl.pallas_call(
        collect_kernel,
        out_shape=jax.ShapeDtypeStruct((device_count * cap, columns), jnp.bfloat16),
        in_specs=[smem] + [vmem] * device_count,
        out_specs=vmem,
        compiler_params=pltpu.CompilerParams(vmem_limit_bytes=8 * MIB),
        name="collect",
    )(firsts, *arrived)


def solution(mesh):
    placed = (
        P(("section", "tm"), None),
        P("section", None),
        P(),
        P(None, None, "mp"),
        P("mp", None),
        P(("section", "tm"), None),
        P(None, "mp"),
    )
    return jax.shard_map(
        local, mesh=mesh, in_specs=placed, out_specs=P(("section", "tm"), "mp"), check_vma=False
    )
```

```python
import functools
import math

import jax
import jax.numpy as jnp
from jax import lax
from jax.experimental import pallas as pl
from jax.experimental.pallas import tpu as pltpu
from jax.sharding import PartitionSpec as P

HDE = 96
D = 5120
STRIDE = 4
LANES = 128
SUBLANES = 8
HALO = 16
EDGE = 32
BLOCK = 16
MIB = 1 << 20
HIDDEN = -1e30


def conv_blocks(src, dst, taps, blocks, firsts, recs, bounds, starts_ref, ends_ref):
    count = taps.shape[0] // SUBLANES
    reach = count // 2
    span = BLOCK + count - 1
    shape = (SUBLANES, LANES)
    upper = lax.broadcasted_iota(jnp.int32, shape, 0) < SUBLANES // 2

    def both(values):
        if len(values) == 1:
            return jnp.full(shape, values[0], jnp.int32)
        return jnp.where(upper, values[0], values[1])

    def block(i, carry):
        base = i * BLOCK
        positions = [first + base for first in firsts]

        def frame(k):
            at = (base + k + HALO - reach) * SUBLANES
            return src[pl.ds(pl.multiple_of(at, SUBLANES), SUBLANES), :]

        def out(t):
            return pl.ds(pl.multiple_of((base + t) * SUBLANES, SUBLANES), SUBLANES)

        def convolve(inside):
            kernel = [taps[j * SUBLANES : (j + 1) * SUBLANES, :] for j in range(count)]
            totals = [None] * BLOCK
            for k in range(span):
                value = frame(k)
                if inside is not None:
                    value = jnp.where(inside(k), value, 0.0)
                for t in range(max(0, k - count + 1), min(BLOCK, k + 1)):
                    term = kernel[k - t] * value
                    totals[t] = term if totals[t] is None else totals[t] + term
            for t in range(BLOCK):
                half = 0.5 * totals[t]
                value = frame(t + reach) + half * (1.0 + jnp.tanh(half))
                if inside is not None:
                    value = jnp.where(inside(t + reach), value, dst[out(t), :])
                dst[out(t), :] = value

        touched = jnp.zeros((), jnp.bool_)
        for position in positions:
            for bound in bounds[:-1]:
                at = bound - position
                touched = touched | ((at > -reach) & (at < BLOCK + reach))

        @pl.when(jnp.logical_not(touched))
        def _():
            convolve(None)

        @pl.when(touched)
        def _():
            begin, extra = [], jnp.zeros((), jnp.int32)
            for position in positions:
                first = last = jnp.zeros((), jnp.int32)
                for bound in bounds[:-1]:
                    first += (bound <= position).astype(jnp.int32)
                    last += (bound <= position + BLOCK - 1).astype(jnp.int32)
                begin.append(first)
                extra = jnp.maximum(extra, last - first)

            def once(turn, carry):
                which = [jnp.minimum(first + turn, recs - 1) for first in begin]
                low = both([starts_ref[r] - p for r, p in zip(which, positions)])
                high = both([ends_ref[r] - p for r, p in zip(which, positions)])
                convolve(lambda k: (low <= k - reach) & (high > k - reach))
                return carry

            lax.fori_loop(0, extra + 1, once, 0)

        return carry

    lax.fori_loop(0, blocks, block, 0)


def spread(value, ref, row, blocks, first, upper_only):
    frames = value.shape[0]
    for k in range(blocks):
        at = (first + k) * LANES
        start = row * SUBLANES + k + (SUBLANES // 2 if upper_only else 0)
        ref[pl.ds(start, frames, stride=SUBLANES), :] = value[:, at : at + LANES]


def recording_bounds(lengths_ref, starts_ref, ends_ref):
    bounds, total = [], jnp.zeros((), jnp.int32)
    for r in range(lengths_ref.shape[1]):
        starts_ref[r] = total
        total = total + lengths_ref[0, r]
        ends_ref[r] = total
        bounds.append(total)
    return bounds


def spread_taps(taps_ref, full_taps, half_taps):
    count = taps_ref.shape[0]
    blocks = taps_ref.shape[1] // LANES
    for k in range(blocks):
        value = taps_ref[:, k * LANES : (k + 1) * LANES]
        if k < SUBLANES:
            full_taps[pl.ds(k, count, stride=SUBLANES), :] = value
        else:
            for half in range(2):
                at = k - SUBLANES + half * SUBLANES // 2
                half_taps[pl.ds(at, count, stride=SUBLANES), :] = value


def normalise(sources, rows, mixed, normed, at):
    parts = []
    for ref, frame, sublane, blocks in sources:
        for k in range(blocks):
            start = frame * SUBLANES + sublane + k
            parts.append(ref[pl.ds(start, rows, stride=SUBLANES), :])
    low = jnp.concatenate(parts, axis=1).astype(jnp.bfloat16)
    mixed[at, :] = low
    values = low.astype(jnp.float32)
    centred = values - jnp.mean(values, -1, keepdims=True)
    variance = jnp.mean(centred * centred, -1, keepdims=True)
    normed[at, :] = (centred * lax.rsqrt(variance + 1e-05)).astype(jnp.bfloat16)


def pool_rows(rows):
    few = rows // STRIDE
    chosen = (
        lax.broadcasted_iota(jnp.int32, (few, rows), 1) // STRIDE
        == lax.broadcasted_iota(jnp.int32, (few, rows), 0)
    )
    return (chosen.astype(jnp.float32) * (1.0 / STRIDE)).astype(jnp.bfloat16)


def project_heads(normed_rows, w_vmem, position, bounds, at, q_ref, kv_ref):
    recs = len(bounds)
    heads = w_vmem.shape[2] // HDE
    lane = lax.broadcasted_iota(jnp.int32, position.shape, 1)
    mine = jnp.zeros(position.shape, jnp.int32)
    for bound in bounds:
        mine += (position >= bound).astype(jnp.int32)
    same = lane - HDE == mine
    extra_q = jnp.where(same | (lane >= HDE + recs), 0.0, HIDDEN)
    extra_k = jnp.where(same, 1.0, 0.0)
    extra_v = jnp.where(lane == HDE, 1.0, 0.0)
    score_scale = HDE ** (-0.5) * math.log2(math.e)
    for kind, extra in enumerate((extra_q, extra_k, extra_v)):
        result = jnp.dot(normed_rows, w_vmem[kind], preferred_element_type=jnp.float32)
        if kind == 0:
            result = result * score_scale
        for h in range(heads):
            tile, start = divmod(h * HDE, LANES)
            tiles = 1 if start + HDE <= LANES else 2
            head = result[:, tile * LANES : (tile + tiles) * LANES]
            if start:
                head = pltpu.roll(head, tiles * LANES - start, 1)
            head = jnp.where(lane < HDE, head[:, :LANES], extra).astype(jnp.bfloat16)
            if kind == 0:
                q_ref[at, h * LANES : (h + 1) * LANES] = head
            else:
                first = ((kind - 1) * heads + h) * LANES
                kv_ref[at, first : first + LANES] = head


def interior_kernel(
    lengths_ref,
    where_ref,
    taps_ref,
    audio_ref,
    w_ref,
    q_ref,
    kv_ref,
    pooled_ref,
    audio,
    full_src,
    full_dst,
    half_src,
    half_dst,
    full_taps,
    half_taps,
    mixed,
    normed,
    w_vmem,
    starts_ref,
    ends_ref,
    audio_sem,
    w_sem,
):
    rows = q_ref.shape[0]
    inner = rows + 2 * HALO
    skip = EDGE - HALO
    half = rows // 2
    load_audio = pltpu.make_async_copy(audio_ref.at[skip : skip + inner], audio, audio_sem)
    load_audio.start()
    load_w = pltpu.make_async_copy(w_ref, w_vmem, w_sem)
    load_w.start()
    bounds = recording_bounds(lengths_ref, starts_ref, ends_ref)
    spread_taps(taps_ref, full_taps, half_taps)
    start = where_ref[0] + EDGE
    load_audio.wait()
    few = 2 * SUBLANES
    for row in range(0, inner, few):
        value = audio[row : row + few, :].astype(jnp.float32)
        spread(value, full_src, row, SUBLANES, 0, False)
        if row < half + 2 * HALO:
            spread(value, half_src, row, SUBLANES // 2, SUBLANES, False)
        if row >= half:
            spread(value, half_src, row - half, SUBLANES // 2, SUBLANES, True)
    recs = len(bounds)
    common = (recs, bounds, starts_ref, ends_ref)
    conv_blocks(full_src, full_dst, full_taps, rows // BLOCK, [start], *common)
    conv_blocks(half_src, half_dst, half_taps, half // BLOCK, [start, start + half], *common)

    for side in range(2):

        def step(i, carry, side=side):
            row = i * few
            at = pl.ds(pl.multiple_of(side * half + row, few), few)
            sources = (
                (full_dst, side * half + row, 0, SUBLANES),
                (half_dst, row, side * SUBLANES // 2, SUBLANES // 2),
            )
            normalise(sources, few, mixed, normed, at)
            return carry

        lax.fori_loop(0, half // few, step, 0)

    width = pooled_ref.shape[1]
    own_columns = pl.ds(pl.multiple_of(where_ref[1] * width, LANES), width)
    pooled_ref[...] = jnp.dot(
        pool_rows(rows), mixed[:, own_columns], preferred_element_type=jnp.float32
    )
    load_w.wait()
    for side in range(2):
        at = slice(side * half, (side + 1) * half)
        position = start + side * half + lax.broadcasted_iota(jnp.int32, (half, LANES), 0)
        project_heads(normed[at, :], w_vmem, position, bounds, at, q_ref, kv_ref)


def edge_kernel(
    lengths_ref,
    where_ref,
    taps_ref,
    first_ref,
    last_ref,
    halo_ref,
    w_ref,
    q_ref,
    kv_ref,
    pooled_ref,
    full_src,
    full_dst,
    half_src,
    half_dst,
    full_taps,
    half_taps,
    mixed,
    normed,
    w_vmem,
    starts_ref,
    ends_ref,
    w_sem,
):
    load_w = pltpu.make_async_copy(w_ref, w_vmem, w_sem)
    load_w.start()
    bounds = recording_bounds(lengths_ref, starts_ref, ends_ref)
    spread_taps(taps_ref, full_taps, half_taps)
    frames = where_ref[2]
    starts = [where_ref[0], where_ref[0] + frames - EDGE]
    length = EDGE + 2 * HALO
    has_before = (starts[0] > 0).astype(jnp.float32)
    has_after = (starts[0] + frames < bounds[-1]).astype(jnp.float32)
    few = 2 * SUBLANES
    for side in range(2):
        for row in range(0, length, few):
            if side == 0 and row == 0:
                value = halo_ref[HALO:, :].astype(jnp.float32) * has_before
            elif side == 0:
                value = first_ref[row - HALO : row - HALO + few, :].astype(jnp.float32)
            elif row < length - HALO:
                value = last_ref[row : row + few, :].astype(jnp.float32)
            else:
                value = halo_ref[:HALO, :].astype(jnp.float32) * has_after
            spread(value, full_src.at[side], row, SUBLANES, 0, False)
            spread(value, half_src, row, SUBLANES // 2, SUBLANES, side == 1)
    recs = len(bounds)
    common = (recs, bounds, starts_ref, ends_ref)
    for side in range(2):
        conv_blocks(
            full_src.at[side],
            full_dst.at[side],
            full_taps,
            EDGE // BLOCK,
            [starts[side]],
            *common,
        )
    conv_blocks(half_src, half_dst, half_taps, EDGE // BLOCK, starts, *common)
    for side in range(2):
        for row in range(0, EDGE, few):
            at = slice(side * EDGE + row, side * EDGE + row + few)
            sources = (
                (full_dst.at[side], row, 0, SUBLANES),
                (half_dst, row, side * SUBLANES // 2, SUBLANES // 2),
            )
            normalise(sources, few, mixed, normed, at)
    width = pooled_ref.shape[1]
    own_columns = pl.ds(pl.multiple_of(where_ref[1] * width, LANES), width)
    pooled_ref[...] = jnp.dot(
        pool_rows(2 * EDGE), mixed[:, own_columns], preferred_element_type=jnp.float32
    )
    load_w.wait()
    row = lax.broadcasted_iota(jnp.int32, (2 * EDGE, LANES), 0)
    position = jnp.where(row < EDGE, starts[0] + row, starts[1] - EDGE + row)
    project_heads(normed[...], w_vmem, position, bounds, slice(None), q_ref, kv_ref)


def attend_kernel(count, rows, targets_ref, mid_q, edge_q, mid_mixed, edge_mixed, w_ref, *refs):
    kv_refs, out_refs = refs[: 2 * count], refs[2 * count : -6]
    queries, kv, mixed, pooled, w_vmem, w_sem = refs[-6:]
    frames = queries.shape[0]
    heads = queries.shape[1] // LANES
    width = mixed.shape[1]
    loads = [
        pltpu.make_async_copy(
            w_ref.at[h * HDE : (h + 1) * HDE], w_vmem.at[h * LANES : h * LANES + HDE], w_sem.at[h]
        )
        for h in range(heads)
    ]
    for load in loads:
        load.start()
    for h in range(heads):
        w_vmem[h * LANES + HDE : (h + 1) * LANES, :] = jnp.zeros(
            (LANES - HDE, w_vmem.shape[1]), jnp.bfloat16
        )
    for out, mid, edge, cut in (
        (queries, mid_q, edge_q, EDGE),
        (mixed, mid_mixed, edge_mixed, EDGE // STRIDE),
    ):
        out[:cut, :] = edge[:cut, :]
        out[cut : out.shape[0] - cut, :] = mid[...]
        out[out.shape[0] - cut :, :] = edge[cut:, :]
    at = 0
    for ref in kv_refs:
        kv[at : at + ref.shape[0], :] = ref[...]
        at += ref.shape[0]
    few = rows // STRIDE
    pool = pool_rows(rows)

    def step(i, carry):
        at = pl.ds(pl.multiple_of(i * rows, rows), rows)
        for h in range(heads):
            lanes = slice(h * LANES, (h + 1) * LANES)
            scores = lax.dot_general(
                queries[at, lanes],
                kv[:, lanes],
                (((1,), (1,)), ((), ())),
                preferred_element_type=jnp.float32,
            )
            peak = jnp.max(scores, axis=1, keepdims=True)
            weights = jnp.exp2(scores - peak).astype(jnp.bfloat16)
            values = kv[:, (heads + h) * LANES : (heads + h + 1) * LANES]
            out = jnp.dot(weights, values, preferred_element_type=jnp.float32)
            attended = (out * (1.0 / out[:, HDE : HDE + 1])).astype(jnp.bfloat16)
            pooled[pl.ds(pl.multiple_of(i * few, few), few), lanes] = jnp.dot(
                pool, attended, preferred_element_type=jnp.float32
            ).astype(jnp.bfloat16)
        return carry

    lax.fori_loop(0, frames // rows, step, 0)
    for load in loads:
        load.wait()
    for k, out_ref in enumerate(out_refs):
        columns = pl.ds(pl.multiple_of(targets_ref[k] * width, LANES), width)
        total = jnp.dot(pooled[...], w_vmem[:, columns], preferred_element_type=jnp.float32)
        if k == 0:
            total += mixed[...]
        out_ref[...] = total.astype(out_ref.dtype)


def project_kernel(targets_ref, *refs):
    *part_refs, w_ref, out_ref, squares_ref, pooled = refs
    width = part_refs[0].shape[1]
    for k, part_ref in enumerate(part_refs):
        at = pl.ds(pl.multiple_of(targets_ref[k] * width, LANES), width)
        pooled[:, at] = part_ref[...]
    total = jnp.dot(pooled[...], w_ref[...], preferred_element_type=jnp.float32)
    out_ref[...] = total
    rows = total.shape[0]
    squares = jnp.sum(total * total, axis=1, keepdims=True)
    squares_ref[...] = jnp.transpose(jnp.broadcast_to(squares, (rows, rows)))[:SUBLANES]


def route_kernel(cap, firsts_ref, place_ref, rows_ref, *refs):
    square_refs, out_refs = refs[: -firsts_ref.shape[0]], refs[-firsts_ref.shape[0] :]
    rows = rows_ref.shape[0]
    devices = sum(ref.shape[0] for ref in out_refs) // cap
    squares = square_refs[0][...]
    for ref in square_refs[1:]:
        squares += ref[...]
    scale = lax.rsqrt(squares[:1] / D + 1e-05)
    scale = jnp.transpose(jnp.broadcast_to(scale, (rows, rows)))[:, :1]
    normal_rows = (rows_ref[...] * scale).astype(jnp.bfloat16)
    destination = place_ref[...]
    named = lax.broadcasted_iota(jnp.int32, (devices, rows), 0) == destination
    earlier = lax.broadcasted_iota(jnp.int32, (rows, rows), 0) < lax.broadcasted_iota(
        jnp.int32, (rows, rows), 1
    )
    counts = jnp.dot(
        named.astype(jnp.float32).astype(jnp.bfloat16),
        earlier.astype(jnp.float32).astype(jnp.bfloat16),
        preferred_element_type=jnp.float32,
    )
    rank = jnp.sum(jnp.where(named, counts, 0.0), axis=0, keepdims=True).astype(jnp.int32)
    target = destination * cap + rank
    for k, out_ref in enumerate(out_refs):
        slots = out_ref.shape[0]
        slot = firsts_ref[k] + lax.broadcasted_iota(jnp.int32, (slots, rows), 0)
        one_hot = (slot == target).astype(jnp.float32).astype(jnp.bfloat16)
        out_ref[...] = jnp.dot(
            one_hot, normal_rows, preferred_element_type=jnp.float32
        ).astype(jnp.bfloat16)


def collect_kernel(firsts_ref, *refs):
    *block_refs, out_ref = refs
    for k, block_ref in enumerate(block_refs):
        slots = block_ref.shape[0]
        at = pl.ds(pl.multiple_of(firsts_ref[k], slots), slots)
        out_ref[at, :] = block_ref[...]


def partner(index, k, devices):
    if devices & (devices - 1) == 0:
        return index ^ k
    return (index + k) % devices


def sender(index, k, devices):
    if devices & (devices - 1) == 0:
        return index ^ k
    return (index - k) % devices


def exchange(value, axes, k, devices):
    return lax.ppermute(value, axes, [(i, partner(i, k, devices)) for i in range(devices)])


def local(audio, lengths, conv_kernel, w_qkv, w_out, place, w_adapt):
    frame_count, channels = audio.shape
    seq_devices = lax.axis_size("tm")
    mp_devices = lax.axis_size("mp")
    recs = lengths.shape[1]
    group_frames = frame_count * seq_devices
    width = channels // mp_devices
    pooled_rows = frame_count // STRIDE
    heads = w_qkv.shape[2] // HDE
    where = jnp.stack(
        [lax.axis_index("tm") * frame_count, lax.axis_index("mp"), jnp.int32(frame_count)]
    )

    if seq_devices == 2:
        ends = jnp.concatenate([audio[:HALO], audio[frame_count - HALO :]], axis=0)
        halo = exchange(ends, "tm", 1, 2)
    else:
        up = [(i, i + 1) for i in range(seq_devices - 1)]
        down = [(j, i) for i, j in up]
        after = lax.ppermute(audio[:HALO], "tm", down)
        before = lax.ppermute(audio[frame_count - HALO :], "tm", up)
        halo = jnp.concatenate([after, before], axis=0)

    smem = pl.BlockSpec(memory_space=pltpu.SMEM)
    vmem = pl.BlockSpec(memory_space=pltpu.VMEM)
    anywhere = pl.BlockSpec(memory_space=pl.ANY)
    w_three = jnp.transpose(w_qkv, (1, 0, 2))
    taps = conv_kernel.shape[0]

    def tiles(count, *lead):
        return pltpu.VMEM((*lead, count * SUBLANES, LANES), jnp.float32)

    def results(rows):
        return [
            jax.ShapeDtypeStruct((rows, heads * LANES), jnp.bfloat16),
            jax.ShapeDtypeStruct((rows, 2 * heads * LANES), jnp.bfloat16),
            jax.ShapeDtypeStruct((rows // STRIDE, width), jnp.float32),
        ]

    def shared(rows):
        return [
            tiles(taps),
            tiles(taps),
            pltpu.VMEM((rows, channels), jnp.bfloat16),
            pltpu.VMEM((rows, channels), jnp.bfloat16),
            pltpu.VMEM(w_three.shape, jnp.bfloat16),
            pltpu.SMEM((recs,), jnp.int32),
            pltpu.SMEM((recs,), jnp.int32),
        ]

    mid = frame_count - 2 * EDGE
    mid_q, mid_kv, mid_mixed = pl.pallas_call(
        interior_kernel,
        out_shape=results(mid),
        in_specs=[smem, smem, vmem, anywhere, anywhere],
        out_specs=[vmem] * 3,
        scratch_shapes=[
            pltpu.VMEM((mid + 2 * HALO, channels), jnp.bfloat16),
            tiles(mid + 2 * HALO),
            tiles(mid),
            tiles(mid // 2 + 2 * HALO),
            tiles(mid // 2),
            *shared(mid),
            pltpu.SemaphoreType.DMA,
            pltpu.SemaphoreType.DMA,
        ],
        compiler_params=pltpu.CompilerParams(vmem_limit_bytes=24 * MIB),
        cost_estimate=pl.CostEstimate(
            flops=6 * mid * channels * w_qkv.shape[2], bytes_accessed=40 * MIB, transcendentals=0
        ),
        name="interior",
    )(lengths, where, conv_kernel, audio, w_three)
    edge_q, edge_kv, edge_mixed = pl.pallas_call(
        edge_kernel,
        out_shape=results(2 * EDGE),
        in_specs=[smem, smem] + [vmem] * 4 + [anywhere],
        out_specs=[vmem] * 3,
        scratch_shapes=[
            tiles(EDGE + 2 * HALO, 2),
            tiles(EDGE, 2),
            tiles(EDGE + 2 * HALO),
            tiles(EDGE),
            *shared(2 * EDGE),
            pltpu.SemaphoreType.DMA,
        ],
        compiler_params=pltpu.CompilerParams(vmem_limit_bytes=12 * MIB),
        cost_estimate=pl.CostEstimate(
            flops=12 * EDGE * channels * w_qkv.shape[2], bytes_accessed=8 * MIB, transcendentals=0
        ),
        name="edges",
    )(
        lengths,
        where,
        conv_kernel,
        audio[: EDGE + HALO],
        audio[frame_count - EDGE - HALO :],
        halo,
        w_three,
    )

    kv_blocks = [mid_kv, edge_kv]
    for k in range(1, seq_devices):
        kv_blocks += [exchange(block, "tm", k, seq_devices) for block in (mid_kv, edge_kv)]
    mp_index = lax.axis_index("mp")
    mp_targets = jnp.stack([partner(mp_index, k, mp_devices) for k in range(mp_devices)])
    mp_senders = jnp.stack([sender(mp_index, k, mp_devices) for k in range(mp_devices)])
    part = (pooled_rows, width)
    own_part, *parts = pl.pallas_call(
        functools.partial(attend_kernel, seq_devices, 256 if seq_devices <= 2 else 64),
        out_shape=[jax.ShapeDtypeStruct(part, jnp.float32)]
        + [jax.ShapeDtypeStruct(part, jnp.bfloat16)] * (mp_devices - 1),
        in_specs=[smem] + [vmem] * 4 + [anywhere] + [vmem] * len(kv_blocks),
        out_specs=[vmem] * mp_devices,
        scratch_shapes=[
            pltpu.VMEM((frame_count, heads * LANES), jnp.bfloat16),
            pltpu.VMEM((group_frames, 2 * heads * LANES), jnp.bfloat16),
            pltpu.VMEM(part, jnp.float32),
            pltpu.VMEM((pooled_rows, heads * LANES), jnp.bfloat16),
            pltpu.VMEM((heads * LANES, channels), jnp.bfloat16),
            pltpu.SemaphoreType.DMA((heads,)),
        ],
        compiler_params=pltpu.CompilerParams(
            vmem_limit_bytes=(24 if seq_devices <= 2 else 48) * MIB
        ),
        name="attend",
    )(mp_targets, mid_q, edge_q, mid_mixed, edge_mixed, w_out, *kv_blocks)
    others = range(1, mp_devices)
    for k in others:
        own_part += exchange(parts[k - 1], "mp", k, mp_devices).astype(jnp.float32)
    own_part = own_part.astype(jnp.bfloat16)
    pooled = [own_part] + [exchange(own_part, "mp", k, mp_devices) for k in others]

    columns = w_adapt.shape[1]
    projected, squares = pl.pallas_call(
        project_kernel,
        out_shape=[
            jax.ShapeDtypeStruct((pooled_rows, columns), jnp.float32),
            jax.ShapeDtypeStruct((SUBLANES, pooled_rows), jnp.float32),
        ],
        in_specs=[smem] + [vmem] * (mp_devices + 1),
        out_specs=[vmem] * 2,
        scratch_shapes=[pltpu.VMEM((pooled_rows, channels), jnp.bfloat16)],
        compiler_params=pltpu.CompilerParams(vmem_limit_bytes=16 * MIB),
        name="project",
    )(mp_senders, *pooled, w_adapt)
    squares = [squares] + [exchange(squares, "mp", k, mp_devices) for k in others]

    axes = ("section", "tm")
    device_count = lax.axis_size("section") * seq_devices
    me = lax.axis_index(axes)
    cap = max(2, (2 * pooled_rows + device_count - 1) // device_count)
    direct = device_count <= 8
    if direct:
        firsts = jnp.stack([partner(me, k, device_count) * cap for k in range(device_count)])
        blocks = [jax.ShapeDtypeStruct((cap, columns), jnp.bfloat16)] * device_count
    else:
        firsts = jnp.zeros((1,), jnp.int32)
        blocks = [jax.ShapeDtypeStruct((device_count * cap, columns), jnp.bfloat16)]
    blocks = pl.pallas_call(
        functools.partial(route_kernel, cap),
        out_shape=blocks,
        in_specs=[smem] + [vmem] * (mp_devices + 2),
        out_specs=[vmem] * len(blocks),
        compiler_params=pltpu.CompilerParams(vmem_limit_bytes=16 * MIB),
        name="route",
    )(firsts, place.T, projected, *squares)
    if not direct:
        return lax.all_to_all(blocks[0], axes, split_axis=0, concat_axis=0, tiled=True)
    arrived = [blocks[0]] + [
        exchange(blocks[k], axes, k, device_count) for k in range(1, device_count)
    ]
    firsts = jnp.stack([sender(me, k, device_count) * cap for k in range(device_count)])
    return pl.pallas_call(
        collect_kernel,
        out_shape=jax.ShapeDtypeStruct((device_count * cap, columns), jnp.bfloat16),
        in_specs=[smem] + [vmem] * device_count,
        out_specs=vmem,
        compiler_params=pltpu.CompilerParams(vmem_limit_bytes=8 * MIB),
        name="collect",
    )(firsts, *arrived)


def solution(mesh):
    placed = (
        P(("section", "tm"), None),
        P("section", None),
        P(),
        P(None, None, "mp"),
        P("mp", None),
        P(("section", "tm"), None),
        P(None, "mp"),
    )
    return jax.shard_map(
        local, mesh=mesh, in_specs=placed, out_specs=P(("section", "tm"), "mp"), check_vma=False
    )
```

```python
import functools
import math

import jax
import jax.numpy as jnp
from jax import lax
from jax.experimental import pallas as pl
from jax.experimental.pallas import tpu as pltpu
from jax.sharding import PartitionSpec as P

HDE = 96
D = 5120
STRIDE = 4
LANES = 128
SUBLANES = 8
HALO = 16
EDGE = 32
BLOCK = 16
GROUP = 16
MIB = 1 << 20
HIDDEN = -1e30


def conv_blocks(src, dst, taps, blocks, firsts, recs, bounds, starts_ref, ends_ref):
    count = taps.shape[0] // SUBLANES
    reach = count // 2
    span = BLOCK + count - 1
    shape = (SUBLANES, LANES)
    upper = lax.broadcasted_iota(jnp.int32, shape, 0) < SUBLANES // 2

    def both(values):
        if len(values) == 1:
            return jnp.full(shape, values[0], jnp.int32)
        return jnp.where(upper, values[0], values[1])

    def block(i, carry):
        base = i * BLOCK
        positions = [first + base for first in firsts]

        def frame(k):
            at = (base + k + HALO - reach) * SUBLANES
            return src[pl.ds(pl.multiple_of(at, SUBLANES), SUBLANES), :]

        def out(t):
            return pl.ds(pl.multiple_of((base + t) * SUBLANES, SUBLANES), SUBLANES)

        def convolve(inside):
            kernel = [taps[j * SUBLANES : (j + 1) * SUBLANES, :] for j in range(count)]
            totals = [None] * BLOCK
            for k in range(span):
                value = frame(k)
                if inside is not None:
                    value = jnp.where(inside(k), value, 0.0)
                for t in range(max(0, k - count + 1), min(BLOCK, k + 1)):
                    term = kernel[k - t] * value
                    totals[t] = term if totals[t] is None else totals[t] + term
            for t in range(BLOCK):
                half = 0.5 * totals[t]
                value = frame(t + reach) + half * (1.0 + jnp.tanh(half))
                if inside is not None:
                    value = jnp.where(inside(t + reach), value, dst[out(t), :])
                dst[out(t), :] = value

        touched = jnp.zeros((), jnp.bool_)
        for position in positions:
            for bound in bounds[:-1]:
                at = bound - position
                touched = touched | ((at > -reach) & (at < BLOCK + reach))

        @pl.when(jnp.logical_not(touched))
        def _():
            convolve(None)

        @pl.when(touched)
        def _():
            begin, extra = [], jnp.zeros((), jnp.int32)
            for position in positions:
                first = last = jnp.zeros((), jnp.int32)
                for bound in bounds[:-1]:
                    first += (bound <= position).astype(jnp.int32)
                    last += (bound <= position + BLOCK - 1).astype(jnp.int32)
                begin.append(first)
                extra = jnp.maximum(extra, last - first)

            def once(turn, carry):
                which = [jnp.minimum(first + turn, recs - 1) for first in begin]
                low = both([starts_ref[r] - p for r, p in zip(which, positions)])
                high = both([ends_ref[r] - p for r, p in zip(which, positions)])
                convolve(lambda k: (low <= k - reach) & (high > k - reach))
                return carry

            lax.fori_loop(0, extra + 1, once, 0)

        return carry

    lax.fori_loop(0, blocks, block, 0)


def shuffle(back):
    row = lax.broadcasted_iota(jnp.int32, (LANES, LANES), 1 if back else 0)
    column = lax.broadcasted_iota(jnp.int32, (LANES, LANES), 0 if back else 1)
    moved = (row // SUBLANES == column % GROUP) & (row % SUBLANES == column // GROUP)
    return moved.astype(jnp.float32).astype(jnp.bfloat16)


def to_tiles(matrix, values, ref, frame):
    stack = jnp.concatenate(values, axis=0)
    at = pl.ds(frame * SUBLANES, GROUP * SUBLANES)
    ref[at, :] = jnp.dot(matrix, stack, preferred_element_type=jnp.float32)


def from_tiles(matrix, ref, frame):
    rows = GROUP * SUBLANES
    low = ref[pl.ds(pl.multiple_of(frame * SUBLANES, rows), rows), :].astype(jnp.bfloat16)
    moved = jnp.dot(matrix, low, preferred_element_type=jnp.float32)
    return [moved[k * GROUP : (k + 1) * GROUP] for k in range(SUBLANES)]


def blocks_of(value, first, count):
    return [value[:, k * LANES : (k + 1) * LANES] for k in range(first, first + count)]


def recording_bounds(where_ref, starts_ref, ends_ref):
    bounds, total = [], jnp.zeros((), jnp.int32)
    for r in range(where_ref.shape[0] - 2):
        starts_ref[r] = total
        total = total + where_ref[2 + r]
        ends_ref[r] = total
        bounds.append(total)
    return bounds


def spread_taps(taps_ref, full_taps, half_taps):
    count = taps_ref.shape[0]
    blocks = taps_ref.shape[1] // LANES
    for k in range(blocks):
        value = taps_ref[:, k * LANES : (k + 1) * LANES]
        if k < SUBLANES:
            full_taps[pl.ds(k, count, stride=SUBLANES), :] = value
        else:
            for half in range(2):
                at = k - SUBLANES + half * SUBLANES // 2
                half_taps[pl.ds(at, count, stride=SUBLANES), :] = value


def normalise(blocks, mixed, normed, at):
    values = jnp.concatenate(blocks, axis=1)
    mixed[at, :] = values.astype(jnp.bfloat16)
    centred = values - jnp.mean(values, -1, keepdims=True)
    variance = jnp.mean(centred * centred, -1, keepdims=True)
    normed[at, :] = (centred * lax.rsqrt(variance + 1e-05)).astype(jnp.bfloat16)


def pool_rows(rows):
    few = rows // STRIDE
    chosen = (
        lax.broadcasted_iota(jnp.int32, (few, rows), 1) // STRIDE
        == lax.broadcasted_iota(jnp.int32, (few, rows), 0)
    )
    return (chosen.astype(jnp.float32) * (1.0 / STRIDE)).astype(jnp.bfloat16)


def project_heads(normed_rows, w_vmem, position, bounds, at, q_ref, kv_ref):
    recs = len(bounds)
    heads = w_vmem.shape[2] // HDE
    lane = lax.broadcasted_iota(jnp.int32, position.shape, 1)
    mine = jnp.zeros(position.shape, jnp.int32)
    for bound in bounds:
        mine += (position >= bound).astype(jnp.int32)
    same = lane - HDE == mine
    extra_q = jnp.where(same | (lane >= HDE + recs), 0.0, HIDDEN)
    extra_k = jnp.where(same, 1.0, 0.0)
    extra_v = jnp.where(lane == HDE, 1.0, 0.0)
    score_scale = HDE ** (-0.5) * math.log2(math.e)
    for kind, extra in enumerate((extra_q, extra_k, extra_v)):
        result = jnp.dot(normed_rows, w_vmem[kind], preferred_element_type=jnp.float32)
        if kind == 0:
            result = result * score_scale
        for h in range(heads):
            tile, start = divmod(h * HDE, LANES)
            tiles = 1 if start + HDE <= LANES else 2
            head = result[:, tile * LANES : (tile + tiles) * LANES]
            if start:
                head = pltpu.roll(head, tiles * LANES - start, 1)
            head = jnp.where(lane < HDE, head[:, :LANES], extra).astype(jnp.bfloat16)
            if kind == 0:
                q_ref[at, h * LANES : (h + 1) * LANES] = head
            else:
                first = ((kind - 1) * heads + h) * LANES
                kv_ref[at, first : first + LANES] = head


def interior_kernel(
    where_ref,
    taps_hbm,
    audio_ref,
    w_ref,
    q_ref,
    kv_ref,
    pooled_ref,
    audio,
    full_src,
    full_dst,
    half_src,
    half_dst,
    taps_ref,
    full_taps,
    half_taps,
    mixed,
    normed,
    w_vmem,
    starts_ref,
    ends_ref,
    audio_sem,
    taps_sem,
    w_sem,
):
    rows = q_ref.shape[0]
    inner = rows + 2 * HALO
    skip = EDGE - HALO
    half = rows // 2
    load_audio = pltpu.make_async_copy(audio_ref.at[skip : skip + inner], audio, audio_sem)
    load_taps = pltpu.make_async_copy(taps_hbm, taps_ref, taps_sem)
    load_audio.start()
    load_taps.start()
    load_w = pltpu.make_async_copy(w_ref, w_vmem, w_sem)
    load_w.start()
    bounds = recording_bounds(where_ref, starts_ref, ends_ref)
    start = where_ref[0] + EDGE
    forward, back = shuffle(False), shuffle(True)
    load_audio.wait()
    side = SUBLANES // 2
    for row in range(0, inner, GROUP):
        value = audio[row : row + GROUP, : SUBLANES * LANES]
        to_tiles(forward, blocks_of(value, 0, SUBLANES), full_src, row)
    for row in range(0, half + 2 * HALO, GROUP):
        pair = [
            block
            for at in (row, row + half)
            for block in blocks_of(audio[at : at + GROUP, :], SUBLANES, side)
        ]
        to_tiles(forward, pair, half_src, row)
    load_taps.wait()
    spread_taps(taps_ref, full_taps, half_taps)
    recs = len(bounds)
    common = (recs, bounds, starts_ref, ends_ref)
    conv_blocks(full_src, full_dst, full_taps, rows // BLOCK, [start], *common)
    conv_blocks(half_src, half_dst, half_taps, half // BLOCK, [start, start + half], *common)


    def step(i, carry):
        row = i * GROUP
        pair = from_tiles(back, half_dst, row)
        for which in range(2):
            at = which * half + row
            blocks = from_tiles(back, full_dst, at) + pair[which * side : (which + 1) * side]
            normalise(blocks, mixed, normed, pl.ds(pl.multiple_of(at, GROUP), GROUP))
        return carry

    lax.fori_loop(0, half // GROUP, step, 0)

    width = pooled_ref.shape[1]
    own_columns = pl.ds(pl.multiple_of(where_ref[1] * width, LANES), width)
    pooled_ref[...] = jnp.dot(
        pool_rows(rows), mixed[:, own_columns], preferred_element_type=jnp.float32
    )
    load_w.wait()
    for which in range(2):
        at = slice(which * half, (which + 1) * half)
        position = start + which * half + lax.broadcasted_iota(jnp.int32, (half, LANES), 0)
        project_heads(normed[at, :], w_vmem, position, bounds, at, q_ref, kv_ref)


def edge_kernel(
    where_ref,
    taps_hbm,
    audio_ref,
    halo_ref,
    w_ref,
    q_ref,
    kv_ref,
    pooled_ref,
    audio,
    full_src,
    full_dst,
    half_src,
    half_dst,
    taps_ref,
    full_taps,
    half_taps,
    mixed,
    normed,
    w_vmem,
    starts_ref,
    ends_ref,
    first_sem,
    last_sem,
    taps_sem,
    w_sem,
):
    frames = audio_ref.shape[0]
    known = EDGE + HALO
    loads = [
        pltpu.make_async_copy(audio_ref.at[:known], audio.at[:known], first_sem),
        pltpu.make_async_copy(audio_ref.at[frames - known :], audio.at[known:], last_sem),
        pltpu.make_async_copy(taps_hbm, taps_ref, taps_sem),
        pltpu.make_async_copy(w_ref, w_vmem, w_sem),
    ]
    for load in loads:
        load.start()
    bounds = recording_bounds(where_ref, starts_ref, ends_ref)
    forward, back = shuffle(False), shuffle(True)
    starts = [where_ref[0], where_ref[0] + frames - EDGE]
    length = EDGE + 2 * HALO
    has_before = (starts[0] > 0).astype(jnp.float32)
    has_after = (starts[0] + frames < bounds[-1]).astype(jnp.float32)
    before = (halo_ref[HALO:, :].astype(jnp.float32) * has_before).astype(jnp.bfloat16)
    after = (halo_ref[:HALO, :].astype(jnp.float32) * has_after).astype(jnp.bfloat16)
    for load in loads[:3]:
        load.wait()
    side = SUBLANES // 2
    for row in range(0, length, GROUP):
        first = before if row == 0 else audio[row - HALO : row - HALO + GROUP, :]
        last = after if row == known else audio[known + row : known + row + GROUP, :]
        for which, value in enumerate((first, last)):
            to_tiles(forward, blocks_of(value, 0, SUBLANES), full_src.at[which], row)
        pair = blocks_of(first, SUBLANES, side) + blocks_of(last, SUBLANES, side)
        to_tiles(forward, pair, half_src, row)
    spread_taps(taps_ref, full_taps, half_taps)
    recs = len(bounds)
    common = (recs, bounds, starts_ref, ends_ref)
    for which in range(2):
        conv_blocks(
            full_src.at[which],
            full_dst.at[which],
            full_taps,
            EDGE // BLOCK,
            [starts[which]],
            *common,
        )
    conv_blocks(half_src, half_dst, half_taps, EDGE // BLOCK, starts, *common)
    for row in range(0, EDGE, GROUP):
        pair = from_tiles(back, half_dst, row)
        for which in range(2):
            blocks = from_tiles(back, full_dst.at[which], row)
            blocks += pair[which * side : (which + 1) * side]
            at = which * EDGE + row
            normalise(blocks, mixed, normed, slice(at, at + GROUP))
    width = pooled_ref.shape[1]
    own_columns = pl.ds(pl.multiple_of(where_ref[1] * width, LANES), width)
    pooled_ref[...] = jnp.dot(
        pool_rows(2 * EDGE), mixed[:, own_columns], preferred_element_type=jnp.float32
    )
    loads[3].wait()
    row = lax.broadcasted_iota(jnp.int32, (2 * EDGE, LANES), 0)
    position = jnp.where(row < EDGE, starts[0] + row, starts[1] - EDGE + row)
    project_heads(normed[...], w_vmem, position, bounds, slice(None), q_ref, kv_ref)


def attend_kernel(count, rows, targets_ref, mid_q, edge_q, mid_mixed, edge_mixed, w_ref, *refs):
    kv_refs, out_refs = refs[: 2 * count], refs[2 * count : -6]
    queries, kv, mixed, pooled, w_vmem, w_sem = refs[-6:]
    frames = queries.shape[0]
    heads = queries.shape[1] // LANES
    width = mixed.shape[1]
    loads = [
        pltpu.make_async_copy(
            w_ref.at[h * HDE : (h + 1) * HDE], w_vmem.at[h * LANES : h * LANES + HDE], w_sem.at[h]
        )
        for h in range(heads)
    ]
    for load in loads:
        load.start()
    for h in range(heads):
        w_vmem[h * LANES + HDE : (h + 1) * LANES, :] = jnp.zeros(
            (LANES - HDE, w_vmem.shape[1]), jnp.bfloat16
        )
    for out, mid, edge, cut in (
        (queries, mid_q, edge_q, EDGE),
        (mixed, mid_mixed, edge_mixed, EDGE // STRIDE),
    ):
        out[:cut, :] = edge[:cut, :]
        out[cut : out.shape[0] - cut, :] = mid[...]
        out[out.shape[0] - cut :, :] = edge[cut:, :]
    at = 0
    for ref in kv_refs:
        kv[at : at + ref.shape[0], :] = ref[...]
        at += ref.shape[0]
    few = rows // STRIDE
    pool = pool_rows(rows)

    def step(i, carry):
        at = pl.ds(pl.multiple_of(i * rows, rows), rows)
        for h in range(heads):
            lanes = slice(h * LANES, (h + 1) * LANES)
            scores = lax.dot_general(
                queries[at, lanes],
                kv[:, lanes],
                (((1,), (1,)), ((), ())),
                preferred_element_type=jnp.float32,
            )
            peak = jnp.max(scores, axis=1, keepdims=True)
            weights = jnp.exp2(scores - peak).astype(jnp.bfloat16)
            values = kv[:, (heads + h) * LANES : (heads + h + 1) * LANES]
            out = jnp.dot(weights, values, preferred_element_type=jnp.float32)
            attended = (out * (1.0 / out[:, HDE : HDE + 1])).astype(jnp.bfloat16)
            pooled[pl.ds(pl.multiple_of(i * few, few), few), lanes] = jnp.dot(
                pool, attended, preferred_element_type=jnp.float32
            ).astype(jnp.bfloat16)
        return carry

    lax.fori_loop(0, frames // rows, step, 0)
    for load in loads:
        load.wait()
    for k, out_ref in enumerate(out_refs):
        columns = pl.ds(pl.multiple_of(targets_ref[k] * width, LANES), width)
        total = jnp.dot(pooled[...], w_vmem[:, columns], preferred_element_type=jnp.float32)
        if k == 0:
            total += mixed[...]
        out_ref[...] = total.astype(out_ref.dtype)


def project_kernel(targets_ref, *refs):
    *part_refs, w_ref, out_ref, squares_ref, pooled = refs
    width = part_refs[0].shape[1]
    for k, part_ref in enumerate(part_refs):
        at = pl.ds(pl.multiple_of(targets_ref[k] * width, LANES), width)
        pooled[:, at] = part_ref[...]
    total = jnp.dot(pooled[...], w_ref[...], preferred_element_type=jnp.float32)
    out_ref[...] = total
    rows = total.shape[0]
    squares = jnp.sum(total * total, axis=1, keepdims=True)
    squares_ref[...] = jnp.transpose(jnp.broadcast_to(squares, (rows, rows)))[:SUBLANES]


def route_kernel(cap, firsts_ref, place_ref, rows_ref, *refs):
    square_refs, out_refs = refs[: -firsts_ref.shape[0]], refs[-firsts_ref.shape[0] :]
    rows = rows_ref.shape[0]
    devices = sum(ref.shape[0] for ref in out_refs) // cap
    squares = square_refs[0][...]
    for ref in square_refs[1:]:
        squares += ref[...]
    scale = lax.rsqrt(squares[:1] / D + 1e-05)
    scale = jnp.transpose(jnp.broadcast_to(scale, (rows, rows)))[:, :1]
    normal_rows = (rows_ref[...] * scale).astype(jnp.bfloat16)
    destination = place_ref[...]
    named = lax.broadcasted_iota(jnp.int32, (devices, rows), 0) == destination
    earlier = lax.broadcasted_iota(jnp.int32, (rows, rows), 0) < lax.broadcasted_iota(
        jnp.int32, (rows, rows), 1
    )
    counts = jnp.dot(
        named.astype(jnp.float32).astype(jnp.bfloat16),
        earlier.astype(jnp.float32).astype(jnp.bfloat16),
        preferred_element_type=jnp.float32,
    )
    rank = jnp.sum(jnp.where(named, counts, 0.0), axis=0, keepdims=True).astype(jnp.int32)
    target = destination * cap + rank
    for k, out_ref in enumerate(out_refs):
        slots = out_ref.shape[0]
        slot = firsts_ref[k] + lax.broadcasted_iota(jnp.int32, (slots, rows), 0)
        one_hot = (slot == target).astype(jnp.float32).astype(jnp.bfloat16)
        out_ref[...] = jnp.dot(
            one_hot, normal_rows, preferred_element_type=jnp.float32
        ).astype(jnp.bfloat16)


def collect_kernel(firsts_ref, *refs):
    *block_refs, out_ref = refs
    for k, block_ref in enumerate(block_refs):
        slots = block_ref.shape[0]
        at = pl.ds(pl.multiple_of(firsts_ref[k], slots), slots)
        out_ref[at, :] = block_ref[...]


def partner(index, k, devices):
    if devices & (devices - 1) == 0:
        return index ^ k
    return (index + k) % devices


def sender(index, k, devices):
    if devices & (devices - 1) == 0:
        return index ^ k
    return (index - k) % devices


def exchange(value, axes, k, devices):
    return lax.ppermute(value, axes, [(i, partner(i, k, devices)) for i in range(devices)])


def local(audio, lengths, conv_kernel, w_qkv, w_out, place, w_adapt):
    frame_count, channels = audio.shape
    seq_devices = lax.axis_size("tm")
    mp_devices = lax.axis_size("mp")
    recs = lengths.shape[1]
    group_frames = frame_count * seq_devices
    width = channels // mp_devices
    pooled_rows = frame_count // STRIDE
    heads = w_qkv.shape[2] // HDE
    where = jnp.concatenate(
        [jnp.stack([lax.axis_index("tm") * frame_count, lax.axis_index("mp")]), lengths[0]]
    )

    if seq_devices == 2:
        ends = jnp.concatenate([audio[:HALO], audio[frame_count - HALO :]], axis=0)
        halo = exchange(ends, "tm", 1, 2)
    else:
        up = [(i, i + 1) for i in range(seq_devices - 1)]
        down = [(j, i) for i, j in up]
        after = lax.ppermute(audio[:HALO], "tm", down)
        before = lax.ppermute(audio[frame_count - HALO :], "tm", up)
        halo = jnp.concatenate([after, before], axis=0)

    smem = pl.BlockSpec(memory_space=pltpu.SMEM)
    vmem = pl.BlockSpec(memory_space=pltpu.VMEM)
    hbm = pl.BlockSpec(memory_space=pltpu.HBM)
    w_three = jnp.transpose(w_qkv, (1, 0, 2))
    taps = conv_kernel.shape[0]

    def tiles(count, *lead):
        return pltpu.VMEM((*lead, count * SUBLANES, LANES), jnp.float32)

    def results(rows):
        return [
            jax.ShapeDtypeStruct((rows, heads * LANES), jnp.bfloat16),
            jax.ShapeDtypeStruct((rows, 2 * heads * LANES), jnp.bfloat16),
            jax.ShapeDtypeStruct((rows // STRIDE, width), jnp.float32),
        ]

    def shared(rows):
        return [
            pltpu.VMEM(conv_kernel.shape, jnp.float32),
            tiles(taps),
            tiles(taps),
            pltpu.VMEM((rows, channels), jnp.bfloat16),
            pltpu.VMEM((rows, channels), jnp.bfloat16),
            pltpu.VMEM(w_three.shape, jnp.bfloat16),
            pltpu.SMEM((recs,), jnp.int32),
            pltpu.SMEM((recs,), jnp.int32),
        ]

    mid = frame_count - 2 * EDGE
    mid_q, mid_kv, mid_mixed = pl.pallas_call(
        interior_kernel,
        out_shape=results(mid),
        in_specs=[smem, hbm, hbm, hbm],
        out_specs=[vmem] * 3,
        scratch_shapes=[
            pltpu.VMEM((mid + 2 * HALO, channels), jnp.bfloat16),
            tiles(mid + 2 * HALO),
            tiles(mid),
            tiles(mid // 2 + 2 * HALO),
            tiles(mid // 2),
            *shared(mid),
            *[pltpu.SemaphoreType.DMA] * 3,
        ],
        compiler_params=pltpu.CompilerParams(vmem_limit_bytes=53 * MIB),
        cost_estimate=pl.CostEstimate(
            flops=6 * mid * channels * w_qkv.shape[2], bytes_accessed=40 * MIB, transcendentals=0
        ),
        name="interior",
    )(where, conv_kernel, audio, w_three)
    edge_q, edge_kv, edge_mixed = pl.pallas_call(
        edge_kernel,
        out_shape=results(2 * EDGE),
        in_specs=[smem, hbm, hbm, vmem, hbm],
        out_specs=[vmem] * 3,
        scratch_shapes=[
            pltpu.VMEM((2 * (EDGE + HALO), channels), jnp.bfloat16),
            tiles(EDGE + 2 * HALO, 2),
            tiles(EDGE, 2),
            tiles(EDGE + 2 * HALO),
            tiles(EDGE),
            *shared(2 * EDGE),
            *[pltpu.SemaphoreType.DMA] * 4,
        ],
        compiler_params=pltpu.CompilerParams(vmem_limit_bytes=53 * MIB),
        cost_estimate=pl.CostEstimate(
            flops=12 * EDGE * channels * w_qkv.shape[2], bytes_accessed=8 * MIB, transcendentals=0
        ),
        name="edges",
    )(
        where,
        conv_kernel,
        audio,
        halo,
        w_three,
    )

    kv_blocks = [mid_kv, edge_kv]
    for k in range(1, seq_devices):
        kv_blocks += [exchange(block, "tm", k, seq_devices) for block in (mid_kv, edge_kv)]
    mp_index = lax.axis_index("mp")
    mp_targets = jnp.stack([partner(mp_index, k, mp_devices) for k in range(mp_devices)])
    mp_senders = jnp.stack([sender(mp_index, k, mp_devices) for k in range(mp_devices)])
    part = (pooled_rows, width)
    own_part, *parts = pl.pallas_call(
        functools.partial(attend_kernel, seq_devices, 256 if seq_devices <= 2 else 64),
        out_shape=[jax.ShapeDtypeStruct(part, jnp.float32)]
        + [jax.ShapeDtypeStruct(part, jnp.bfloat16)] * (mp_devices - 1),
        in_specs=[smem] + [vmem] * 4 + [hbm] + [vmem] * len(kv_blocks),
        out_specs=[vmem] * mp_devices,
        scratch_shapes=[
            pltpu.VMEM((frame_count, heads * LANES), jnp.bfloat16),
            pltpu.VMEM((group_frames, 2 * heads * LANES), jnp.bfloat16),
            pltpu.VMEM(part, jnp.float32),
            pltpu.VMEM((pooled_rows, heads * LANES), jnp.bfloat16),
            pltpu.VMEM((heads * LANES, channels), jnp.bfloat16),
            pltpu.SemaphoreType.DMA((heads,)),
        ],
        compiler_params=pltpu.CompilerParams(
            vmem_limit_bytes=44 * MIB
        ),
        name="attend",
    )(mp_targets, mid_q, edge_q, mid_mixed, edge_mixed, w_out, *kv_blocks)
    others = range(1, mp_devices)
    for k in others:
        own_part += exchange(parts[k - 1], "mp", k, mp_devices).astype(jnp.float32)
    own_part = own_part.astype(jnp.bfloat16)
    pooled = [own_part] + [exchange(own_part, "mp", k, mp_devices) for k in others]

    columns = w_adapt.shape[1]
    projected, squares = pl.pallas_call(
        project_kernel,
        out_shape=[
            jax.ShapeDtypeStruct((pooled_rows, columns), jnp.float32),
            jax.ShapeDtypeStruct((SUBLANES, pooled_rows), jnp.float32),
        ],
        in_specs=[smem] + [vmem] * (mp_devices + 1),
        out_specs=[vmem] * 2,
        scratch_shapes=[pltpu.VMEM((pooled_rows, channels), jnp.bfloat16)],
        compiler_params=pltpu.CompilerParams(vmem_limit_bytes=16 * MIB),
        name="project",
    )(mp_senders, *pooled, w_adapt)
    squares = [squares] + [exchange(squares, "mp", k, mp_devices) for k in others]

    axes = ("section", "tm")
    device_count = lax.axis_size("section") * seq_devices
    me = lax.axis_index(axes)
    cap = max(2, (2 * pooled_rows + device_count - 1) // device_count)
    direct = device_count <= 8
    if direct:
        firsts = jnp.stack([partner(me, k, device_count) * cap for k in range(device_count)])
        blocks = [jax.ShapeDtypeStruct((cap, columns), jnp.bfloat16)] * device_count
    else:
        firsts = jnp.zeros((1,), jnp.int32)
        blocks = [jax.ShapeDtypeStruct((device_count * cap, columns), jnp.bfloat16)]
    blocks = pl.pallas_call(
        functools.partial(route_kernel, cap),
        out_shape=blocks,
        in_specs=[smem] + [vmem] * (mp_devices + 2),
        out_specs=[vmem] * len(blocks),
        compiler_params=pltpu.CompilerParams(vmem_limit_bytes=16 * MIB),
        name="route",
    )(firsts, place.T, projected, *squares)
    if not direct:
        return lax.all_to_all(blocks[0], axes, split_axis=0, concat_axis=0, tiled=True)
    arrived = [blocks[0]] + [
        exchange(blocks[k], axes, k, device_count) for k in range(1, device_count)
    ]
    firsts = jnp.stack([sender(me, k, device_count) * cap for k in range(device_count)])
    return pl.pallas_call(
        collect_kernel,
        out_shape=jax.ShapeDtypeStruct((device_count * cap, columns), jnp.bfloat16),
        in_specs=[smem] + [vmem] * device_count,
        out_specs=vmem,
        compiler_params=pltpu.CompilerParams(vmem_limit_bytes=8 * MIB),
        name="collect",
    )(firsts, *arrived)


def solution(mesh):
    placed = (
        P(("section", "tm"), None),
        P("section", None),
        P(),
        P(None, None, "mp"),
        P("mp", None),
        P(("section", "tm"), None),
        P(None, "mp"),
    )
    return jax.shard_map(
        local, mesh=mesh, in_specs=placed, out_specs=P(("section", "tm"), "mp"), check_vma=False
    )
```

```python
import functools
import math

import jax
import jax.numpy as jnp
from jax import lax
from jax.experimental import pallas as pl
from jax.experimental.pallas import tpu as pltpu
from jax.sharding import PartitionSpec as P

HDE = 96
D = 5120
STRIDE = 4
LANES = 128
SUBLANES = 8
HALO = 16
EDGE = 32
BLOCK = 8
GROUP = 16
TILE = 16
MIB = 1 << 20
HIDDEN = -1e30


def conv_blocks(src, dst, taps, count, blocks, firsts, bounds, starts_ref, ends_ref):
    recs = len(bounds)
    reach = count // 2
    span = BLOCK + count - 1
    shape = (TILE, LANES)
    stretch = lax.broadcasted_iota(jnp.int32, shape, 0) // (TILE // len(firsts))

    def spread(values):
        out = jnp.full(shape, values[0], jnp.int32)
        for i, value in enumerate(values[1:]):
            out = jnp.where(stretch > i, value, out)
        return out

    def block(i, carry):
        base = i * BLOCK
        positions = [first + base for first in firsts]

        def frame(k):
            at = (base + k + HALO - reach) * TILE
            return src[pl.ds(pl.multiple_of(at, TILE), TILE), :]

        def convolve(inside):
            kernel = [taps[j * TILE : (j + 1) * TILE, :] for j in range(count)]
            totals = [[None] * BLOCK, [None] * BLOCK]
            for k in range(span):
                value = frame(k)
                if inside is not None:
                    value = value * jnp.where(inside(k), 1.0, 0.0).astype(jnp.bfloat16)
                for t in range(max(0, k - count + 1), min(BLOCK, k + 1)):
                    term = kernel[k - t] * value
                    part = totals[(k - t) // TILE]
                    part[t] = term if part[t] is None else part[t] + term
            for t in range(BLOCK):
                at = pl.ds(pl.multiple_of((base + t) * TILE, TILE), TILE)
                depthwise = totals[0][t].astype(jnp.float32) + totals[1][t].astype(jnp.float32)
                half = 0.5 * depthwise
                value = frame(t + reach).astype(jnp.float32) + half * (1.0 + jnp.tanh(half))
                if inside is not None:
                    value = jnp.where(inside(t + reach), value, dst[at, :].astype(jnp.float32))
                dst[at, :] = value.astype(jnp.bfloat16)

        touched = jnp.zeros((), jnp.bool_)
        for position in positions:
            for bound in bounds[:-1]:
                at = bound - position
                touched = touched | ((at > -reach) & (at < BLOCK + reach))

        @pl.when(jnp.logical_not(touched))
        def _():
            convolve(None)

        @pl.when(touched)
        def _():
            begin, extra = [], jnp.zeros((), jnp.int32)
            for position in positions:
                first = last = jnp.zeros((), jnp.int32)
                for bound in bounds[:-1]:
                    first += (bound <= position).astype(jnp.int32)
                    last += (bound <= position + BLOCK - 1).astype(jnp.int32)
                begin.append(first)
                extra = jnp.maximum(extra, last - first)

            def once(turn, carry):
                which = [jnp.minimum(first + turn, recs - 1) for first in begin]
                low = spread([starts_ref[r] - p for r, p in zip(which, positions)])
                high = spread([ends_ref[r] - p for r, p in zip(which, positions)])
                convolve(lambda k: (low <= k - reach) & (high > k - reach))
                return carry

            lax.fori_loop(0, extra + 1, once, 0)

        return carry

    lax.fori_loop(0, blocks, block, 0)


def shuffle(back):
    shape = (GROUP * TILE, GROUP * TILE)
    row = lax.broadcasted_iota(jnp.int32, shape, 1 if back else 0)
    column = lax.broadcasted_iota(jnp.int32, shape, 0 if back else 1)
    moved = (row // TILE == column % GROUP) & (row % TILE == column // GROUP)
    return moved.astype(jnp.float32).astype(jnp.bfloat16)


def to_tiles(matrix, values, ref, frame):
    stack = jnp.concatenate(values, axis=0)
    tiles = jnp.dot(matrix, stack, preferred_element_type=jnp.float32)
    ref[frame * TILE : (frame + GROUP) * TILE, :] = tiles.astype(jnp.bfloat16)


def from_tiles(matrix, ref, frame):
    rows = GROUP * TILE
    low = ref[pl.ds(pl.multiple_of(frame * TILE, rows), rows), :]
    moved = jnp.dot(matrix, low, preferred_element_type=jnp.float32)
    return [moved[k * GROUP : (k + 1) * GROUP] for k in range(TILE)]


def blocks_of(value, first, count):
    return [value[:, k * LANES : (k + 1) * LANES] for k in range(first, first + count)]


def fill_tiles(forward, window, half, full_src, half_src):
    quarter = half // 2
    for row in range(0, half + 2 * HALO, GROUP):
        values = [block for side in range(2) for block in blocks_of(window(side, row), 0, TILE // 2)]
        to_tiles(forward, values, full_src, row)
    for row in range(0, quarter + 2 * HALO, GROUP):
        values = [
            block
            for side in range(2)
            for skip in (0, quarter)
            for block in blocks_of(window(side, skip + row), TILE // 2, TILE // 4)
        ]
        to_tiles(forward, values, half_src, row)


def spread_taps(forward, taps_ref, full_taps, half_taps):
    count, channels = taps_ref.shape
    for row in range(0, count, GROUP):
        value = taps_ref[row : min(row + GROUP, count), :]
        if row + GROUP > count:
            none = jnp.zeros((row + GROUP - count, channels), jnp.float32)
            value = jnp.concatenate([value, none], axis=0)
        value = value.astype(jnp.bfloat16)
        to_tiles(forward, blocks_of(value, 0, TILE // 2) * 2, full_taps, row)
        to_tiles(forward, blocks_of(value, TILE // 2, TILE // 4) * 4, half_taps, row)


def normalise_tiles(back, half, full_dst, half_dst, mixed, normed):
    quarter = half // 2

    def step(i, carry):
        row = i * GROUP
        ends = from_tiles(back, half_dst, row)
        for which in range(2):
            both = from_tiles(back, full_dst, which * quarter + row)
            for side in range(2):
                part = side * 2 + which
                blocks = both[side * TILE // 2 : (side + 1) * TILE // 2]
                blocks = blocks + ends[part * TILE // 4 : (part + 1) * TILE // 4]
                at = pl.ds(pl.multiple_of(part * quarter + row, GROUP), GROUP)
                values = jnp.concatenate(blocks, axis=1)
                mixed[at, :] = values.astype(jnp.bfloat16)
                centred = values - jnp.mean(values, -1, keepdims=True)
                variance = jnp.mean(centred * centred, -1, keepdims=True)
                normed[at, :] = (centred * lax.rsqrt(variance + 1e-05)).astype(jnp.bfloat16)
        return carry

    lax.fori_loop(0, quarter // GROUP, step, 0)


def recording_bounds(where_ref, starts_ref, ends_ref):
    bounds, total = [], jnp.zeros((), jnp.int32)
    for r in range(where_ref.shape[0] - 2):
        starts_ref[r] = total
        total = total + where_ref[2 + r]
        ends_ref[r] = total
        bounds.append(total)
    return bounds


def pool_rows(rows):
    few = rows // STRIDE
    chosen = (
        lax.broadcasted_iota(jnp.int32, (few, rows), 1) // STRIDE
        == lax.broadcasted_iota(jnp.int32, (few, rows), 0)
    )
    return (chosen.astype(jnp.float32) * (1.0 / STRIDE)).astype(jnp.bfloat16)


def project_heads(normed_rows, w_vmem, position, bounds, at, q_ref, kv_ref):
    recs = len(bounds)
    heads = w_vmem.shape[2] // HDE
    lane = lax.broadcasted_iota(jnp.int32, position.shape, 1)
    mine = jnp.zeros(position.shape, jnp.int32)
    for bound in bounds:
        mine += (position >= bound).astype(jnp.int32)
    same = lane - HDE == mine
    extra_q = jnp.where(same | (lane >= HDE + recs), 0.0, HIDDEN)
    extra_k = jnp.where(same, 1.0, 0.0)
    extra_v = jnp.where(lane == HDE, 1.0, 0.0)
    score_scale = HDE ** (-0.5) * math.log2(math.e)
    for kind, extra in enumerate((extra_q, extra_k, extra_v)):
        result = jnp.dot(normed_rows, w_vmem[kind], preferred_element_type=jnp.float32)
        if kind == 0:
            result = result * score_scale
        for h in range(heads):
            tile, start = divmod(h * HDE, LANES)
            tiles = 1 if start + HDE <= LANES else 2
            head = result[:, tile * LANES : (tile + tiles) * LANES]
            if start:
                head = pltpu.roll(head, tiles * LANES - start, 1)
            head = jnp.where(lane < HDE, head[:, :LANES], extra).astype(jnp.bfloat16)
            if kind == 0:
                q_ref[at, h * LANES : (h + 1) * LANES] = head
            else:
                first = ((kind - 1) * heads + h) * LANES
                kv_ref[at, first : first + LANES] = head


def interior_kernel(
    where_ref,
    taps_hbm,
    audio_ref,
    w_ref,
    q_ref,
    kv_ref,
    pooled_ref,
    audio,
    full_src,
    full_dst,
    half_src,
    half_dst,
    taps_ref,
    full_taps,
    half_taps,
    mixed,
    normed,
    w_vmem,
    starts_ref,
    ends_ref,
    audio_sem,
    taps_sem,
    w_sem,
):
    rows = q_ref.shape[0]
    inner = rows + 2 * HALO
    skip = EDGE - HALO
    half = rows // 2
    load_audio = pltpu.make_async_copy(audio_ref.at[skip : skip + inner], audio, audio_sem)
    load_taps = pltpu.make_async_copy(taps_hbm, taps_ref, taps_sem)
    load_audio.start()
    load_taps.start()
    load_w = pltpu.make_async_copy(w_ref, w_vmem, w_sem)
    load_w.start()
    bounds = recording_bounds(where_ref, starts_ref, ends_ref)
    start = where_ref[0] + EDGE
    forward, back = shuffle(False), shuffle(True)
    load_audio.wait()

    def window(side, row):
        return audio[side * half + row : side * half + row + GROUP, :]

    fill_tiles(forward, window, half, full_src, half_src)
    load_taps.wait()
    spread_taps(forward, taps_ref, full_taps, half_taps)
    sides = [start, start + half]
    parts = [start + i * half // 2 for i in range(4)]
    taps = taps_hbm.shape[0]
    common = (bounds, starts_ref, ends_ref)
    conv_blocks(full_src, full_dst, full_taps, taps, half // BLOCK, sides, *common)
    conv_blocks(half_src, half_dst, half_taps, taps, half // 2 // BLOCK, parts, *common)
    normalise_tiles(back, half, full_dst, half_dst, mixed, normed)

    width = pooled_ref.shape[1]
    own_columns = pl.ds(pl.multiple_of(where_ref[1] * width, LANES), width)
    pooled_ref[...] = jnp.dot(
        pool_rows(rows), mixed[:, own_columns], preferred_element_type=jnp.float32
    )
    load_w.wait()
    for which in range(2):
        at = slice(which * half, (which + 1) * half)
        position = start + which * half + lax.broadcasted_iota(jnp.int32, (half, LANES), 0)
        project_heads(normed[at, :], w_vmem, position, bounds, at, q_ref, kv_ref)


def edge_kernel(
    where_ref,
    taps_hbm,
    audio_ref,
    halo_ref,
    w_ref,
    q_ref,
    kv_ref,
    pooled_ref,
    audio,
    full_src,
    full_dst,
    half_src,
    half_dst,
    taps_ref,
    full_taps,
    half_taps,
    mixed,
    normed,
    w_vmem,
    starts_ref,
    ends_ref,
    first_sem,
    last_sem,
    taps_sem,
    w_sem,
):
    frames = audio_ref.shape[0]
    known = EDGE + HALO
    loads = [
        pltpu.make_async_copy(audio_ref.at[:known], audio.at[:known], first_sem),
        pltpu.make_async_copy(audio_ref.at[frames - known :], audio.at[known:], last_sem),
        pltpu.make_async_copy(taps_hbm, taps_ref, taps_sem),
        pltpu.make_async_copy(w_ref, w_vmem, w_sem),
    ]
    for load in loads:
        load.start()
    bounds = recording_bounds(where_ref, starts_ref, ends_ref)
    forward, back = shuffle(False), shuffle(True)
    starts = [where_ref[0], where_ref[0] + frames - EDGE]
    has_before = (starts[0] > 0).astype(jnp.float32)
    has_after = (starts[0] + frames < bounds[-1]).astype(jnp.float32)
    before = (halo_ref[HALO:, :].astype(jnp.float32) * has_before).astype(jnp.bfloat16)
    after = (halo_ref[:HALO, :].astype(jnp.float32) * has_after).astype(jnp.bfloat16)
    for load in loads[:3]:
        load.wait()

    def window(side, row):
        if side == 0:
            return before if row == 0 else audio[row - HALO : row - HALO + GROUP, :]
        return after if row == known else audio[known + row : known + row + GROUP, :]

    fill_tiles(forward, window, EDGE, full_src, half_src)
    spread_taps(forward, taps_ref, full_taps, half_taps)
    parts = [first + skip for first in starts for skip in (0, EDGE // 2)]
    taps = taps_hbm.shape[0]
    common = (bounds, starts_ref, ends_ref)
    conv_blocks(full_src, full_dst, full_taps, taps, EDGE // BLOCK, starts, *common)
    conv_blocks(half_src, half_dst, half_taps, taps, EDGE // 2 // BLOCK, parts, *common)
    normalise_tiles(back, EDGE, full_dst, half_dst, mixed, normed)
    width = pooled_ref.shape[1]
    own_columns = pl.ds(pl.multiple_of(where_ref[1] * width, LANES), width)
    pooled_ref[...] = jnp.dot(
        pool_rows(2 * EDGE), mixed[:, own_columns], preferred_element_type=jnp.float32
    )
    loads[3].wait()
    row = lax.broadcasted_iota(jnp.int32, (2 * EDGE, LANES), 0)
    position = jnp.where(row < EDGE, starts[0] + row, starts[1] - EDGE + row)
    project_heads(normed[...], w_vmem, position, bounds, slice(None), q_ref, kv_ref)


def attend_kernel(count, rows, targets_ref, mid_q, edge_q, mid_mixed, edge_mixed, w_ref, *refs):
    kv_refs, out_refs = refs[: 2 * count], refs[2 * count : -6]
    queries, kv, mixed, pooled, w_vmem, w_sem = refs[-6:]
    frames = queries.shape[0]
    heads = queries.shape[1] // LANES
    width = mixed.shape[1]
    loads = [
        pltpu.make_async_copy(
            w_ref.at[h * HDE : (h + 1) * HDE], w_vmem.at[h * LANES : h * LANES + HDE], w_sem.at[h]
        )
        for h in range(heads)
    ]
    for load in loads:
        load.start()
    for h in range(heads):
        w_vmem[h * LANES + HDE : (h + 1) * LANES, :] = jnp.zeros(
            (LANES - HDE, w_vmem.shape[1]), jnp.bfloat16
        )
    for out, mid, edge, cut in (
        (queries, mid_q, edge_q, EDGE),
        (mixed, mid_mixed, edge_mixed, EDGE // STRIDE),
    ):
        out[:cut, :] = edge[:cut, :]
        out[cut : out.shape[0] - cut, :] = mid[...]
        out[out.shape[0] - cut :, :] = edge[cut:, :]
    at = 0
    for ref in kv_refs:
        kv[at : at + ref.shape[0], :] = ref[...]
        at += ref.shape[0]
    few = rows // STRIDE
    pool = pool_rows(rows)

    def step(i, carry):
        at = pl.ds(pl.multiple_of(i * rows, rows), rows)
        for h in range(heads):
            lanes = slice(h * LANES, (h + 1) * LANES)
            scores = lax.dot_general(
                queries[at, lanes],
                kv[:, lanes],
                (((1,), (1,)), ((), ())),
                preferred_element_type=jnp.float32,
            )
            peak = jnp.max(scores, axis=1, keepdims=True)
            weights = jnp.exp2(scores - peak).astype(jnp.bfloat16)
            values = kv[:, (heads + h) * LANES : (heads + h + 1) * LANES]
            out = jnp.dot(weights, values, preferred_element_type=jnp.float32)
            attended = (out * (1.0 / out[:, HDE : HDE + 1])).astype(jnp.bfloat16)
            pooled[pl.ds(pl.multiple_of(i * few, few), few), lanes] = jnp.dot(
                pool, attended, preferred_element_type=jnp.float32
            ).astype(jnp.bfloat16)
        return carry

    lax.fori_loop(0, frames // rows, step, 0)
    for load in loads:
        load.wait()
    for k, out_ref in enumerate(out_refs):
        columns = pl.ds(pl.multiple_of(targets_ref[k] * width, LANES), width)
        total = jnp.dot(pooled[...], w_vmem[:, columns], preferred_element_type=jnp.float32)
        if k == 0:
            total += mixed[...]
        out_ref[...] = total.astype(out_ref.dtype)


def project_kernel(targets_ref, *refs):
    *part_refs, w_ref, out_ref, squares_ref, pooled = refs
    width = part_refs[0].shape[1]
    for k, part_ref in enumerate(part_refs):
        at = pl.ds(pl.multiple_of(targets_ref[k] * width, LANES), width)
        pooled[:, at] = part_ref[...]
    total = jnp.dot(pooled[...], w_ref[...], preferred_element_type=jnp.float32)
    out_ref[...] = total
    rows = total.shape[0]
    squares = jnp.sum(total * total, axis=1, keepdims=True)
    squares_ref[...] = jnp.transpose(jnp.broadcast_to(squares, (rows, rows)))[:SUBLANES]


def route_kernel(cap, firsts_ref, place_ref, rows_ref, *refs):
    square_refs, out_refs = refs[: -firsts_ref.shape[0]], refs[-firsts_ref.shape[0] :]
    rows = rows_ref.shape[0]
    devices = sum(ref.shape[0] for ref in out_refs) // cap
    squares = square_refs[0][...]
    for ref in square_refs[1:]:
        squares += ref[...]
    scale = lax.rsqrt(squares[:1] / D + 1e-05)
    scale = jnp.transpose(jnp.broadcast_to(scale, (rows, rows)))[:, :1]
    normal_rows = (rows_ref[...] * scale).astype(jnp.bfloat16)
    destination = place_ref[...]
    named = lax.broadcasted_iota(jnp.int32, (devices, rows), 0) == destination
    earlier = lax.broadcasted_iota(jnp.int32, (rows, rows), 0) < lax.broadcasted_iota(
        jnp.int32, (rows, rows), 1
    )
    counts = jnp.dot(
        named.astype(jnp.float32).astype(jnp.bfloat16),
        earlier.astype(jnp.float32).astype(jnp.bfloat16),
        preferred_element_type=jnp.float32,
    )
    rank = jnp.sum(jnp.where(named, counts, 0.0), axis=0, keepdims=True).astype(jnp.int32)
    target = destination * cap + rank
    for k, out_ref in enumerate(out_refs):
        slots = out_ref.shape[0]
        slot = firsts_ref[k] + lax.broadcasted_iota(jnp.int32, (slots, rows), 0)
        one_hot = (slot == target).astype(jnp.float32).astype(jnp.bfloat16)
        out_ref[...] = jnp.dot(
            one_hot, normal_rows, preferred_element_type=jnp.float32
        ).astype(jnp.bfloat16)


def collect_kernel(firsts_ref, *refs):
    *block_refs, out_ref = refs
    for k, block_ref in enumerate(block_refs):
        slots = block_ref.shape[0]
        at = pl.ds(pl.multiple_of(firsts_ref[k], slots), slots)
        out_ref[at, :] = block_ref[...]


def partner(index, k, devices):
    if devices & (devices - 1) == 0:
        return index ^ k
    return (index + k) % devices


def sender(index, k, devices):
    if devices & (devices - 1) == 0:
        return index ^ k
    return (index - k) % devices


def exchange(value, axes, k, devices):
    return lax.ppermute(value, axes, [(i, partner(i, k, devices)) for i in range(devices)])


def local(audio, lengths, conv_kernel, w_qkv, w_out, place, w_adapt):
    frame_count, channels = audio.shape
    seq_devices = lax.axis_size("tm")
    mp_devices = lax.axis_size("mp")
    recs = lengths.shape[1]
    group_frames = frame_count * seq_devices
    width = channels // mp_devices
    pooled_rows = frame_count // STRIDE
    heads = w_qkv.shape[2] // HDE
    where = jnp.concatenate(
        [jnp.stack([lax.axis_index("tm") * frame_count, lax.axis_index("mp")]), lengths[0]]
    )

    if seq_devices == 2:
        ends = jnp.concatenate([audio[:HALO], audio[frame_count - HALO :]], axis=0)
        halo = exchange(ends, "tm", 1, 2)
    else:
        up = [(i, i + 1) for i in range(seq_devices - 1)]
        down = [(j, i) for i, j in up]
        after = lax.ppermute(audio[:HALO], "tm", down)
        before = lax.ppermute(audio[frame_count - HALO :], "tm", up)
        halo = jnp.concatenate([after, before], axis=0)

    smem = pl.BlockSpec(memory_space=pltpu.SMEM)
    vmem = pl.BlockSpec(memory_space=pltpu.VMEM)
    hbm = pl.BlockSpec(memory_space=pltpu.HBM)
    w_three = jnp.transpose(w_qkv, (1, 0, 2))
    taps = conv_kernel.shape[0]

    def tiles(count):
        return pltpu.VMEM((count * TILE, LANES), jnp.bfloat16)

    def results(rows):
        return [
            jax.ShapeDtypeStruct((rows, heads * LANES), jnp.bfloat16),
            jax.ShapeDtypeStruct((rows, 2 * heads * LANES), jnp.bfloat16),
            jax.ShapeDtypeStruct((rows // STRIDE, width), jnp.float32),
        ]

    def shared(rows):
        return [
            pltpu.VMEM(conv_kernel.shape, jnp.float32),
            tiles(taps + 1),
            tiles(taps + 1),
            pltpu.VMEM((rows, channels), jnp.bfloat16),
            pltpu.VMEM((rows, channels), jnp.bfloat16),
            pltpu.VMEM(w_three.shape, jnp.bfloat16),
            pltpu.SMEM((recs,), jnp.int32),
            pltpu.SMEM((recs,), jnp.int32),
        ]

    mid = frame_count - 2 * EDGE
    mid_q, mid_kv, mid_mixed = pl.pallas_call(
        interior_kernel,
        out_shape=results(mid),
        in_specs=[smem, hbm, hbm, hbm],
        out_specs=[vmem] * 3,
        scratch_shapes=[
            pltpu.VMEM((mid + 2 * HALO, channels), jnp.bfloat16),
            tiles(mid // 2 + 2 * HALO),
            tiles(mid // 2),
            tiles(mid // 4 + 2 * HALO),
            tiles(mid // 4),
            *shared(mid),
            *[pltpu.SemaphoreType.DMA] * 3,
        ],
        compiler_params=pltpu.CompilerParams(vmem_limit_bytes=53 * MIB),
        cost_estimate=pl.CostEstimate(
            flops=6 * mid * channels * w_qkv.shape[2], bytes_accessed=40 * MIB, transcendentals=0
        ),
        name="interior",
    )(where, conv_kernel, audio, w_three)
    edge_q, edge_kv, edge_mixed = pl.pallas_call(
        edge_kernel,
        out_shape=results(2 * EDGE),
        in_specs=[smem, hbm, hbm, vmem, hbm],
        out_specs=[vmem] * 3,
        scratch_shapes=[
            pltpu.VMEM((2 * (EDGE + HALO), channels), jnp.bfloat16),
            tiles(EDGE + 2 * HALO),
            tiles(EDGE),
            tiles(EDGE // 2 + 2 * HALO),
            tiles(EDGE // 2),
            *shared(2 * EDGE),
            *[pltpu.SemaphoreType.DMA] * 4,
        ],
        compiler_params=pltpu.CompilerParams(vmem_limit_bytes=53 * MIB),
        cost_estimate=pl.CostEstimate(
            flops=12 * EDGE * channels * w_qkv.shape[2], bytes_accessed=8 * MIB, transcendentals=0
        ),
        name="edges",
    )(
        where,
        conv_kernel,
        audio,
        halo,
        w_three,
    )

    kv_blocks = [mid_kv, edge_kv]
    for k in range(1, seq_devices):
        kv_blocks += [exchange(block, "tm", k, seq_devices) for block in (mid_kv, edge_kv)]
    mp_index = lax.axis_index("mp")
    mp_targets = jnp.stack([partner(mp_index, k, mp_devices) for k in range(mp_devices)])
    mp_senders = jnp.stack([sender(mp_index, k, mp_devices) for k in range(mp_devices)])
    part = (pooled_rows, width)
    own_part, *parts = pl.pallas_call(
        functools.partial(attend_kernel, seq_devices, 256 if seq_devices <= 2 else 64),
        out_shape=[jax.ShapeDtypeStruct(part, jnp.float32)]
        + [jax.ShapeDtypeStruct(part, jnp.bfloat16)] * (mp_devices - 1),
        in_specs=[smem] + [vmem] * 4 + [hbm] + [vmem] * len(kv_blocks),
        out_specs=[vmem] * mp_devices,
        scratch_shapes=[
            pltpu.VMEM((frame_count, heads * LANES), jnp.bfloat16),
            pltpu.VMEM((group_frames, 2 * heads * LANES), jnp.bfloat16),
            pltpu.VMEM(part, jnp.float32),
            pltpu.VMEM((pooled_rows, heads * LANES), jnp.bfloat16),
            pltpu.VMEM((heads * LANES, channels), jnp.bfloat16),
            pltpu.SemaphoreType.DMA((heads,)),
        ],
        compiler_params=pltpu.CompilerParams(
            vmem_limit_bytes=44 * MIB
        ),
        name="attend",
    )(mp_targets, mid_q, edge_q, mid_mixed, edge_mixed, w_out, *kv_blocks)
    others = range(1, mp_devices)
    for k in others:
        own_part += exchange(parts[k - 1], "mp", k, mp_devices).astype(jnp.float32)
    own_part = own_part.astype(jnp.bfloat16)
    pooled = [own_part] + [exchange(own_part, "mp", k, mp_devices) for k in others]

    columns = w_adapt.shape[1]
    projected, squares = pl.pallas_call(
        project_kernel,
        out_shape=[
            jax.ShapeDtypeStruct((pooled_rows, columns), jnp.float32),
            jax.ShapeDtypeStruct((SUBLANES, pooled_rows), jnp.float32),
        ],
        in_specs=[smem] + [vmem] * (mp_devices + 1),
        out_specs=[vmem] * 2,
        scratch_shapes=[pltpu.VMEM((pooled_rows, channels), jnp.bfloat16)],
        compiler_params=pltpu.CompilerParams(vmem_limit_bytes=16 * MIB),
        name="project",
    )(mp_senders, *pooled, w_adapt)
    squares = [squares] + [exchange(squares, "mp", k, mp_devices) for k in others]

    axes = ("section", "tm")
    device_count = lax.axis_size("section") * seq_devices
    me = lax.axis_index(axes)
    cap = max(2, (2 * pooled_rows + device_count - 1) // device_count)
    direct = device_count <= 8
    if direct:
        firsts = jnp.stack([partner(me, k, device_count) * cap for k in range(device_count)])
        blocks = [jax.ShapeDtypeStruct((cap, columns), jnp.bfloat16)] * device_count
    else:
        firsts = jnp.zeros((1,), jnp.int32)
        blocks = [jax.ShapeDtypeStruct((device_count * cap, columns), jnp.bfloat16)]
    blocks = pl.pallas_call(
        functools.partial(route_kernel, cap),
        out_shape=blocks,
        in_specs=[smem] + [vmem] * (mp_devices + 2),
        out_specs=[vmem] * len(blocks),
        compiler_params=pltpu.CompilerParams(vmem_limit_bytes=16 * MIB),
        name="route",
    )(firsts, place.T, projected, *squares)
    if not direct:
        return lax.all_to_all(blocks[0], axes, split_axis=0, concat_axis=0, tiled=True)
    arrived = [blocks[0]] + [
        exchange(blocks[k], axes, k, device_count) for k in range(1, device_count)
    ]
    firsts = jnp.stack([sender(me, k, device_count) * cap for k in range(device_count)])
    return pl.pallas_call(
        collect_kernel,
        out_shape=jax.ShapeDtypeStruct((device_count * cap, columns), jnp.bfloat16),
        in_specs=[smem] + [vmem] * device_count,
        out_specs=vmem,
        compiler_params=pltpu.CompilerParams(vmem_limit_bytes=8 * MIB),
        name="collect",
    )(firsts, *arrived)


def solution(mesh):
    placed = (
        P(("section", "tm"), None),
        P("section", None),
        P(),
        P(None, None, "mp"),
        P("mp", None),
        P(("section", "tm"), None),
        P(None, "mp"),
    )
    return jax.shard_map(
        local, mesh=mesh, in_specs=placed, out_specs=P(("section", "tm"), "mp"), check_vma=False
    )
```

```python
import functools
import math

import jax
import jax.numpy as jnp
from jax import lax
from jax.experimental import pallas as pl
from jax.experimental.pallas import tpu as pltpu
from jax.sharding import PartitionSpec as P

HDE = 96
D = 5120
STRIDE = 4
LANES = 128
SUBLANES = 8
HALO = 16
EDGE = 32
BLOCK = 16
GROUP = 16
MIB = 1 << 20
HIDDEN = -1e30


def conv_blocks(src, dst, taps, blocks, run, firsts, recs, bounds, starts_ref, ends_ref):
    count = taps.shape[0] // SUBLANES
    reach = count // 2
    span = BLOCK + count - 1
    shape = (SUBLANES, LANES)
    upper = lax.broadcasted_iota(jnp.int32, shape, 0) < SUBLANES // 2

    def both(values):
        if len(values) == 1:
            return jnp.full(shape, values[0], jnp.int32)
        return jnp.where(upper, values[0], values[1])

    def convolve(base, inside):
        def frame(k):
            at = (base + k + HALO - reach) * SUBLANES
            return src[pl.ds(pl.multiple_of(at, SUBLANES), SUBLANES), :]

        kernel = [taps[j * SUBLANES : (j + 1) * SUBLANES, :] for j in range(count)]
        totals = [None] * BLOCK
        for k in range(span):
            value = frame(k)
            if inside is not None:
                value = jnp.where(inside(k), value, 0.0)
            for t in range(max(0, k - count + 1), min(BLOCK, k + 1)):
                term = kernel[k - t] * value
                totals[t] = term if totals[t] is None else totals[t] + term
        for t in range(BLOCK):
            at = pl.ds(pl.multiple_of((base + t) * SUBLANES, SUBLANES), SUBLANES)
            half = 0.5 * totals[t]
            value = frame(t + reach) + half * (1.0 + jnp.tanh(half))
            if inside is not None:
                value = jnp.where(inside(t + reach), value, dst[at, :])
            dst[at, :] = value

    def touched(base, length):
        found = jnp.zeros((), jnp.bool_)
        for first in firsts:
            for bound in bounds[:-1]:
                at = bound - first - base
                found = found | ((at > -reach) & (at < length + reach))
        return found

    def masked(base):
        positions = [first + base for first in firsts]
        begin, extra = [], jnp.zeros((), jnp.int32)
        for position in positions:
            first = last = jnp.zeros((), jnp.int32)
            for bound in bounds[:-1]:
                first += (bound <= position).astype(jnp.int32)
                last += (bound <= position + BLOCK - 1).astype(jnp.int32)
            begin.append(first)
            extra = jnp.maximum(extra, last - first)

        def once(turn, carry):
            which = [jnp.minimum(first + turn, recs - 1) for first in begin]
            low = both([starts_ref[r] - p for r, p in zip(which, positions)])
            high = both([ends_ref[r] - p for r, p in zip(which, positions)])
            convolve(base, lambda k: (low <= k - reach) & (high > k - reach))
            return carry

        lax.fori_loop(0, extra + 1, once, 0)

    def blocks_of_run(i, carry):
        base = i * run * BLOCK
        any_touched = touched(base, run * BLOCK)

        @pl.when(jnp.logical_not(any_touched))
        def _():
            for j in range(run):
                convolve(base + j * BLOCK, None)

        @pl.when(any_touched)
        def _():
            def one(j, carry):
                here = base + j * BLOCK
                mine = touched(here, BLOCK)

                @pl.when(mine)
                def _():
                    masked(here)

                @pl.when(jnp.logical_not(mine))
                def _():
                    convolve(here, None)

                return carry

            lax.fori_loop(0, run, one, 0)

        return carry

    lax.fori_loop(0, blocks // run, blocks_of_run, 0)


def shuffle(back):
    row = lax.broadcasted_iota(jnp.int32, (LANES, LANES), 1 if back else 0)
    column = lax.broadcasted_iota(jnp.int32, (LANES, LANES), 0 if back else 1)
    moved = (row // SUBLANES == column % GROUP) & (row % SUBLANES == column // GROUP)
    return moved.astype(jnp.float32).astype(jnp.bfloat16)


def to_tiles(matrix, values, ref, frame):
    stack = jnp.concatenate(values, axis=0)
    at = pl.ds(frame * SUBLANES, GROUP * SUBLANES)
    ref[at, :] = jnp.dot(matrix, stack, preferred_element_type=jnp.float32)


def from_tiles(matrix, ref, frame):
    rows = GROUP * SUBLANES
    low = ref[frame * SUBLANES : frame * SUBLANES + rows, :].astype(jnp.bfloat16)
    moved = jnp.dot(matrix, low, preferred_element_type=jnp.float32)
    return [moved[k * GROUP : (k + 1) * GROUP] for k in range(SUBLANES)]


def blocks_of(value, first, count):
    return [value[:, k * LANES : (k + 1) * LANES] for k in range(first, first + count)]


def recording_bounds(where_ref, starts_ref, ends_ref):
    bounds, total = [], jnp.zeros((), jnp.int32)
    for r in range(where_ref.shape[0] - 2):
        starts_ref[r] = total
        total = total + where_ref[2 + r]
        ends_ref[r] = total
        bounds.append(total)
    return bounds


def spread_taps(taps_ref, full_taps, half_taps):
    count = taps_ref.shape[0]
    blocks = taps_ref.shape[1] // LANES
    for k in range(blocks):
        value = taps_ref[:, k * LANES : (k + 1) * LANES]
        if k < SUBLANES:
            full_taps[pl.ds(k, count, stride=SUBLANES), :] = value
        else:
            for half in range(2):
                at = k - SUBLANES + half * SUBLANES // 2
                half_taps[pl.ds(at, count, stride=SUBLANES), :] = value


def normalise(blocks, mixed, normed, at):
    values = jnp.concatenate(blocks, axis=1)
    mixed[at, :] = values.astype(jnp.bfloat16)
    centred = values - jnp.mean(values, -1, keepdims=True)
    variance = jnp.mean(centred * centred, -1, keepdims=True)
    normed[at, :] = (centred * lax.rsqrt(variance + 1e-05)).astype(jnp.bfloat16)


def pool_rows(rows):
    few = rows // STRIDE
    chosen = (
        lax.broadcasted_iota(jnp.int32, (few, rows), 1) // STRIDE
        == lax.broadcasted_iota(jnp.int32, (few, rows), 0)
    )
    return (chosen.astype(jnp.float32) * (1.0 / STRIDE)).astype(jnp.bfloat16)


def project_heads(normed_rows, w_vmem, position, bounds, at, q_ref, kv_ref):
    recs = len(bounds)
    heads = w_vmem.shape[2] // HDE
    lane = lax.broadcasted_iota(jnp.int32, position.shape, 1)
    mine = jnp.zeros(position.shape, jnp.int32)
    for bound in bounds:
        mine += (position >= bound).astype(jnp.int32)
    same = lane - HDE == mine
    extra_q = jnp.where(same | (lane >= HDE + recs), 0.0, HIDDEN)
    extra_k = jnp.where(same, 1.0, 0.0)
    extra_v = jnp.where(lane == HDE, 1.0, 0.0)
    score_scale = HDE ** (-0.5) * math.log2(math.e)
    for kind, extra in enumerate((extra_q, extra_k, extra_v)):
        result = jnp.dot(normed_rows, w_vmem[kind], preferred_element_type=jnp.float32)
        if kind == 0:
            result = result * score_scale
        for h in range(heads):
            tile, start = divmod(h * HDE, LANES)
            tiles = 1 if start + HDE <= LANES else 2
            head = result[:, tile * LANES : (tile + tiles) * LANES]
            if start:
                head = pltpu.roll(head, tiles * LANES - start, 1)
            head = jnp.where(lane < HDE, head[:, :LANES], extra).astype(jnp.bfloat16)
            if kind == 0:
                q_ref[at, h * LANES : (h + 1) * LANES] = head
            else:
                first = ((kind - 1) * heads + h) * LANES
                kv_ref[at, first : first + LANES] = head


def interior_kernel(
    where_ref,
    taps_hbm,
    audio_ref,
    w_ref,
    q_ref,
    kv_ref,
    pooled_ref,
    audio,
    full_src,
    full_dst,
    half_src,
    half_dst,
    taps_ref,
    full_taps,
    half_taps,
    mixed,
    normed,
    w_vmem,
    starts_ref,
    ends_ref,
    audio_sem,
    taps_sem,
    w_sem,
):
    rows = q_ref.shape[0]
    inner = rows + 2 * HALO
    skip = EDGE - HALO
    half = rows // 2
    load_audio = pltpu.make_async_copy(audio_ref.at[skip : skip + inner], audio, audio_sem)
    load_taps = pltpu.make_async_copy(taps_hbm, taps_ref, taps_sem)
    load_audio.start()
    load_taps.start()
    load_w = pltpu.make_async_copy(w_ref, w_vmem, w_sem)
    load_w.start()
    bounds = recording_bounds(where_ref, starts_ref, ends_ref)
    start = where_ref[0] + EDGE
    forward, back = shuffle(False), shuffle(True)
    load_audio.wait()
    side = SUBLANES // 2
    for row in range(0, inner, GROUP):
        value = audio[row : row + GROUP, : SUBLANES * LANES]
        to_tiles(forward, blocks_of(value, 0, SUBLANES), full_src, row)
    for row in range(0, half + 2 * HALO, GROUP):
        pair = [
            block
            for at in (row, row + half)
            for block in blocks_of(audio[at : at + GROUP, :], SUBLANES, side)
        ]
        to_tiles(forward, pair, half_src, row)
    load_taps.wait()
    spread_taps(taps_ref, full_taps, half_taps)
    recs = len(bounds)
    common = (recs, bounds, starts_ref, ends_ref)
    conv_blocks(full_src, full_dst, full_taps, rows // BLOCK, 4, [start], *common)
    conv_blocks(half_src, half_dst, half_taps, half // BLOCK, 2, [start, start + half], *common)


    for row in range(0, half, GROUP):
        pair = from_tiles(back, half_dst, row)
        for which in range(2):
            at = which * half + row
            blocks = from_tiles(back, full_dst, at) + pair[which * side : (which + 1) * side]
            normalise(blocks, mixed, normed, slice(at, at + GROUP))

    width = pooled_ref.shape[1]
    own_columns = pl.ds(pl.multiple_of(where_ref[1] * width, LANES), width)
    pooled_ref[...] = jnp.dot(
        pool_rows(rows), mixed[:, own_columns], preferred_element_type=jnp.float32
    )
    load_w.wait()
    for which in range(2):
        at = slice(which * half, (which + 1) * half)
        position = start + which * half + lax.broadcasted_iota(jnp.int32, (half, LANES), 0)
        project_heads(normed[at, :], w_vmem, position, bounds, at, q_ref, kv_ref)


def edge_kernel(
    where_ref,
    taps_hbm,
    audio_ref,
    halo_ref,
    w_ref,
    q_ref,
    kv_ref,
    pooled_ref,
    audio,
    full_src,
    full_dst,
    half_src,
    half_dst,
    taps_ref,
    full_taps,
    half_taps,
    mixed,
    normed,
    w_vmem,
    starts_ref,
    ends_ref,
    first_sem,
    last_sem,
    taps_sem,
    w_sem,
):
    frames = audio_ref.shape[0]
    known = EDGE + HALO
    loads = [
        pltpu.make_async_copy(audio_ref.at[:known], audio.at[:known], first_sem),
        pltpu.make_async_copy(audio_ref.at[frames - known :], audio.at[known:], last_sem),
        pltpu.make_async_copy(taps_hbm, taps_ref, taps_sem),
        pltpu.make_async_copy(w_ref, w_vmem, w_sem),
    ]
    for load in loads:
        load.start()
    bounds = recording_bounds(where_ref, starts_ref, ends_ref)
    forward, back = shuffle(False), shuffle(True)
    starts = [where_ref[0], where_ref[0] + frames - EDGE]
    length = EDGE + 2 * HALO
    has_before = (starts[0] > 0).astype(jnp.float32)
    has_after = (starts[0] + frames < bounds[-1]).astype(jnp.float32)
    before = (halo_ref[HALO:, :].astype(jnp.float32) * has_before).astype(jnp.bfloat16)
    after = (halo_ref[:HALO, :].astype(jnp.float32) * has_after).astype(jnp.bfloat16)
    for load in loads[:3]:
        load.wait()
    side = SUBLANES // 2
    for row in range(0, length, GROUP):
        first = before if row == 0 else audio[row - HALO : row - HALO + GROUP, :]
        last = after if row == known else audio[known + row : known + row + GROUP, :]
        for which, value in enumerate((first, last)):
            to_tiles(forward, blocks_of(value, 0, SUBLANES), full_src.at[which], row)
        pair = blocks_of(first, SUBLANES, side) + blocks_of(last, SUBLANES, side)
        to_tiles(forward, pair, half_src, row)
    spread_taps(taps_ref, full_taps, half_taps)
    recs = len(bounds)
    common = (recs, bounds, starts_ref, ends_ref)
    for which in range(2):
        conv_blocks(
            full_src.at[which],
            full_dst.at[which],
            full_taps,
            EDGE // BLOCK,
            2,
            [starts[which]],
            *common,
        )
    conv_blocks(half_src, half_dst, half_taps, EDGE // BLOCK, 2, starts, *common)
    for row in range(0, EDGE, GROUP):
        pair = from_tiles(back, half_dst, row)
        for which in range(2):
            blocks = from_tiles(back, full_dst.at[which], row)
            blocks += pair[which * side : (which + 1) * side]
            at = which * EDGE + row
            normalise(blocks, mixed, normed, slice(at, at + GROUP))
    width = pooled_ref.shape[1]
    own_columns = pl.ds(pl.multiple_of(where_ref[1] * width, LANES), width)
    pooled_ref[...] = jnp.dot(
        pool_rows(2 * EDGE), mixed[:, own_columns], preferred_element_type=jnp.float32
    )
    loads[3].wait()
    row = lax.broadcasted_iota(jnp.int32, (2 * EDGE, LANES), 0)
    position = jnp.where(row < EDGE, starts[0] + row, starts[1] - EDGE + row)
    project_heads(normed[...], w_vmem, position, bounds, slice(None), q_ref, kv_ref)


def attend_kernel(count, rows, targets_ref, mid_q, edge_q, mid_mixed, edge_mixed, w_ref, *refs):
    kv_refs, out_refs = refs[: 2 * count], refs[2 * count : -6]
    queries, kv, mixed, pooled, w_vmem, w_sem = refs[-6:]
    frames = queries.shape[0]
    heads = queries.shape[1] // LANES
    width = mixed.shape[1]
    loads = [
        pltpu.make_async_copy(
            w_ref.at[h * HDE : (h + 1) * HDE], w_vmem.at[h * LANES : h * LANES + HDE], w_sem.at[h]
        )
        for h in range(heads)
    ]
    for load in loads:
        load.start()
    for h in range(heads):
        w_vmem[h * LANES + HDE : (h + 1) * LANES, :] = jnp.zeros(
            (LANES - HDE, w_vmem.shape[1]), jnp.bfloat16
        )
    for out, mid, edge, cut in (
        (queries, mid_q, edge_q, EDGE),
        (mixed, mid_mixed, edge_mixed, EDGE // STRIDE),
    ):
        out[:cut, :] = edge[:cut, :]
        out[cut : out.shape[0] - cut, :] = mid[...]
        out[out.shape[0] - cut :, :] = edge[cut:, :]
    at = 0
    for ref in kv_refs:
        kv[at : at + ref.shape[0], :] = ref[...]
        at += ref.shape[0]
    few = rows // STRIDE
    pool = pool_rows(rows)

    def step(i, carry):
        at = pl.ds(pl.multiple_of(i * rows, rows), rows)
        for h in range(heads):
            lanes = slice(h * LANES, (h + 1) * LANES)
            scores = lax.dot_general(
                queries[at, lanes],
                kv[:, lanes],
                (((1,), (1,)), ((), ())),
                preferred_element_type=jnp.float32,
            )
            peak = jnp.max(scores, axis=1, keepdims=True)
            weights = jnp.exp2(scores - peak).astype(jnp.bfloat16)
            values = kv[:, (heads + h) * LANES : (heads + h + 1) * LANES]
            out = jnp.dot(weights, values, preferred_element_type=jnp.float32)
            attended = (out * (1.0 / out[:, HDE : HDE + 1])).astype(jnp.bfloat16)
            pooled[pl.ds(pl.multiple_of(i * few, few), few), lanes] = jnp.dot(
                pool, attended, preferred_element_type=jnp.float32
            ).astype(jnp.bfloat16)
        return carry

    lax.fori_loop(0, frames // rows, step, 0)
    for load in loads:
        load.wait()
    for k, out_ref in enumerate(out_refs):
        columns = pl.ds(pl.multiple_of(targets_ref[k] * width, LANES), width)
        total = jnp.dot(pooled[...], w_vmem[:, columns], preferred_element_type=jnp.float32)
        if k == 0:
            total += mixed[...]
        out_ref[...] = total.astype(out_ref.dtype)


def project_kernel(targets_ref, *refs):
    *part_refs, w_ref, out_ref, squares_ref, pooled = refs
    width = part_refs[0].shape[1]
    for k, part_ref in enumerate(part_refs):
        at = pl.ds(pl.multiple_of(targets_ref[k] * width, LANES), width)
        pooled[:, at] = part_ref[...]
    total = jnp.dot(pooled[...], w_ref[...], preferred_element_type=jnp.float32)
    out_ref[...] = total
    rows = total.shape[0]
    squares = jnp.sum(total * total, axis=1, keepdims=True)
    squares_ref[...] = jnp.transpose(jnp.broadcast_to(squares, (rows, rows)))[:SUBLANES]


def route_kernel(cap, firsts_ref, place_ref, rows_ref, *refs):
    square_refs, out_refs = refs[: -firsts_ref.shape[0]], refs[-firsts_ref.shape[0] :]
    rows = rows_ref.shape[0]
    devices = sum(ref.shape[0] for ref in out_refs) // cap
    squares = square_refs[0][...]
    for ref in square_refs[1:]:
        squares += ref[...]
    scale = lax.rsqrt(squares[:1] / D + 1e-05)
    scale = jnp.transpose(jnp.broadcast_to(scale, (rows, rows)))[:, :1]
    normal_rows = (rows_ref[...] * scale).astype(jnp.bfloat16)
    destination = place_ref[...]
    named = lax.broadcasted_iota(jnp.int32, (devices, rows), 0) == destination
    earlier = lax.broadcasted_iota(jnp.int32, (rows, rows), 0) < lax.broadcasted_iota(
        jnp.int32, (rows, rows), 1
    )
    counts = jnp.dot(
        named.astype(jnp.float32).astype(jnp.bfloat16),
        earlier.astype(jnp.float32).astype(jnp.bfloat16),
        preferred_element_type=jnp.float32,
    )
    rank = jnp.sum(jnp.where(named, counts, 0.0), axis=0, keepdims=True).astype(jnp.int32)
    target = destination * cap + rank
    for k, out_ref in enumerate(out_refs):
        slots = out_ref.shape[0]
        slot = firsts_ref[k] + lax.broadcasted_iota(jnp.int32, (slots, rows), 0)
        one_hot = (slot == target).astype(jnp.float32).astype(jnp.bfloat16)
        out_ref[...] = jnp.dot(
            one_hot, normal_rows, preferred_element_type=jnp.float32
        ).astype(jnp.bfloat16)


def collect_kernel(firsts_ref, *refs):
    *block_refs, out_ref = refs
    for k, block_ref in enumerate(block_refs):
        slots = block_ref.shape[0]
        at = pl.ds(pl.multiple_of(firsts_ref[k], slots), slots)
        out_ref[at, :] = block_ref[...]


def partner(index, k, devices):
    if devices & (devices - 1) == 0:
        return index ^ k
    return (index + k) % devices


def sender(index, k, devices):
    if devices & (devices - 1) == 0:
        return index ^ k
    return (index - k) % devices


def exchange(value, axes, k, devices):
    return lax.ppermute(value, axes, [(i, partner(i, k, devices)) for i in range(devices)])


def local(audio, lengths, conv_kernel, w_qkv, w_out, place, w_adapt):
    frame_count, channels = audio.shape
    seq_devices = lax.axis_size("tm")
    mp_devices = lax.axis_size("mp")
    recs = lengths.shape[1]
    group_frames = frame_count * seq_devices
    width = channels // mp_devices
    pooled_rows = frame_count // STRIDE
    heads = w_qkv.shape[2] // HDE
    where = jnp.concatenate(
        [jnp.stack([lax.axis_index("tm") * frame_count, lax.axis_index("mp")]), lengths[0]]
    )

    if seq_devices == 2:
        ends = jnp.concatenate([audio[:HALO], audio[frame_count - HALO :]], axis=0)
        halo = exchange(ends, "tm", 1, 2)
    else:
        up = [(i, i + 1) for i in range(seq_devices - 1)]
        down = [(j, i) for i, j in up]
        after = lax.ppermute(audio[:HALO], "tm", down)
        before = lax.ppermute(audio[frame_count - HALO :], "tm", up)
        halo = jnp.concatenate([after, before], axis=0)

    smem = pl.BlockSpec(memory_space=pltpu.SMEM)
    vmem = pl.BlockSpec(memory_space=pltpu.VMEM)
    hbm = pl.BlockSpec(memory_space=pltpu.HBM)
    w_three = jnp.transpose(w_qkv, (1, 0, 2))
    taps = conv_kernel.shape[0]

    def tiles(count, *lead):
        return pltpu.VMEM((*lead, count * SUBLANES, LANES), jnp.float32)

    def results(rows):
        return [
            jax.ShapeDtypeStruct((rows, heads * LANES), jnp.bfloat16),
            jax.ShapeDtypeStruct((rows, 2 * heads * LANES), jnp.bfloat16),
            jax.ShapeDtypeStruct((rows // STRIDE, width), jnp.float32),
        ]

    def shared(rows):
        return [
            pltpu.VMEM(conv_kernel.shape, jnp.float32),
            tiles(taps),
            tiles(taps),
            pltpu.VMEM((rows, channels), jnp.bfloat16),
            pltpu.VMEM((rows, channels), jnp.bfloat16),
            pltpu.VMEM(w_three.shape, jnp.bfloat16),
            pltpu.SMEM((recs,), jnp.int32),
            pltpu.SMEM((recs,), jnp.int32),
        ]

    mid = frame_count - 2 * EDGE
    mid_q, mid_kv, mid_mixed = pl.pallas_call(
        interior_kernel,
        out_shape=results(mid),
        in_specs=[smem, hbm, hbm, hbm],
        out_specs=[vmem] * 3,
        scratch_shapes=[
            pltpu.VMEM((mid + 2 * HALO, channels), jnp.bfloat16),
            tiles(mid + 2 * HALO),
            tiles(mid),
            tiles(mid // 2 + 2 * HALO),
            tiles(mid // 2),
            *shared(mid),
            *[pltpu.SemaphoreType.DMA] * 3,
        ],
        compiler_params=pltpu.CompilerParams(vmem_limit_bytes=53 * MIB),
        cost_estimate=pl.CostEstimate(
            flops=6 * mid * channels * w_qkv.shape[2], bytes_accessed=40 * MIB, transcendentals=0
        ),
        name="interior",
    )(where, conv_kernel, audio, w_three)
    edge_q, edge_kv, edge_mixed = pl.pallas_call(
        edge_kernel,
        out_shape=results(2 * EDGE),
        in_specs=[smem, hbm, hbm, vmem, hbm],
        out_specs=[vmem] * 3,
        scratch_shapes=[
            pltpu.VMEM((2 * (EDGE + HALO), channels), jnp.bfloat16),
            tiles(EDGE + 2 * HALO, 2),
            tiles(EDGE, 2),
            tiles(EDGE + 2 * HALO),
            tiles(EDGE),
            *shared(2 * EDGE),
            *[pltpu.SemaphoreType.DMA] * 4,
        ],
        compiler_params=pltpu.CompilerParams(vmem_limit_bytes=53 * MIB),
        cost_estimate=pl.CostEstimate(
            flops=12 * EDGE * channels * w_qkv.shape[2], bytes_accessed=8 * MIB, transcendentals=0
        ),
        name="edges",
    )(
        where,
        conv_kernel,
        audio,
        halo,
        w_three,
    )

    kv_blocks = [mid_kv, edge_kv]
    for k in range(1, seq_devices):
        kv_blocks += [exchange(block, "tm", k, seq_devices) for block in (mid_kv, edge_kv)]
    mp_index = lax.axis_index("mp")
    mp_targets = jnp.stack([partner(mp_index, k, mp_devices) for k in range(mp_devices)])
    mp_senders = jnp.stack([sender(mp_index, k, mp_devices) for k in range(mp_devices)])
    part = (pooled_rows, width)
    own_part, *parts = pl.pallas_call(
        functools.partial(attend_kernel, seq_devices, 256 if seq_devices <= 2 else 64),
        out_shape=[jax.ShapeDtypeStruct(part, jnp.float32)]
        + [jax.ShapeDtypeStruct(part, jnp.bfloat16)] * (mp_devices - 1),
        in_specs=[smem] + [vmem] * 4 + [hbm] + [vmem] * len(kv_blocks),
        out_specs=[vmem] * mp_devices,
        scratch_shapes=[
            pltpu.VMEM((frame_count, heads * LANES), jnp.bfloat16),
            pltpu.VMEM((group_frames, 2 * heads * LANES), jnp.bfloat16),
            pltpu.VMEM(part, jnp.float32),
            pltpu.VMEM((pooled_rows, heads * LANES), jnp.bfloat16),
            pltpu.VMEM((heads * LANES, channels), jnp.bfloat16),
            pltpu.SemaphoreType.DMA((heads,)),
        ],
        compiler_params=pltpu.CompilerParams(
            vmem_limit_bytes=44 * MIB
        ),
        name="attend",
    )(mp_targets, mid_q, edge_q, mid_mixed, edge_mixed, w_out, *kv_blocks)
    others = range(1, mp_devices)
    for k in others:
        own_part += exchange(parts[k - 1], "mp", k, mp_devices).astype(jnp.float32)
    own_part = own_part.astype(jnp.bfloat16)
    pooled = [own_part] + [exchange(own_part, "mp", k, mp_devices) for k in others]

    columns = w_adapt.shape[1]
    projected, squares = pl.pallas_call(
        project_kernel,
        out_shape=[
            jax.ShapeDtypeStruct((pooled_rows, columns), jnp.float32),
            jax.ShapeDtypeStruct((SUBLANES, pooled_rows), jnp.float32),
        ],
        in_specs=[smem] + [vmem] * (mp_devices + 1),
        out_specs=[vmem] * 2,
        scratch_shapes=[pltpu.VMEM((pooled_rows, channels), jnp.bfloat16)],
        compiler_params=pltpu.CompilerParams(vmem_limit_bytes=16 * MIB),
        name="project",
    )(mp_senders, *pooled, w_adapt)
    squares = [squares] + [exchange(squares, "mp", k, mp_devices) for k in others]

    axes = ("section", "tm")
    device_count = lax.axis_size("section") * seq_devices
    me = lax.axis_index(axes)
    cap = max(2, (2 * pooled_rows + device_count - 1) // device_count)
    direct = device_count <= 8
    if direct:
        firsts = jnp.stack([partner(me, k, device_count) * cap for k in range(device_count)])
        blocks = [jax.ShapeDtypeStruct((cap, columns), jnp.bfloat16)] * device_count
    else:
        firsts = jnp.zeros((1,), jnp.int32)
        blocks = [jax.ShapeDtypeStruct((device_count * cap, columns), jnp.bfloat16)]
    blocks = pl.pallas_call(
        functools.partial(route_kernel, cap),
        out_shape=blocks,
        in_specs=[smem] + [vmem] * (mp_devices + 2),
        out_specs=[vmem] * len(blocks),
        compiler_params=pltpu.CompilerParams(vmem_limit_bytes=16 * MIB),
        name="route",
    )(firsts, place.T, projected, *squares)
    if not direct:
        return lax.all_to_all(blocks[0], axes, split_axis=0, concat_axis=0, tiled=True)
    arrived = [blocks[0]] + [
        exchange(blocks[k], axes, k, device_count) for k in range(1, device_count)
    ]
    firsts = jnp.stack([sender(me, k, device_count) * cap for k in range(device_count)])
    return pl.pallas_call(
        collect_kernel,
        out_shape=jax.ShapeDtypeStruct((device_count * cap, columns), jnp.bfloat16),
        in_specs=[smem] + [vmem] * device_count,
        out_specs=vmem,
        compiler_params=pltpu.CompilerParams(vmem_limit_bytes=8 * MIB),
        name="collect",
    )(firsts, *arrived)


def solution(mesh):
    placed = (
        P(("section", "tm"), None),
        P("section", None),
        P(),
        P(None, None, "mp"),
        P("mp", None),
        P(("section", "tm"), None),
        P(None, "mp"),
    )
    return jax.shard_map(
        local, mesh=mesh, in_specs=placed, out_specs=P(("section", "tm"), "mp"), check_vma=False
    )
```

```python
import functools
import math

import jax
import jax.numpy as jnp
from jax import lax
from jax.experimental import pallas as pl
from jax.experimental.pallas import tpu as pltpu
from jax.sharding import PartitionSpec as P

HDE = 96
D = 5120
STRIDE = 4
LANES = 128
SUBLANES = 8
HALO = 16
EDGE = 32
BLOCK = 16
GROUP = 16
MIB = 1 << 20
HIDDEN = -1e30


def conv_blocks(src, dst, taps, blocks, run, firsts, recs, bounds, starts_ref, ends_ref):
    count = taps.shape[0] // SUBLANES
    reach = count // 2
    span = BLOCK + count - 1
    shape = (SUBLANES, LANES)
    upper = lax.broadcasted_iota(jnp.int32, shape, 0) < SUBLANES // 2

    def both(values):
        if len(values) == 1:
            return jnp.full(shape, values[0], jnp.int32)
        return jnp.where(upper, values[0], values[1])

    def convolve(base, inside):
        def frame(k):
            at = (base + k + HALO - reach) * SUBLANES
            return src[pl.ds(pl.multiple_of(at, SUBLANES), SUBLANES), :]

        kernel = [taps[j * SUBLANES : (j + 1) * SUBLANES, :] for j in range(count)]
        totals = [None] * BLOCK
        for k in range(span):
            value = frame(k)
            if inside is not None:
                value = jnp.where(inside(k), value, 0.0)
            for t in range(max(0, k - count + 1), min(BLOCK, k + 1)):
                term = kernel[k - t] * value
                totals[t] = term if totals[t] is None else totals[t] + term
        for t in range(BLOCK):
            at = pl.ds(pl.multiple_of((base + t) * SUBLANES, SUBLANES), SUBLANES)
            half = 0.5 * totals[t]
            value = frame(t + reach) + half * (1.0 + jnp.tanh(half))
            if inside is not None:
                value = jnp.where(inside(t + reach), value, dst[at, :])
            dst[at, :] = value

    def touched(base, length):
        found = jnp.zeros((), jnp.bool_)
        for first in firsts:
            for bound in bounds[:-1]:
                at = bound - first - base
                found = found | ((at > -reach) & (at < length + reach))
        return found

    def masked(base):
        positions = [first + base for first in firsts]
        begin, extra = [], jnp.zeros((), jnp.int32)
        for position in positions:
            first = last = jnp.zeros((), jnp.int32)
            for bound in bounds[:-1]:
                first += (bound <= position).astype(jnp.int32)
                last += (bound <= position + BLOCK - 1).astype(jnp.int32)
            begin.append(first)
            extra = jnp.maximum(extra, last - first)

        def once(turn, carry):
            which = [jnp.minimum(first + turn, recs - 1) for first in begin]
            low = both([starts_ref[r] - p for r, p in zip(which, positions)])
            high = both([ends_ref[r] - p for r, p in zip(which, positions)])
            convolve(base, lambda k: (low <= k - reach) & (high > k - reach))
            return carry

        lax.fori_loop(0, extra + 1, once, 0)

    def blocks_of_run(i, carry):
        base = i * run * BLOCK
        any_touched = touched(base, run * BLOCK)

        @pl.when(jnp.logical_not(any_touched))
        def _():
            for j in range(run):
                convolve(base + j * BLOCK, None)

        @pl.when(any_touched)
        def _():
            def one(j, carry):
                here = base + j * BLOCK
                mine = touched(here, BLOCK)

                @pl.when(mine)
                def _():
                    masked(here)

                @pl.when(jnp.logical_not(mine))
                def _():
                    convolve(here, None)

                return carry

            lax.fori_loop(0, run, one, 0)

        return carry

    lax.fori_loop(0, blocks // run, blocks_of_run, 0)


def shuffle(back):
    row = lax.broadcasted_iota(jnp.int32, (LANES, LANES), 1 if back else 0)
    column = lax.broadcasted_iota(jnp.int32, (LANES, LANES), 0 if back else 1)
    moved = (row // SUBLANES == column % GROUP) & (row % SUBLANES == column // GROUP)
    return moved.astype(jnp.float32).astype(jnp.bfloat16)


def to_tiles(matrix, values, ref, frame):
    stack = jnp.concatenate(values, axis=0)
    at = pl.ds(frame * SUBLANES, GROUP * SUBLANES)
    ref[at, :] = jnp.dot(matrix, stack, preferred_element_type=jnp.float32)


def from_tiles(matrix, ref, frame):
    rows = GROUP * SUBLANES
    low = ref[frame * SUBLANES : frame * SUBLANES + rows, :].astype(jnp.bfloat16)
    moved = jnp.dot(matrix, low, preferred_element_type=jnp.float32)
    return [moved[k * GROUP : (k + 1) * GROUP] for k in range(SUBLANES)]


def blocks_of(value, first, count):
    return [value[:, k * LANES : (k + 1) * LANES] for k in range(first, first + count)]


def recording_bounds(where_ref, starts_ref, ends_ref):
    bounds, total = [], jnp.zeros((), jnp.int32)
    for r in range(where_ref.shape[0] - 2):
        starts_ref[r] = total
        total = total + where_ref[2 + r]
        ends_ref[r] = total
        bounds.append(total)
    return bounds


def spread_taps(taps_ref, full_taps, half_taps):
    count = taps_ref.shape[0]
    blocks = taps_ref.shape[1] // LANES
    for k in range(blocks):
        value = taps_ref[:, k * LANES : (k + 1) * LANES]
        if k < SUBLANES:
            full_taps[pl.ds(k, count, stride=SUBLANES), :] = value
        else:
            for half in range(2):
                at = k - SUBLANES + half * SUBLANES // 2
                half_taps[pl.ds(at, count, stride=SUBLANES), :] = value


def normalise(blocks, mixed, normed, at):
    values = jnp.concatenate(blocks, axis=1)
    mixed[at, :] = values.astype(jnp.bfloat16)
    centred = values - jnp.mean(values, -1, keepdims=True)
    variance = jnp.mean(centred * centred, -1, keepdims=True)
    normed[at, :] = (centred * lax.rsqrt(variance + 1e-05)).astype(jnp.bfloat16)


def pool_rows(rows):
    few = rows // STRIDE
    chosen = (
        lax.broadcasted_iota(jnp.int32, (few, rows), 1) // STRIDE
        == lax.broadcasted_iota(jnp.int32, (few, rows), 0)
    )
    return (chosen.astype(jnp.float32) * (1.0 / STRIDE)).astype(jnp.bfloat16)


def project_heads(normed_rows, w_vmem, position, bounds, at, q_ref, kv_ref):
    recs = len(bounds)
    heads = w_vmem.shape[2] // HDE
    lane = lax.broadcasted_iota(jnp.int32, position.shape, 1)
    mine = jnp.zeros(position.shape, jnp.int32)
    for bound in bounds:
        mine += (position >= bound).astype(jnp.int32)
    same = lane - HDE == mine
    extra_q = jnp.where(same | (lane >= HDE + recs), 0.0, HIDDEN)
    extra_k = jnp.where(same, 1.0, 0.0)
    extra_v = jnp.where(lane == HDE, 1.0, 0.0)
    score_scale = HDE ** (-0.5) * math.log2(math.e)
    for kind, extra in enumerate((extra_q, extra_k, extra_v)):
        result = jnp.dot(normed_rows, w_vmem[kind], preferred_element_type=jnp.float32)
        if kind == 0:
            result = result * score_scale
        for h in range(heads):
            tile, start = divmod(h * HDE, LANES)
            tiles = 1 if start + HDE <= LANES else 2
            head = result[:, tile * LANES : (tile + tiles) * LANES]
            if start:
                head = pltpu.roll(head, tiles * LANES - start, 1)
            head = jnp.where(lane < HDE, head[:, :LANES], extra).astype(jnp.bfloat16)
            if kind == 0:
                q_ref[at, h * LANES : (h + 1) * LANES] = head
            else:
                first = ((kind - 1) * heads + h) * LANES
                kv_ref[at, first : first + LANES] = head


def interior_kernel(
    where_ref,
    taps_hbm,
    audio_ref,
    w_ref,
    q_ref,
    kv_ref,
    pooled_ref,
    audio,
    full_src,
    full_dst,
    half_src,
    half_dst,
    taps_ref,
    full_taps,
    half_taps,
    mixed,
    normed,
    w_vmem,
    starts_ref,
    ends_ref,
    audio_sem,
    taps_sem,
    w_sem,
):
    rows = q_ref.shape[0]
    inner = rows + 2 * HALO
    skip = EDGE - HALO
    half = rows // 2
    load_audio = pltpu.make_async_copy(audio_ref.at[skip : skip + inner], audio, audio_sem)
    load_taps = pltpu.make_async_copy(taps_hbm, taps_ref, taps_sem)
    load_audio.start()
    load_taps.start()
    load_w = pltpu.make_async_copy(w_ref, w_vmem, w_sem)
    load_w.start()
    bounds = recording_bounds(where_ref, starts_ref, ends_ref)
    start = where_ref[0] + EDGE
    forward, back = shuffle(False), shuffle(True)
    load_audio.wait()
    side = SUBLANES // 2
    for row in range(0, inner, GROUP):
        value = audio[row : row + GROUP, : SUBLANES * LANES]
        to_tiles(forward, blocks_of(value, 0, SUBLANES), full_src, row)
    for row in range(0, half + 2 * HALO, GROUP):
        pair = [
            block
            for at in (row, row + half)
            for block in blocks_of(audio[at : at + GROUP, :], SUBLANES, side)
        ]
        to_tiles(forward, pair, half_src, row)
    load_taps.wait()
    spread_taps(taps_ref, full_taps, half_taps)
    recs = len(bounds)
    common = (recs, bounds, starts_ref, ends_ref)
    conv_blocks(full_src, full_dst, full_taps, rows // BLOCK, 4, [start], *common)
    conv_blocks(half_src, half_dst, half_taps, half // BLOCK, 2, [start, start + half], *common)


    for row in range(0, half, GROUP):
        pair = from_tiles(back, half_dst, row)
        for which in range(2):
            at = which * half + row
            blocks = from_tiles(back, full_dst, at) + pair[which * side : (which + 1) * side]
            normalise(blocks, mixed, normed, slice(at, at + GROUP))

    width = pooled_ref.shape[1]
    own_columns = pl.ds(pl.multiple_of(where_ref[1] * width, LANES), width)
    pooled_ref[...] = jnp.dot(
        pool_rows(rows), mixed[:, own_columns], preferred_element_type=jnp.float32
    )
    load_w.wait()
    for which in range(2):
        at = slice(which * half, (which + 1) * half)
        position = start + which * half + lax.broadcasted_iota(jnp.int32, (half, LANES), 0)
        project_heads(normed[at, :], w_vmem, position, bounds, at, q_ref, kv_ref)


def edge_kernel(
    where_ref,
    taps_hbm,
    audio_ref,
    halo_ref,
    w_ref,
    q_ref,
    kv_ref,
    pooled_ref,
    audio,
    full_src,
    full_dst,
    half_src,
    half_dst,
    taps_ref,
    full_taps,
    half_taps,
    mixed,
    normed,
    w_vmem,
    starts_ref,
    ends_ref,
    first_sem,
    last_sem,
    taps_sem,
    w_sem,
):
    frames = audio_ref.shape[0]
    known = EDGE + HALO
    loads = [
        pltpu.make_async_copy(audio_ref.at[:known], audio.at[:known], first_sem),
        pltpu.make_async_copy(audio_ref.at[frames - known :], audio.at[known:], last_sem),
        pltpu.make_async_copy(taps_hbm, taps_ref, taps_sem),
        pltpu.make_async_copy(w_ref, w_vmem, w_sem),
    ]
    for load in loads:
        load.start()
    bounds = recording_bounds(where_ref, starts_ref, ends_ref)
    forward, back = shuffle(False), shuffle(True)
    starts = [where_ref[0], where_ref[0] + frames - EDGE]
    length = EDGE + 2 * HALO
    has_before = (starts[0] > 0).astype(jnp.float32)
    has_after = (starts[0] + frames < bounds[-1]).astype(jnp.float32)
    before = (halo_ref[HALO:, :].astype(jnp.float32) * has_before).astype(jnp.bfloat16)
    after = (halo_ref[:HALO, :].astype(jnp.float32) * has_after).astype(jnp.bfloat16)
    for load in loads[:3]:
        load.wait()
    side = SUBLANES // 2
    for row in range(0, length, GROUP):
        first = before if row == 0 else audio[row - HALO : row - HALO + GROUP, :]
        last = after if row == known else audio[known + row : known + row + GROUP, :]
        for which, value in enumerate((first, last)):
            to_tiles(forward, blocks_of(value, 0, SUBLANES), full_src.at[which], row)
        pair = blocks_of(first, SUBLANES, side) + blocks_of(last, SUBLANES, side)
        to_tiles(forward, pair, half_src, row)
    spread_taps(taps_ref, full_taps, half_taps)
    recs = len(bounds)
    common = (recs, bounds, starts_ref, ends_ref)
    for which in range(2):
        conv_blocks(
            full_src.at[which],
            full_dst.at[which],
            full_taps,
            EDGE // BLOCK,
            2,
            [starts[which]],
            *common,
        )
    conv_blocks(half_src, half_dst, half_taps, EDGE // BLOCK, 2, starts, *common)
    for row in range(0, EDGE, GROUP):
        pair = from_tiles(back, half_dst, row)
        for which in range(2):
            blocks = from_tiles(back, full_dst.at[which], row)
            blocks += pair[which * side : (which + 1) * side]
            at = which * EDGE + row
            normalise(blocks, mixed, normed, slice(at, at + GROUP))
    width = pooled_ref.shape[1]
    own_columns = pl.ds(pl.multiple_of(where_ref[1] * width, LANES), width)
    pooled_ref[...] = jnp.dot(
        pool_rows(2 * EDGE), mixed[:, own_columns], preferred_element_type=jnp.float32
    )
    loads[3].wait()
    row = lax.broadcasted_iota(jnp.int32, (2 * EDGE, LANES), 0)
    position = jnp.where(row < EDGE, starts[0] + row, starts[1] - EDGE + row)
    project_heads(normed[...], w_vmem, position, bounds, slice(None), q_ref, kv_ref)


def attend_kernel(count, part, rows, targets_ref, mid_q, edge_q, mid_mixed, edge_mixed, w_ref, *refs):
    kv_refs, out_refs = refs[: 2 * count], refs[2 * count : -6]
    queries, kv, mixed, pooled, w_vmem, w_sem = refs[-6:]
    frames = queries.shape[0]
    heads = queries.shape[1] // LANES
    width = mixed.shape[1]
    loads = [
        pltpu.make_async_copy(
            w_ref.at[h * HDE : (h + 1) * HDE], w_vmem.at[h * LANES : h * LANES + HDE], w_sem.at[h]
        )
        for h in range(heads)
    ]
    for load in loads:
        load.start()
    for h in range(heads):
        w_vmem[h * LANES + HDE : (h + 1) * LANES, :] = jnp.zeros(
            (LANES - HDE, w_vmem.shape[1]), jnp.bfloat16
        )
    for out, mid, edge, cut in (
        (queries, mid_q, edge_q, EDGE),
        (mixed, mid_mixed, edge_mixed, EDGE // STRIDE),
    ):
        inner = out.shape[0] - cut
        if part == 0:
            out[:cut, :] = edge[:cut, :]
            out[cut:, :] = mid[:inner, :]
        else:
            out[:inner, :] = mid[inner:, :]
            out[inner:, :] = edge[cut:, :]
    at = 0
    for ref in kv_refs:
        kv[at : at + ref.shape[0], :] = ref[...]
        at += ref.shape[0]
    few = rows // STRIDE
    pool = pool_rows(rows)

    def step(i, carry):
        at = pl.ds(pl.multiple_of(i * rows, rows), rows)
        for h in range(heads):
            lanes = slice(h * LANES, (h + 1) * LANES)
            scores = lax.dot_general(
                queries[at, lanes],
                kv[:, lanes],
                (((1,), (1,)), ((), ())),
                preferred_element_type=jnp.float32,
            )
            peak = jnp.max(scores, axis=1, keepdims=True)
            weights = jnp.exp2(scores - peak).astype(jnp.bfloat16)
            values = kv[:, (heads + h) * LANES : (heads + h + 1) * LANES]
            out = jnp.dot(weights, values, preferred_element_type=jnp.float32)
            attended = (out * (1.0 / out[:, HDE : HDE + 1])).astype(jnp.bfloat16)
            pooled[pl.ds(pl.multiple_of(i * few, few), few), lanes] = jnp.dot(
                pool, attended, preferred_element_type=jnp.float32
            ).astype(jnp.bfloat16)
        return carry

    lax.fori_loop(0, frames // rows, step, 0)
    for load in loads:
        load.wait()
    for k, out_ref in enumerate(out_refs):
        columns = pl.ds(pl.multiple_of(targets_ref[k] * width, LANES), width)
        total = jnp.dot(pooled[...], w_vmem[:, columns], preferred_element_type=jnp.float32)
        if k == 0:
            total += mixed[...]
        out_ref[...] = total.astype(out_ref.dtype)


def project_kernel(targets_ref, *refs):
    *part_refs, w_ref, out_ref, squares_ref, pooled = refs
    width = part_refs[0].shape[1]
    for k, part_ref in enumerate(part_refs):
        at = pl.ds(pl.multiple_of(targets_ref[k] * width, LANES), width)
        pooled[:, at] = part_ref[...]
    total = jnp.dot(pooled[...], w_ref[...], preferred_element_type=jnp.float32)
    out_ref[...] = total
    rows = total.shape[0]
    squares = jnp.sum(total * total, axis=1, keepdims=True)
    squares_ref[...] = jnp.transpose(jnp.broadcast_to(squares, (rows, LANES)))[:SUBLANES]


def route_kernel(cap, firsts_ref, place_ref, first_ref, second_ref, *refs):
    square_refs, out_refs = refs[: -firsts_ref.shape[0]], refs[-firsts_ref.shape[0] :]
    rows = place_ref.shape[1]
    devices = sum(ref.shape[0] for ref in out_refs) // cap
    count = len(square_refs) // 2
    normal_rows = []
    for ref, parts in ((first_ref, square_refs[:count]), (second_ref, square_refs[count:])):
        squares = functools.reduce(jnp.add, [part[...] for part in parts])
        scale = lax.rsqrt(squares[:1] / D + 1e-05)
        scale = jnp.transpose(jnp.broadcast_to(scale, (LANES, ref.shape[0])))[:, :1]
        normal_rows.append((ref[...] * scale).astype(jnp.bfloat16))
    normal_rows = jnp.concatenate(normal_rows, axis=0)
    destination = place_ref[...]
    named = lax.broadcasted_iota(jnp.int32, (devices, rows), 0) == destination
    earlier = lax.broadcasted_iota(jnp.int32, (rows, rows), 0) < lax.broadcasted_iota(
        jnp.int32, (rows, rows), 1
    )
    counts = jnp.dot(
        named.astype(jnp.float32).astype(jnp.bfloat16),
        earlier.astype(jnp.float32).astype(jnp.bfloat16),
        preferred_element_type=jnp.float32,
    )
    rank = jnp.sum(jnp.where(named, counts, 0.0), axis=0, keepdims=True).astype(jnp.int32)
    target = destination * cap + rank
    for k, out_ref in enumerate(out_refs):
        slots = out_ref.shape[0]
        slot = firsts_ref[k] + lax.broadcasted_iota(jnp.int32, (slots, rows), 0)
        one_hot = (slot == target).astype(jnp.float32).astype(jnp.bfloat16)
        out_ref[...] = jnp.dot(
            one_hot, normal_rows, preferred_element_type=jnp.float32
        ).astype(jnp.bfloat16)


def collect_kernel(firsts_ref, *refs):
    *block_refs, out_ref = refs
    for k, block_ref in enumerate(block_refs):
        slots = block_ref.shape[0]
        at = pl.ds(pl.multiple_of(firsts_ref[k], slots), slots)
        out_ref[at, :] = block_ref[...]


def partner(index, k, devices):
    if devices & (devices - 1) == 0:
        return index ^ k
    return (index + k) % devices


def sender(index, k, devices):
    if devices & (devices - 1) == 0:
        return index ^ k
    return (index - k) % devices


def exchange(value, axes, k, devices):
    return lax.ppermute(value, axes, [(i, partner(i, k, devices)) for i in range(devices)])


def local(audio, lengths, conv_kernel, w_qkv, w_out, place, w_adapt):
    frame_count, channels = audio.shape
    seq_devices = lax.axis_size("tm")
    mp_devices = lax.axis_size("mp")
    recs = lengths.shape[1]
    group_frames = frame_count * seq_devices
    width = channels // mp_devices
    pooled_rows = frame_count // STRIDE
    heads = w_qkv.shape[2] // HDE
    where = jnp.concatenate(
        [jnp.stack([lax.axis_index("tm") * frame_count, lax.axis_index("mp")]), lengths[0]]
    )

    if seq_devices == 2:
        ends = jnp.concatenate([audio[:HALO], audio[frame_count - HALO :]], axis=0)
        halo = exchange(ends, "tm", 1, 2)
    else:
        up = [(i, i + 1) for i in range(seq_devices - 1)]
        down = [(j, i) for i, j in up]
        after = lax.ppermute(audio[:HALO], "tm", down)
        before = lax.ppermute(audio[frame_count - HALO :], "tm", up)
        halo = jnp.concatenate([after, before], axis=0)

    smem = pl.BlockSpec(memory_space=pltpu.SMEM)
    vmem = pl.BlockSpec(memory_space=pltpu.VMEM)
    hbm = pl.BlockSpec(memory_space=pltpu.HBM)
    w_three = jnp.transpose(w_qkv, (1, 0, 2))
    taps = conv_kernel.shape[0]

    def tiles(count, *lead):
        return pltpu.VMEM((*lead, count * SUBLANES, LANES), jnp.float32)

    def results(rows):
        return [
            jax.ShapeDtypeStruct((rows, heads * LANES), jnp.bfloat16),
            jax.ShapeDtypeStruct((rows, 2 * heads * LANES), jnp.bfloat16),
            jax.ShapeDtypeStruct((rows // STRIDE, width), jnp.float32),
        ]

    def shared(rows):
        return [
            pltpu.VMEM(conv_kernel.shape, jnp.float32),
            tiles(taps),
            tiles(taps),
            pltpu.VMEM((rows, channels), jnp.bfloat16),
            pltpu.VMEM((rows, channels), jnp.bfloat16),
            pltpu.VMEM(w_three.shape, jnp.bfloat16),
            pltpu.SMEM((recs,), jnp.int32),
            pltpu.SMEM((recs,), jnp.int32),
        ]

    mid = frame_count - 2 * EDGE
    mid_q, mid_kv, mid_mixed = pl.pallas_call(
        interior_kernel,
        out_shape=results(mid),
        in_specs=[smem, hbm, hbm, hbm],
        out_specs=[vmem] * 3,
        scratch_shapes=[
            pltpu.VMEM((mid + 2 * HALO, channels), jnp.bfloat16),
            tiles(mid + 2 * HALO),
            tiles(mid),
            tiles(mid // 2 + 2 * HALO),
            tiles(mid // 2),
            *shared(mid),
            *[pltpu.SemaphoreType.DMA] * 3,
        ],
        compiler_params=pltpu.CompilerParams(vmem_limit_bytes=53 * MIB),
        cost_estimate=pl.CostEstimate(
            flops=6 * mid * channels * w_qkv.shape[2], bytes_accessed=40 * MIB, transcendentals=0
        ),
        name="interior",
    )(where, conv_kernel, audio, w_three)
    edge_q, edge_kv, edge_mixed = pl.pallas_call(
        edge_kernel,
        out_shape=results(2 * EDGE),
        in_specs=[smem, hbm, hbm, vmem, hbm],
        out_specs=[vmem] * 3,
        scratch_shapes=[
            pltpu.VMEM((2 * (EDGE + HALO), channels), jnp.bfloat16),
            tiles(EDGE + 2 * HALO, 2),
            tiles(EDGE, 2),
            tiles(EDGE + 2 * HALO),
            tiles(EDGE),
            *shared(2 * EDGE),
            *[pltpu.SemaphoreType.DMA] * 4,
        ],
        compiler_params=pltpu.CompilerParams(vmem_limit_bytes=53 * MIB),
        cost_estimate=pl.CostEstimate(
            flops=12 * EDGE * channels * w_qkv.shape[2], bytes_accessed=8 * MIB, transcendentals=0
        ),
        name="edges",
    )(
        where,
        conv_kernel,
        audio,
        halo,
        w_three,
    )

    kv_blocks = [mid_kv, edge_kv]
    for k in range(1, seq_devices):
        kv_blocks += [exchange(block, "tm", k, seq_devices) for block in (mid_kv, edge_kv)]
    mp_index = lax.axis_index("mp")
    mp_targets = jnp.stack([partner(mp_index, k, mp_devices) for k in range(mp_devices)])
    mp_senders = jnp.stack([sender(mp_index, k, mp_devices) for k in range(mp_devices)])
    others = range(1, mp_devices)
    half = frame_count // 2
    part = (pooled_rows // 2, width)
    columns = w_adapt.shape[1]

    def attend(side):
        return pl.pallas_call(
            functools.partial(attend_kernel, seq_devices, side, 256 if seq_devices <= 2 else 64),
            out_shape=[jax.ShapeDtypeStruct(part, jnp.float32)]
            + [jax.ShapeDtypeStruct(part, jnp.bfloat16)] * (mp_devices - 1),
            in_specs=[smem] + [vmem] * 4 + [hbm] + [vmem] * len(kv_blocks),
            out_specs=[vmem] * mp_devices,
            scratch_shapes=[
                pltpu.VMEM((half, heads * LANES), jnp.bfloat16),
                pltpu.VMEM((group_frames, 2 * heads * LANES), jnp.bfloat16),
                pltpu.VMEM(part, jnp.float32),
                pltpu.VMEM((part[0], heads * LANES), jnp.bfloat16),
                pltpu.VMEM((heads * LANES, channels), jnp.bfloat16),
                pltpu.SemaphoreType.DMA((heads,)),
            ],
            compiler_params=pltpu.CompilerParams(vmem_limit_bytes=44 * MIB),
            cost_estimate=pl.CostEstimate(
                flops=16 * half * group_frames * heads * LANES, bytes_accessed=0, transcendentals=0
            ),
            name="attend",
        )(mp_targets, mid_q, edge_q, mid_mixed, edge_mixed, w_out, *kv_blocks)

    def sum_heads(parts):
        own, *sent = parts
        for k in others:
            own += exchange(sent[k - 1], "mp", k, mp_devices).astype(jnp.float32)
        return own.astype(jnp.bfloat16)

    def project(own):
        pooled = [own] + [exchange(own, "mp", k, mp_devices) for k in others]
        rows, squares = pl.pallas_call(
            project_kernel,
            out_shape=[
                jax.ShapeDtypeStruct((part[0], columns), jnp.float32),
                jax.ShapeDtypeStruct((SUBLANES, part[0]), jnp.float32),
            ],
            in_specs=[smem] + [vmem] * (mp_devices + 1),
            out_specs=[vmem] * 2,
            scratch_shapes=[pltpu.VMEM((part[0], channels), jnp.bfloat16)],
            compiler_params=pltpu.CompilerParams(vmem_limit_bytes=16 * MIB),
            cost_estimate=pl.CostEstimate(
                flops=4 * part[0] * channels * columns, bytes_accessed=0, transcendentals=0
            ),
            name="project",
        )(mp_senders, *pooled, w_adapt)
        return rows, [squares] + [exchange(squares, "mp", k, mp_devices) for k in others]

    first, first_squares = project(sum_heads(attend(0)))
    second, second_squares = project(sum_heads(attend(1)))

    axes = ("section", "tm")
    device_count = lax.axis_size("section") * seq_devices
    me = lax.axis_index(axes)
    cap = max(2, (2 * pooled_rows + device_count - 1) // device_count)
    direct = device_count <= 8
    if direct:
        firsts = jnp.stack([partner(me, k, device_count) * cap for k in range(device_count)])
        blocks = [jax.ShapeDtypeStruct((cap, columns), jnp.bfloat16)] * device_count
    else:
        firsts = jnp.zeros((1,), jnp.int32)
        blocks = [jax.ShapeDtypeStruct((device_count * cap, columns), jnp.bfloat16)]
    blocks = pl.pallas_call(
        functools.partial(route_kernel, cap),
        out_shape=blocks,
        in_specs=[smem] + [vmem] * (2 * mp_devices + 3),
        out_specs=[vmem] * len(blocks),
        compiler_params=pltpu.CompilerParams(vmem_limit_bytes=16 * MIB),
        name="route",
    )(firsts, place.T, first, second, *first_squares, *second_squares)
    if not direct:
        return lax.all_to_all(blocks[0], axes, split_axis=0, concat_axis=0, tiled=True)
    arrived = [blocks[0]] + [
        exchange(blocks[k], axes, k, device_count) for k in range(1, device_count)
    ]
    firsts = jnp.stack([sender(me, k, device_count) * cap for k in range(device_count)])
    return pl.pallas_call(
        collect_kernel,
        out_shape=jax.ShapeDtypeStruct((device_count * cap, columns), jnp.bfloat16),
        in_specs=[smem] + [vmem] * device_count,
        out_specs=vmem,
        compiler_params=pltpu.CompilerParams(vmem_limit_bytes=8 * MIB),
        name="collect",
    )(firsts, *arrived)


def solution(mesh):
    placed = (
        P(("section", "tm"), None),
        P("section", None),
        P(),
        P(None, None, "mp"),
        P("mp", None),
        P(("section", "tm"), None),
        P(None, "mp"),
    )
    return jax.shard_map(
        local, mesh=mesh, in_specs=placed, out_specs=P(("section", "tm"), "mp"), check_vma=False
    )
```

```python
import functools
import math

import jax
import jax.numpy as jnp
from jax import lax
from jax.experimental import pallas as pl
from jax.experimental.pallas import tpu as pltpu
from jax.sharding import PartitionSpec as P

HDE = 96
D = 5120
STRIDE = 4
LANES = 128
SUBLANES = 8
HALO = 16
EDGE = 32
BLOCK = 16
GROUP = 16
MIB = 1 << 20
HIDDEN = -1e30


def conv_blocks(src, dst, taps, blocks, run, firsts, recs, bounds, starts_ref, ends_ref):
    count = taps.shape[0] // SUBLANES
    reach = count // 2
    span = BLOCK + count - 1
    shape = (SUBLANES, LANES)
    upper = lax.broadcasted_iota(jnp.int32, shape, 0) < SUBLANES // 2

    def both(values):
        if len(values) == 1:
            return jnp.full(shape, values[0], jnp.int32)
        return jnp.where(upper, values[0], values[1])

    def convolve(base, inside):
        def frame(k):
            at = (base + k + HALO - reach) * SUBLANES
            return src[pl.ds(pl.multiple_of(at, SUBLANES), SUBLANES), :]

        kernel = [taps[j * SUBLANES : (j + 1) * SUBLANES, :] for j in range(count)]
        totals = [None] * BLOCK
        for k in range(span):
            value = frame(k)
            if inside is not None:
                value = jnp.where(inside(k), value, 0.0)
            for t in range(max(0, k - count + 1), min(BLOCK, k + 1)):
                term = kernel[k - t] * value
                totals[t] = term if totals[t] is None else totals[t] + term
        for t in range(BLOCK):
            at = pl.ds(pl.multiple_of((base + t) * SUBLANES, SUBLANES), SUBLANES)
            half = 0.5 * totals[t]
            value = frame(t + reach) + half * (1.0 + jnp.tanh(half))
            if inside is not None:
                value = jnp.where(inside(t + reach), value, dst[at, :])
            dst[at, :] = value

    def touched(base, length):
        found = jnp.zeros((), jnp.bool_)
        for first in firsts:
            for bound in bounds[:-1]:
                at = bound - first - base
                found = found | ((at > -reach) & (at < length + reach))
        return found

    def masked(base):
        positions = [first + base for first in firsts]
        begin, extra = [], jnp.zeros((), jnp.int32)
        for position in positions:
            first = last = jnp.zeros((), jnp.int32)
            for bound in bounds[:-1]:
                first += (bound <= position).astype(jnp.int32)
                last += (bound <= position + BLOCK - 1).astype(jnp.int32)
            begin.append(first)
            extra = jnp.maximum(extra, last - first)

        def once(turn, carry):
            which = [jnp.minimum(first + turn, recs - 1) for first in begin]
            low = both([starts_ref[r] - p for r, p in zip(which, positions)])
            high = both([ends_ref[r] - p for r, p in zip(which, positions)])
            convolve(base, lambda k: (low <= k - reach) & (high > k - reach))
            return carry

        lax.fori_loop(0, extra + 1, once, 0)

    def blocks_of_run(i, carry):
        base = i * run * BLOCK
        any_touched = touched(base, run * BLOCK)

        @pl.when(jnp.logical_not(any_touched))
        def _():
            for j in range(run):
                convolve(base + j * BLOCK, None)

        @pl.when(any_touched)
        def _():
            def one(j, carry):
                here = base + j * BLOCK
                mine = touched(here, BLOCK)

                @pl.when(mine)
                def _():
                    masked(here)

                @pl.when(jnp.logical_not(mine))
                def _():
                    convolve(here, None)

                return carry

            lax.fori_loop(0, run, one, 0)

        return carry

    lax.fori_loop(0, blocks // run, blocks_of_run, 0)


def shuffle(back):
    row = lax.broadcasted_iota(jnp.int32, (LANES, LANES), 1 if back else 0)
    column = lax.broadcasted_iota(jnp.int32, (LANES, LANES), 0 if back else 1)
    moved = (row // SUBLANES == column % GROUP) & (row % SUBLANES == column // GROUP)
    return moved.astype(jnp.float32).astype(jnp.bfloat16)


def to_tiles(matrix, values, ref, frame):
    stack = jnp.concatenate(values, axis=0)
    at = pl.ds(frame * SUBLANES, GROUP * SUBLANES)
    ref[at, :] = jnp.dot(matrix, stack, preferred_element_type=jnp.float32)


def from_tiles(matrix, ref, frame):
    rows = GROUP * SUBLANES
    low = ref[frame * SUBLANES : frame * SUBLANES + rows, :].astype(jnp.bfloat16)
    moved = jnp.dot(matrix, low, preferred_element_type=jnp.float32)
    return [moved[k * GROUP : (k + 1) * GROUP] for k in range(SUBLANES)]


def blocks_of(value, first, count):
    return [value[:, k * LANES : (k + 1) * LANES] for k in range(first, first + count)]


def recording_bounds(where_ref, starts_ref, ends_ref):
    bounds, total = [], jnp.zeros((), jnp.int32)
    for r in range(where_ref.shape[0] - 2):
        starts_ref[r] = total
        total = total + where_ref[2 + r]
        ends_ref[r] = total
        bounds.append(total)
    return bounds


def spread_taps(taps_ref, full_taps, half_taps):
    count = taps_ref.shape[0]
    blocks = taps_ref.shape[1] // LANES
    for k in range(blocks):
        value = taps_ref[:, k * LANES : (k + 1) * LANES]
        if k < SUBLANES:
            full_taps[pl.ds(k, count, stride=SUBLANES), :] = value
        else:
            for half in range(2):
                at = k - SUBLANES + half * SUBLANES // 2
                half_taps[pl.ds(at, count, stride=SUBLANES), :] = value


def normalise(blocks, mixed, normed, at):
    values = jnp.concatenate(blocks, axis=1)
    mixed[at, :] = values.astype(jnp.bfloat16)
    centred = values - jnp.mean(values, -1, keepdims=True)
    variance = jnp.mean(centred * centred, -1, keepdims=True)
    normed[at, :] = (centred * lax.rsqrt(variance + 1e-05)).astype(jnp.bfloat16)


def pool_rows(rows):
    few = rows // STRIDE
    chosen = (
        lax.broadcasted_iota(jnp.int32, (few, rows), 1) // STRIDE
        == lax.broadcasted_iota(jnp.int32, (few, rows), 0)
    )
    return (chosen.astype(jnp.float32) * (1.0 / STRIDE)).astype(jnp.bfloat16)


def project_heads(normed_rows, w_vmem, position, bounds, at, q_ref, kv_ref):
    recs = len(bounds)
    heads = w_vmem.shape[2] // HDE
    lane = lax.broadcasted_iota(jnp.int32, position.shape, 1)
    mine = jnp.zeros(position.shape, jnp.int32)
    for bound in bounds:
        mine += (position >= bound).astype(jnp.int32)
    same = lane - HDE == mine
    extra_q = jnp.where(same | (lane >= HDE + recs), 0.0, HIDDEN)
    extra_k = jnp.where(same, 1.0, 0.0)
    extra_v = jnp.where(lane == HDE, 1.0, 0.0)
    score_scale = HDE ** (-0.5) * math.log2(math.e)
    for kind, extra in enumerate((extra_q, extra_k, extra_v)):
        result = jnp.dot(normed_rows, w_vmem[kind], preferred_element_type=jnp.float32)
        if kind == 0:
            result = result * score_scale
        for h in range(heads):
            tile, start = divmod(h * HDE, LANES)
            tiles = 1 if start + HDE <= LANES else 2
            head = result[:, tile * LANES : (tile + tiles) * LANES]
            if start:
                head = pltpu.roll(head, tiles * LANES - start, 1)
            head = jnp.where(lane < HDE, head[:, :LANES], extra).astype(jnp.bfloat16)
            if kind == 0:
                q_ref[at, h * LANES : (h + 1) * LANES] = head
            else:
                first = ((kind - 1) * heads + h) * LANES
                kv_ref[at, first : first + LANES] = head


def interior_kernel(
    where_ref,
    taps_hbm,
    audio_ref,
    w_ref,
    q_ref,
    kv_ref,
    pooled_ref,
    audio,
    full_src,
    full_dst,
    half_src,
    half_dst,
    taps_ref,
    full_taps,
    half_taps,
    mixed,
    normed,
    w_vmem,
    starts_ref,
    ends_ref,
    audio_sem,
    taps_sem,
    w_sem,
):
    rows = q_ref.shape[0]
    inner = rows + 2 * HALO
    skip = EDGE - HALO
    half = rows // 2
    load_audio = pltpu.make_async_copy(audio_ref.at[skip : skip + inner], audio, audio_sem)
    load_taps = pltpu.make_async_copy(taps_hbm, taps_ref, taps_sem)
    load_audio.start()
    load_taps.start()
    load_w = pltpu.make_async_copy(w_ref, w_vmem, w_sem)
    load_w.start()
    bounds = recording_bounds(where_ref, starts_ref, ends_ref)
    start = where_ref[0] + EDGE
    forward, back = shuffle(False), shuffle(True)
    load_audio.wait()
    side = SUBLANES // 2
    for row in range(0, inner, GROUP):
        value = audio[row : row + GROUP, : SUBLANES * LANES]
        to_tiles(forward, blocks_of(value, 0, SUBLANES), full_src, row)
    for row in range(0, half + 2 * HALO, GROUP):
        pair = [
            block
            for at in (row, row + half)
            for block in blocks_of(audio[at : at + GROUP, :], SUBLANES, side)
        ]
        to_tiles(forward, pair, half_src, row)
    load_taps.wait()
    spread_taps(taps_ref, full_taps, half_taps)
    recs = len(bounds)
    common = (recs, bounds, starts_ref, ends_ref)
    conv_blocks(full_src, full_dst, full_taps, rows // BLOCK, 4, [start], *common)
    conv_blocks(half_src, half_dst, half_taps, half // BLOCK, 2, [start, start + half], *common)


    for row in range(0, half, GROUP):
        pair = from_tiles(back, half_dst, row)
        for which in range(2):
            at = which * half + row
            blocks = from_tiles(back, full_dst, at) + pair[which * side : (which + 1) * side]
            normalise(blocks, mixed, normed, slice(at, at + GROUP))

    width = pooled_ref.shape[1]
    own_columns = pl.ds(pl.multiple_of(where_ref[1] * width, LANES), width)
    pooled_ref[...] = jnp.dot(
        pool_rows(rows), mixed[:, own_columns], preferred_element_type=jnp.float32
    )
    load_w.wait()
    for which in range(2):
        at = slice(which * half, (which + 1) * half)
        position = start + which * half + lax.broadcasted_iota(jnp.int32, (half, LANES), 0)
        project_heads(normed[at, :], w_vmem, position, bounds, at, q_ref, kv_ref)


def edge_kernel(
    where_ref,
    taps_hbm,
    audio_ref,
    halo_ref,
    w_ref,
    q_ref,
    kv_ref,
    pooled_ref,
    audio,
    full_src,
    full_dst,
    half_src,
    half_dst,
    taps_ref,
    full_taps,
    half_taps,
    mixed,
    normed,
    w_vmem,
    starts_ref,
    ends_ref,
    first_sem,
    last_sem,
    taps_sem,
    w_sem,
):
    frames = audio_ref.shape[0]
    known = EDGE + HALO
    loads = [
        pltpu.make_async_copy(audio_ref.at[:known], audio.at[:known], first_sem),
        pltpu.make_async_copy(audio_ref.at[frames - known :], audio.at[known:], last_sem),
        pltpu.make_async_copy(taps_hbm, taps_ref, taps_sem),
        pltpu.make_async_copy(w_ref, w_vmem, w_sem),
    ]
    for load in loads:
        load.start()
    bounds = recording_bounds(where_ref, starts_ref, ends_ref)
    forward, back = shuffle(False), shuffle(True)
    starts = [where_ref[0], where_ref[0] + frames - EDGE]
    length = EDGE + 2 * HALO
    has_before = (starts[0] > 0).astype(jnp.float32)
    has_after = (starts[0] + frames < bounds[-1]).astype(jnp.float32)
    before = (halo_ref[HALO:, :].astype(jnp.float32) * has_before).astype(jnp.bfloat16)
    after = (halo_ref[:HALO, :].astype(jnp.float32) * has_after).astype(jnp.bfloat16)
    for load in loads[:3]:
        load.wait()
    side = SUBLANES // 2
    for row in range(0, length, GROUP):
        first = before if row == 0 else audio[row - HALO : row - HALO + GROUP, :]
        last = after if row == known else audio[known + row : known + row + GROUP, :]
        for which, value in enumerate((first, last)):
            to_tiles(forward, blocks_of(value, 0, SUBLANES), full_src.at[which], row)
        pair = blocks_of(first, SUBLANES, side) + blocks_of(last, SUBLANES, side)
        to_tiles(forward, pair, half_src, row)
    spread_taps(taps_ref, full_taps, half_taps)
    recs = len(bounds)
    common = (recs, bounds, starts_ref, ends_ref)
    for which in range(2):
        conv_blocks(
            full_src.at[which],
            full_dst.at[which],
            full_taps,
            EDGE // BLOCK,
            2,
            [starts[which]],
            *common,
        )
    conv_blocks(half_src, half_dst, half_taps, EDGE // BLOCK, 2, starts, *common)
    for row in range(0, EDGE, GROUP):
        pair = from_tiles(back, half_dst, row)
        for which in range(2):
            blocks = from_tiles(back, full_dst.at[which], row)
            blocks += pair[which * side : (which + 1) * side]
            at = which * EDGE + row
            normalise(blocks, mixed, normed, slice(at, at + GROUP))
    width = pooled_ref.shape[1]
    own_columns = pl.ds(pl.multiple_of(where_ref[1] * width, LANES), width)
    pooled_ref[...] = jnp.dot(
        pool_rows(2 * EDGE), mixed[:, own_columns], preferred_element_type=jnp.float32
    )
    loads[3].wait()
    row = lax.broadcasted_iota(jnp.int32, (2 * EDGE, LANES), 0)
    position = jnp.where(row < EDGE, starts[0] + row, starts[1] - EDGE + row)
    project_heads(normed[...], w_vmem, position, bounds, slice(None), q_ref, kv_ref)


def attend_kernel(count, rows, targets_ref, mid_q, edge_q, mid_mixed, edge_mixed, w_ref, *refs):
    kv_refs, out_refs = refs[: 2 * count], refs[2 * count : -6]
    queries, kv, mixed, pooled, w_vmem, w_sem = refs[-6:]
    frames = queries.shape[0]
    heads = queries.shape[1] // LANES
    width = mixed.shape[1]
    loads = [
        pltpu.make_async_copy(
            w_ref.at[h * HDE : (h + 1) * HDE], w_vmem.at[h * LANES : h * LANES + HDE], w_sem.at[h]
        )
        for h in range(heads)
    ]
    for load in loads:
        load.start()
    for h in range(heads):
        w_vmem[h * LANES + HDE : (h + 1) * LANES, :] = jnp.zeros(
            (LANES - HDE, w_vmem.shape[1]), jnp.bfloat16
        )
    for out, mid, edge, cut in (
        (queries, mid_q, edge_q, EDGE),
        (mixed, mid_mixed, edge_mixed, EDGE // STRIDE),
    ):
        out[:cut, :] = edge[:cut, :]
        out[cut : out.shape[0] - cut, :] = mid[...]
        out[out.shape[0] - cut :, :] = edge[cut:, :]
    at = 0
    for ref in kv_refs:
        kv[at : at + ref.shape[0], :] = ref[...]
        at += ref.shape[0]
    few = rows // STRIDE
    pool = pool_rows(rows)

    def step(i, carry):
        at = pl.ds(pl.multiple_of(i * rows, rows), rows)
        for h in range(heads):
            lanes = slice(h * LANES, (h + 1) * LANES)
            scores = lax.dot_general(
                queries[at, lanes],
                kv[:, lanes],
                (((1,), (1,)), ((), ())),
                preferred_element_type=jnp.float32,
            )
            peak = jnp.max(scores, axis=1, keepdims=True)
            weights = jnp.exp2(scores - peak).astype(jnp.bfloat16)
            values = kv[:, (heads + h) * LANES : (heads + h + 1) * LANES]
            out = jnp.dot(weights, values, preferred_element_type=jnp.float32)
            attended = (out * (1.0 / out[:, HDE : HDE + 1])).astype(jnp.bfloat16)
            pooled[pl.ds(pl.multiple_of(i * few, few), few), lanes] = jnp.dot(
                pool, attended, preferred_element_type=jnp.float32
            ).astype(jnp.bfloat16)
        return carry

    lax.fori_loop(0, frames // rows, step, 0)
    for load in loads:
        load.wait()
    for k, out_ref in enumerate(out_refs):
        columns = pl.ds(pl.multiple_of(targets_ref[k] * width, LANES), width)
        total = jnp.dot(pooled[...], w_vmem[:, columns], preferred_element_type=jnp.float32)
        if k == 0:
            total += mixed[...]
        out_ref[...] = total.astype(out_ref.dtype)


def project_kernel(targets_ref, *refs):
    *part_refs, w_ref, out_ref, squares_ref, pooled = refs
    width = part_refs[0].shape[1]
    for k, part_ref in enumerate(part_refs):
        at = pl.ds(pl.multiple_of(targets_ref[k] * width, LANES), width)
        pooled[:, at] = part_ref[...]
    total = jnp.dot(pooled[...], w_ref[...], preferred_element_type=jnp.float32)
    out_ref[...] = total
    rows = total.shape[0]
    squares = jnp.sum(total * total, axis=1, keepdims=True)
    squares_ref[...] = jnp.transpose(jnp.broadcast_to(squares, (rows, rows)))[:SUBLANES]


def route_kernel(cap, outs, firsts_ref, place_ref, rows_ref, *refs):
    square_refs, out_refs = refs[:-outs], refs[-outs:]
    rows = rows_ref.shape[0]
    devices = firsts_ref.shape[0] if len(out_refs) > 1 else out_refs[0].shape[0] // cap
    squares = square_refs[0][...]
    for ref in square_refs[1:]:
        squares += ref[...]
    scale = lax.rsqrt(squares[:1] / D + 1e-05)
    scale = jnp.transpose(jnp.broadcast_to(scale, (rows, rows)))[:, :1]
    normal_rows = (rows_ref[...] * scale).astype(jnp.bfloat16)
    destination = place_ref[...]
    named = lax.broadcasted_iota(jnp.int32, (devices, rows), 0) == destination
    earlier = lax.broadcasted_iota(jnp.int32, (rows, rows), 0) < lax.broadcasted_iota(
        jnp.int32, (rows, rows), 1
    )
    counts = jnp.dot(
        named.astype(jnp.float32).astype(jnp.bfloat16),
        earlier.astype(jnp.float32).astype(jnp.bfloat16),
        preferred_element_type=jnp.float32,
    )
    rank = jnp.sum(jnp.where(named, counts, 0.0), axis=0, keepdims=True).astype(jnp.int32)
    target = destination * cap + rank
    runs = firsts_ref.shape[0] // outs
    for k, out_ref in enumerate(out_refs):
        slots = out_ref.shape[0] // runs
        for run in range(runs):
            first = firsts_ref[k * runs + run]
            slot = first + lax.broadcasted_iota(jnp.int32, (slots, rows), 0)
            one_hot = (slot == target).astype(jnp.float32).astype(jnp.bfloat16)
            out_ref[run * slots : (run + 1) * slots, :] = jnp.dot(
                one_hot, normal_rows, preferred_element_type=jnp.float32
            ).astype(jnp.bfloat16)


def forward_kernel(*refs):
    *block_refs, out_ref = refs
    slots = block_refs[0].shape[0] // 2
    for k, block_ref in enumerate(block_refs):
        out_ref[k * slots : (k + 1) * slots, :] = block_ref[slots:, :]


def collect_kernel(firsts_ref, *refs):
    *block_refs, other_ref, out_ref = refs
    slots = block_refs[0].shape[0] // 2
    for k, block_ref in enumerate(block_refs):
        mine = pl.ds(pl.multiple_of(firsts_ref[2 * k], slots), slots)
        out_ref[mine, :] = block_ref[:slots, :]
        theirs = pl.ds(pl.multiple_of(firsts_ref[2 * k + 1], slots), slots)
        out_ref[theirs, :] = other_ref[k * slots : (k + 1) * slots, :]


def partner(index, k, devices):
    if devices & (devices - 1) == 0:
        return index ^ k
    return (index + k) % devices


def sender(index, k, devices):
    if devices & (devices - 1) == 0:
        return index ^ k
    return (index - k) % devices


def exchange(value, axes, k, devices):
    return lax.ppermute(value, axes, [(i, partner(i, k, devices)) for i in range(devices)])


def local(audio, lengths, conv_kernel, w_qkv, w_out, place, w_adapt):
    frame_count, channels = audio.shape
    seq_devices = lax.axis_size("tm")
    mp_devices = lax.axis_size("mp")
    recs = lengths.shape[1]
    group_frames = frame_count * seq_devices
    width = channels // mp_devices
    pooled_rows = frame_count // STRIDE
    heads = w_qkv.shape[2] // HDE
    where = jnp.concatenate(
        [jnp.stack([lax.axis_index("tm") * frame_count, lax.axis_index("mp")]), lengths[0]]
    )

    if seq_devices == 2:
        ends = jnp.concatenate([audio[:HALO], audio[frame_count - HALO :]], axis=0)
        halo = exchange(ends, "tm", 1, 2)
    else:
        up = [(i, i + 1) for i in range(seq_devices - 1)]
        down = [(j, i) for i, j in up]
        after = lax.ppermute(audio[:HALO], "tm", down)
        before = lax.ppermute(audio[frame_count - HALO :], "tm", up)
        halo = jnp.concatenate([after, before], axis=0)

    smem = pl.BlockSpec(memory_space=pltpu.SMEM)
    vmem = pl.BlockSpec(memory_space=pltpu.VMEM)
    hbm = pl.BlockSpec(memory_space=pltpu.HBM)
    w_three = jnp.transpose(w_qkv, (1, 0, 2))
    taps = conv_kernel.shape[0]

    def tiles(count, *lead):
        return pltpu.VMEM((*lead, count * SUBLANES, LANES), jnp.float32)

    def results(rows):
        return [
            jax.ShapeDtypeStruct((rows, heads * LANES), jnp.bfloat16),
            jax.ShapeDtypeStruct((rows, 2 * heads * LANES), jnp.bfloat16),
            jax.ShapeDtypeStruct((rows // STRIDE, width), jnp.float32),
        ]

    def shared(rows):
        return [
            pltpu.VMEM(conv_kernel.shape, jnp.float32),
            tiles(taps),
            tiles(taps),
            pltpu.VMEM((rows, channels), jnp.bfloat16),
            pltpu.VMEM((rows, channels), jnp.bfloat16),
            pltpu.VMEM(w_three.shape, jnp.bfloat16),
            pltpu.SMEM((recs,), jnp.int32),
            pltpu.SMEM((recs,), jnp.int32),
        ]

    mid = frame_count - 2 * EDGE
    mid_q, mid_kv, mid_mixed = pl.pallas_call(
        interior_kernel,
        out_shape=results(mid),
        in_specs=[smem, hbm, hbm, hbm],
        out_specs=[vmem] * 3,
        scratch_shapes=[
            pltpu.VMEM((mid + 2 * HALO, channels), jnp.bfloat16),
            tiles(mid + 2 * HALO),
            tiles(mid),
            tiles(mid // 2 + 2 * HALO),
            tiles(mid // 2),
            *shared(mid),
            *[pltpu.SemaphoreType.DMA] * 3,
        ],
        compiler_params=pltpu.CompilerParams(vmem_limit_bytes=53 * MIB),
        cost_estimate=pl.CostEstimate(
            flops=60 * mid * channels * w_qkv.shape[2], bytes_accessed=4 * MIB, transcendentals=0
        ),
        name="interior",
    )(where, conv_kernel, audio, w_three)
    edge_q, edge_kv, edge_mixed = pl.pallas_call(
        edge_kernel,
        out_shape=results(2 * EDGE),
        in_specs=[smem, hbm, hbm, vmem, hbm],
        out_specs=[vmem] * 3,
        scratch_shapes=[
            pltpu.VMEM((2 * (EDGE + HALO), channels), jnp.bfloat16),
            tiles(EDGE + 2 * HALO, 2),
            tiles(EDGE, 2),
            tiles(EDGE + 2 * HALO),
            tiles(EDGE),
            *shared(2 * EDGE),
            *[pltpu.SemaphoreType.DMA] * 4,
        ],
        compiler_params=pltpu.CompilerParams(vmem_limit_bytes=44 * MIB),
        cost_estimate=pl.CostEstimate(
            flops=240 * EDGE * channels * w_qkv.shape[2], bytes_accessed=4 * MIB, transcendentals=0
        ),
        name="edges",
    )(
        where,
        conv_kernel,
        audio,
        halo,
        w_three,
    )

    kv_blocks = [mid_kv, edge_kv]
    for k in range(1, seq_devices):
        kv_blocks += [exchange(block, "tm", k, seq_devices) for block in (mid_kv, edge_kv)]
    mp_index = lax.axis_index("mp")
    mp_targets = jnp.stack([partner(mp_index, k, mp_devices) for k in range(mp_devices)])
    mp_senders = jnp.stack([sender(mp_index, k, mp_devices) for k in range(mp_devices)])
    part = (pooled_rows, width)
    own_part, *parts = pl.pallas_call(
        functools.partial(attend_kernel, seq_devices, 256 if seq_devices <= 2 else 64),
        out_shape=[jax.ShapeDtypeStruct(part, jnp.float32)]
        + [jax.ShapeDtypeStruct(part, jnp.bfloat16)] * (mp_devices - 1),
        in_specs=[smem] + [vmem] * 4 + [hbm] + [vmem] * len(kv_blocks),
        out_specs=[vmem] * mp_devices,
        scratch_shapes=[
            pltpu.VMEM((frame_count, heads * LANES), jnp.bfloat16),
            pltpu.VMEM((group_frames, 2 * heads * LANES), jnp.bfloat16),
            pltpu.VMEM(part, jnp.float32),
            pltpu.VMEM((pooled_rows, heads * LANES), jnp.bfloat16),
            pltpu.VMEM((heads * LANES, channels), jnp.bfloat16),
            pltpu.SemaphoreType.DMA((heads,)),
        ],
        compiler_params=pltpu.CompilerParams(
            vmem_limit_bytes=44 * MIB
        ),
        name="attend",
    )(mp_targets, mid_q, edge_q, mid_mixed, edge_mixed, w_out, *kv_blocks)
    others = range(1, mp_devices)
    for k in others:
        own_part += exchange(parts[k - 1], "mp", k, mp_devices).astype(jnp.float32)
    own_part = own_part.astype(jnp.bfloat16)
    pooled = [own_part] + [exchange(own_part, "mp", k, mp_devices) for k in others]

    columns = w_adapt.shape[1]
    projected, squares = pl.pallas_call(
        project_kernel,
        out_shape=[
            jax.ShapeDtypeStruct((pooled_rows, columns), jnp.float32),
            jax.ShapeDtypeStruct((SUBLANES, pooled_rows), jnp.float32),
        ],
        in_specs=[smem] + [vmem] * (mp_devices + 1),
        out_specs=[vmem] * 2,
        scratch_shapes=[pltpu.VMEM((pooled_rows, channels), jnp.bfloat16)],
        compiler_params=pltpu.CompilerParams(vmem_limit_bytes=16 * MIB),
        name="project",
    )(mp_senders, *pooled, w_adapt)
    squares = [squares] + [exchange(squares, "mp", k, mp_devices) for k in others]

    axes = ("section", "tm")
    sections = lax.axis_size("section")
    device_count = sections * seq_devices
    cap = max(2, (2 * pooled_rows + device_count - 1) // device_count)
    section, core = lax.axis_index("section"), lax.axis_index("tm")
    direct = seq_devices == 2 and sections <= 4
    if direct:

        def slots_of(pairing):
            chosen = [pairing(section, k, sections) * 2 for k in range(sections)]
            return jnp.stack([(chip + c) * cap for chip in chosen for c in (core, 1 - core)])

        firsts = slots_of(partner)
        blocks = [jax.ShapeDtypeStruct((2 * cap, columns), jnp.bfloat16)] * sections
    else:
        firsts = jnp.zeros((1,), jnp.int32)
        blocks = [jax.ShapeDtypeStruct((device_count * cap, columns), jnp.bfloat16)]
    blocks = pl.pallas_call(
        functools.partial(route_kernel, cap, len(blocks)),
        out_shape=blocks,
        in_specs=[smem] + [vmem] * (mp_devices + 2),
        out_specs=[vmem] * len(blocks),
        compiler_params=pltpu.CompilerParams(vmem_limit_bytes=16 * MIB),
        name="route",
    )(firsts, place.T, projected, *squares)
    if not direct:
        return lax.all_to_all(blocks[0], axes, split_axis=0, concat_axis=0, tiled=True)
    arrived = [blocks[0]] + [
        exchange(blocks[k], "section", k, sections) for k in range(1, sections)
    ]
    passed = pl.pallas_call(
        forward_kernel,
        out_shape=jax.ShapeDtypeStruct((sections * cap, columns), jnp.bfloat16),
        in_specs=[vmem] * sections,
        out_specs=vmem,
        compiler_params=pltpu.CompilerParams(vmem_limit_bytes=8 * MIB),
        name="forward",
    )(*arrived)
    return pl.pallas_call(
        collect_kernel,
        out_shape=jax.ShapeDtypeStruct((device_count * cap, columns), jnp.bfloat16),
        in_specs=[smem] + [vmem] * (sections + 1),
        out_specs=vmem,
        compiler_params=pltpu.CompilerParams(vmem_limit_bytes=8 * MIB),
        name="collect",
    )(slots_of(sender), *arrived, exchange(passed, "tm", 1, 2))


def solution(mesh):
    placed = (
        P(("section", "tm"), None),
        P("section", None),
        P(),
        P(None, None, "mp"),
        P("mp", None),
        P(("section", "tm"), None),
        P(None, "mp"),
    )
    return jax.shard_map(
        local, mesh=mesh, in_specs=placed, out_specs=P(("section", "tm"), "mp"), check_vma=False
    )
```

```python
import functools
import math

import jax
import jax.numpy as jnp
from jax import lax
from jax.experimental import pallas as pl
from jax.experimental.pallas import tpu as pltpu
from jax.sharding import PartitionSpec as P

HDE = 96
D = 5120
STRIDE = 4
LANES = 128
SUBLANES = 8
HALO = 16
EDGE = 32
BLOCK = 16
GROUP = 16
MIB = 1 << 20
HIDDEN = -1e30


def conv_blocks(src, dst, taps, blocks, run, firsts, recs, bounds, starts_ref, ends_ref):
    count = taps.shape[0] // SUBLANES
    reach = count // 2
    span = BLOCK + count - 1
    shape = (SUBLANES, LANES)
    upper = lax.broadcasted_iota(jnp.int32, shape, 0) < SUBLANES // 2

    def both(values):
        if len(values) == 1:
            return jnp.full(shape, values[0], jnp.int32)
        return jnp.where(upper, values[0], values[1])

    def convolve(base, inside):
        def frame(k):
            at = (base + k + HALO - reach) * SUBLANES
            return src[pl.ds(pl.multiple_of(at, SUBLANES), SUBLANES), :]

        kernel = [taps[j * SUBLANES : (j + 1) * SUBLANES, :] for j in range(count)]
        totals = [None] * BLOCK
        for k in range(span):
            value = frame(k)
            if inside is not None:
                value = jnp.where(inside(k), value, 0.0)
            for t in range(max(0, k - count + 1), min(BLOCK, k + 1)):
                term = kernel[k - t] * value
                totals[t] = term if totals[t] is None else totals[t] + term
        for t in range(BLOCK):
            at = pl.ds(pl.multiple_of((base + t) * SUBLANES, SUBLANES), SUBLANES)
            half = 0.5 * totals[t]
            value = frame(t + reach) + half * (1.0 + jnp.tanh(half))
            if inside is not None:
                value = jnp.where(inside(t + reach), value, dst[at, :])
            dst[at, :] = value

    def touched(base, length):
        found = jnp.zeros((), jnp.bool_)
        for first in firsts:
            for bound in bounds[:-1]:
                at = bound - first - base
                found = found | ((at > -reach) & (at < length + reach))
        return found

    def masked(base):
        positions = [first + base for first in firsts]
        begin, extra = [], jnp.zeros((), jnp.int32)
        for position in positions:
            first = last = jnp.zeros((), jnp.int32)
            for bound in bounds[:-1]:
                first += (bound <= position).astype(jnp.int32)
                last += (bound <= position + BLOCK - 1).astype(jnp.int32)
            begin.append(first)
            extra = jnp.maximum(extra, last - first)

        def once(turn, carry):
            which = [jnp.minimum(first + turn, recs - 1) for first in begin]
            low = both([starts_ref[r] - p for r, p in zip(which, positions)])
            high = both([ends_ref[r] - p for r, p in zip(which, positions)])
            convolve(base, lambda k: (low <= k - reach) & (high > k - reach))
            return carry

        lax.fori_loop(0, extra + 1, once, 0)

    def blocks_of_run(i, carry):
        base = i * run * BLOCK
        any_touched = touched(base, run * BLOCK)

        @pl.when(jnp.logical_not(any_touched))
        def _():
            for j in range(run):
                convolve(base + j * BLOCK, None)

        @pl.when(any_touched)
        def _():
            def one(j, carry):
                here = base + j * BLOCK
                mine = touched(here, BLOCK)

                @pl.when(mine)
                def _():
                    masked(here)

                @pl.when(jnp.logical_not(mine))
                def _():
                    convolve(here, None)

                return carry

            lax.fori_loop(0, run, one, 0)

        return carry

    lax.fori_loop(0, blocks // run, blocks_of_run, 0)


def shuffle(back):
    row = lax.broadcasted_iota(jnp.int32, (LANES, LANES), 1 if back else 0)
    column = lax.broadcasted_iota(jnp.int32, (LANES, LANES), 0 if back else 1)
    moved = (row // SUBLANES == column % GROUP) & (row % SUBLANES == column // GROUP)
    return moved.astype(jnp.float32).astype(jnp.bfloat16)


def to_tiles(matrix, values, ref, frame):
    stack = jnp.concatenate(values, axis=0)
    at = pl.ds(frame * SUBLANES, GROUP * SUBLANES)
    ref[at, :] = jnp.dot(matrix, stack, preferred_element_type=jnp.float32)


def from_tiles(matrix, ref, frame):
    rows = GROUP * SUBLANES
    low = ref[frame * SUBLANES : frame * SUBLANES + rows, :].astype(jnp.bfloat16)
    moved = jnp.dot(matrix, low, preferred_element_type=jnp.float32)
    return [moved[k * GROUP : (k + 1) * GROUP] for k in range(SUBLANES)]


def blocks_of(value, first, count):
    return [value[:, k * LANES : (k + 1) * LANES] for k in range(first, first + count)]


def recording_bounds(where_ref, starts_ref, ends_ref):
    bounds, total = [], jnp.zeros((), jnp.int32)
    for r in range(where_ref.shape[0] - 2):
        starts_ref[r] = total
        total = total + where_ref[2 + r]
        ends_ref[r] = total
        bounds.append(total)
    return bounds


def spread_taps(taps_ref, full_taps, half_taps):
    count = taps_ref.shape[0]
    blocks = taps_ref.shape[1] // LANES
    for k in range(blocks):
        value = taps_ref[:, k * LANES : (k + 1) * LANES]
        if k < SUBLANES:
            full_taps[pl.ds(k, count, stride=SUBLANES), :] = value
        else:
            for half in range(2):
                at = k - SUBLANES + half * SUBLANES // 2
                half_taps[pl.ds(at, count, stride=SUBLANES), :] = value


def normalise(blocks, mixed, normed, at):
    values = jnp.concatenate(blocks, axis=1)
    mixed[at, :] = values.astype(jnp.bfloat16)
    centred = values - jnp.mean(values, -1, keepdims=True)
    variance = jnp.mean(centred * centred, -1, keepdims=True)
    normed[at, :] = (centred * lax.rsqrt(variance + 1e-05)).astype(jnp.bfloat16)


def pool_rows(rows):
    few = rows // STRIDE
    chosen = (
        lax.broadcasted_iota(jnp.int32, (few, rows), 1) // STRIDE
        == lax.broadcasted_iota(jnp.int32, (few, rows), 0)
    )
    return (chosen.astype(jnp.float32) * (1.0 / STRIDE)).astype(jnp.bfloat16)


def project_heads(normed_rows, w_vmem, position, bounds, at, q_ref, kv_ref):
    recs = len(bounds)
    heads = w_vmem.shape[2] // HDE
    lane = lax.broadcasted_iota(jnp.int32, position.shape, 1)
    mine = jnp.zeros(position.shape, jnp.int32)
    for bound in bounds:
        mine += (position >= bound).astype(jnp.int32)
    same = lane - HDE == mine
    extra_q = jnp.where(same | (lane >= HDE + recs), 0.0, HIDDEN)
    extra_k = jnp.where(same, 1.0, 0.0)
    extra_v = jnp.where(lane == HDE, 1.0, 0.0)
    score_scale = HDE ** (-0.5) * math.log2(math.e)
    for kind, extra in enumerate((extra_q, extra_k, extra_v)):
        result = jnp.dot(normed_rows, w_vmem[kind], preferred_element_type=jnp.float32)
        if kind == 0:
            result = result * score_scale
        for h in range(heads):
            tile, start = divmod(h * HDE, LANES)
            tiles = 1 if start + HDE <= LANES else 2
            head = result[:, tile * LANES : (tile + tiles) * LANES]
            if start:
                head = pltpu.roll(head, tiles * LANES - start, 1)
            head = jnp.where(lane < HDE, head[:, :LANES], extra).astype(jnp.bfloat16)
            if kind == 0:
                q_ref[at, h * LANES : (h + 1) * LANES] = head
            else:
                first = ((kind - 1) * heads + h) * LANES
                kv_ref[at, first : first + LANES] = head


def interior_kernel(
    where_ref,
    taps_hbm,
    audio_ref,
    w_ref,
    q_ref,
    kv_ref,
    pooled_ref,
    audio,
    full_src,
    full_dst,
    half_src,
    half_dst,
    taps_ref,
    full_taps,
    half_taps,
    mixed,
    normed,
    w_vmem,
    starts_ref,
    ends_ref,
    audio_sem,
    taps_sem,
    w_sem,
):
    rows = q_ref.shape[0]
    inner = rows + 2 * HALO
    skip = EDGE - HALO
    half = rows // 2
    load_audio = pltpu.make_async_copy(audio_ref.at[skip : skip + inner], audio, audio_sem)
    load_taps = pltpu.make_async_copy(taps_hbm, taps_ref, taps_sem)
    load_audio.start()
    load_taps.start()
    load_w = pltpu.make_async_copy(w_ref, w_vmem, w_sem)
    load_w.start()
    bounds = recording_bounds(where_ref, starts_ref, ends_ref)
    start = where_ref[0] + EDGE
    forward, back = shuffle(False), shuffle(True)
    load_audio.wait()
    side = SUBLANES // 2
    for row in range(0, inner, GROUP):
        value = audio[row : row + GROUP, : SUBLANES * LANES]
        to_tiles(forward, blocks_of(value, 0, SUBLANES), full_src, row)
    for row in range(0, half + 2 * HALO, GROUP):
        pair = [
            block
            for at in (row, row + half)
            for block in blocks_of(audio[at : at + GROUP, :], SUBLANES, side)
        ]
        to_tiles(forward, pair, half_src, row)
    load_taps.wait()
    spread_taps(taps_ref, full_taps, half_taps)
    recs = len(bounds)
    common = (recs, bounds, starts_ref, ends_ref)
    conv_blocks(full_src, full_dst, full_taps, rows // BLOCK, 4, [start], *common)
    conv_blocks(half_src, half_dst, half_taps, half // BLOCK, 2, [start, start + half], *common)


    for row in range(0, half, GROUP):
        pair = from_tiles(back, half_dst, row)
        for which in range(2):
            at = which * half + row
            blocks = from_tiles(back, full_dst, at) + pair[which * side : (which + 1) * side]
            normalise(blocks, mixed, normed, slice(at, at + GROUP))

    width = pooled_ref.shape[1]
    own_columns = pl.ds(pl.multiple_of(where_ref[1] * width, LANES), width)
    pooled_ref[...] = jnp.dot(
        pool_rows(rows), mixed[:, own_columns], preferred_element_type=jnp.float32
    )
    load_w.wait()
    for which in range(2):
        at = slice(which * half, (which + 1) * half)
        position = start + which * half + lax.broadcasted_iota(jnp.int32, (half, LANES), 0)
        project_heads(normed[at, :], w_vmem, position, bounds, at, q_ref, kv_ref)


def edge_kernel(
    where_ref,
    taps_hbm,
    audio_ref,
    halo_ref,
    w_ref,
    q_ref,
    kv_ref,
    pooled_ref,
    audio,
    full_src,
    full_dst,
    half_src,
    half_dst,
    taps_ref,
    full_taps,
    half_taps,
    mixed,
    normed,
    w_vmem,
    starts_ref,
    ends_ref,
    first_sem,
    last_sem,
    taps_sem,
    w_sem,
):
    frames = audio_ref.shape[0]
    known = EDGE + HALO
    loads = [
        pltpu.make_async_copy(audio_ref.at[:known], audio.at[:known], first_sem),
        pltpu.make_async_copy(audio_ref.at[frames - known :], audio.at[known:], last_sem),
        pltpu.make_async_copy(taps_hbm, taps_ref, taps_sem),
        pltpu.make_async_copy(w_ref, w_vmem, w_sem),
    ]
    for load in loads:
        load.start()
    bounds = recording_bounds(where_ref, starts_ref, ends_ref)
    forward, back = shuffle(False), shuffle(True)
    starts = [where_ref[0], where_ref[0] + frames - EDGE]
    length = EDGE + 2 * HALO
    has_before = (starts[0] > 0).astype(jnp.float32)
    has_after = (starts[0] + frames < bounds[-1]).astype(jnp.float32)
    before = (halo_ref[HALO:, :].astype(jnp.float32) * has_before).astype(jnp.bfloat16)
    after = (halo_ref[:HALO, :].astype(jnp.float32) * has_after).astype(jnp.bfloat16)
    for load in loads[:3]:
        load.wait()
    side = SUBLANES // 2
    for row in range(0, length, GROUP):
        first = before if row == 0 else audio[row - HALO : row - HALO + GROUP, :]
        last = after if row == known else audio[known + row : known + row + GROUP, :]
        for which, value in enumerate((first, last)):
            to_tiles(forward, blocks_of(value, 0, SUBLANES), full_src.at[which], row)
        pair = blocks_of(first, SUBLANES, side) + blocks_of(last, SUBLANES, side)
        to_tiles(forward, pair, half_src, row)
    spread_taps(taps_ref, full_taps, half_taps)
    recs = len(bounds)
    common = (recs, bounds, starts_ref, ends_ref)
    for which in range(2):
        conv_blocks(
            full_src.at[which],
            full_dst.at[which],
            full_taps,
            EDGE // BLOCK,
            2,
            [starts[which]],
            *common,
        )
    conv_blocks(half_src, half_dst, half_taps, EDGE // BLOCK, 2, starts, *common)
    for row in range(0, EDGE, GROUP):
        pair = from_tiles(back, half_dst, row)
        for which in range(2):
            blocks = from_tiles(back, full_dst.at[which], row)
            blocks += pair[which * side : (which + 1) * side]
            at = which * EDGE + row
            normalise(blocks, mixed, normed, slice(at, at + GROUP))
    width = pooled_ref.shape[1]
    own_columns = pl.ds(pl.multiple_of(where_ref[1] * width, LANES), width)
    pooled_ref[...] = jnp.dot(
        pool_rows(2 * EDGE), mixed[:, own_columns], preferred_element_type=jnp.float32
    )
    loads[3].wait()
    row = lax.broadcasted_iota(jnp.int32, (2 * EDGE, LANES), 0)
    position = jnp.where(row < EDGE, starts[0] + row, starts[1] - EDGE + row)
    project_heads(normed[...], w_vmem, position, bounds, slice(None), q_ref, kv_ref)


def attend_kernel(count, rows, targets_ref, mid_q, edge_q, mid_mixed, edge_mixed, w_ref, *refs):
    kv_refs, out_refs = refs[: 2 * count], refs[2 * count : -7]
    queries, kv, mixed, pooled, w_vmem, w_sem, mixed_sem = refs[-7:]
    frames = queries.shape[0]
    heads = queries.shape[1] // LANES
    width = mixed.shape[1]
    loads = [
        pltpu.make_async_copy(
            w_ref.at[h * HDE : (h + 1) * HDE], w_vmem.at[h * LANES : h * LANES + HDE], w_sem.at[h]
        )
        for h in range(heads)
    ]
    cut = EDGE // STRIDE
    last = mixed.shape[0] - cut
    for i, (source, target) in enumerate(
        (
            (edge_mixed.at[:cut], mixed.at[:cut]),
            (mid_mixed, mixed.at[cut:last]),
            (edge_mixed.at[cut:], mixed.at[last:]),
        )
    ):
        loads.append(pltpu.make_async_copy(source, target, mixed_sem.at[i]))
    for load in loads:
        load.start()
    for h in range(heads):
        w_vmem[h * LANES + HDE : (h + 1) * LANES, :] = jnp.zeros(
            (LANES - HDE, w_vmem.shape[1]), jnp.bfloat16
        )
    queries[:EDGE, :] = edge_q[:EDGE, :]
    queries[EDGE : frames - EDGE, :] = mid_q[...]
    queries[frames - EDGE :, :] = edge_q[EDGE:, :]
    at = 0
    for ref in kv_refs:
        kv[at : at + ref.shape[0], :] = ref[...]
        at += ref.shape[0]
    few = rows // STRIDE
    pool = pool_rows(rows)

    def step(i, carry):
        at = pl.ds(i * rows if isinstance(i, int) else pl.multiple_of(i * rows, rows), rows)
        few_at = pl.ds(i * few if isinstance(i, int) else pl.multiple_of(i * few, few), few)
        for h in range(heads):
            lanes = slice(h * LANES, (h + 1) * LANES)
            scores = lax.dot_general(
                queries[at, lanes],
                kv[:, lanes],
                (((1,), (1,)), ((), ())),
                preferred_element_type=jnp.float32,
            )
            peak = jnp.max(scores, axis=1, keepdims=True)
            weights = jnp.exp2(scores - peak).astype(jnp.bfloat16)
            values = kv[:, (heads + h) * LANES : (heads + h + 1) * LANES]
            out = jnp.dot(weights, values, preferred_element_type=jnp.float32)
            attended = (out * (1.0 / out[:, HDE : HDE + 1])).astype(jnp.bfloat16)
            pooled[few_at, lanes] = jnp.dot(
                pool, attended, preferred_element_type=jnp.float32
            ).astype(jnp.bfloat16)
        return carry

    if frames // rows <= 2:
        for i in range(frames // rows):
            step(i, 0)
    else:
        lax.fori_loop(0, frames // rows, step, 0)
    for load in loads:
        load.wait()
    for k, out_ref in enumerate(out_refs):
        columns = pl.ds(pl.multiple_of(targets_ref[k] * width, LANES), width)
        total = jnp.dot(pooled[...], w_vmem[:, columns], preferred_element_type=jnp.float32)
        if k == 0:
            total += mixed[...]
        out_ref[...] = total.astype(out_ref.dtype)


def project_kernel(targets_ref, *refs):
    *part_refs, w_ref, out_ref, squares_ref, pooled = refs
    width = part_refs[0].shape[1]
    for k, part_ref in enumerate(part_refs):
        at = pl.ds(pl.multiple_of(targets_ref[k] * width, LANES), width)
        pooled[:, at] = part_ref[...]
    total = jnp.dot(pooled[...], w_ref[...], preferred_element_type=jnp.float32)
    out_ref[...] = total
    rows = total.shape[0]
    squares = jnp.sum(total * total, axis=1, keepdims=True)
    squares_ref[...] = jnp.transpose(jnp.broadcast_to(squares, (rows, rows)))[:SUBLANES]


def route_kernel(cap, outs, firsts_ref, place_ref, rows_ref, *refs):
    square_refs, out_refs = refs[:-outs], refs[-outs:]
    rows = rows_ref.shape[0]
    devices = firsts_ref.shape[0] if len(out_refs) > 1 else out_refs[0].shape[0] // cap
    squares = square_refs[0][...]
    for ref in square_refs[1:]:
        squares += ref[...]
    scale = lax.rsqrt(squares[:1] / D + 1e-05)
    scale = jnp.transpose(jnp.broadcast_to(scale, (rows, rows)))[:, :1]
    normal_rows = (rows_ref[...] * scale).astype(jnp.bfloat16)
    destination = place_ref[...]
    named = lax.broadcasted_iota(jnp.int32, (devices, rows), 0) == destination
    earlier = lax.broadcasted_iota(jnp.int32, (rows, rows), 0) < lax.broadcasted_iota(
        jnp.int32, (rows, rows), 1
    )
    counts = jnp.dot(
        named.astype(jnp.float32).astype(jnp.bfloat16),
        earlier.astype(jnp.float32).astype(jnp.bfloat16),
        preferred_element_type=jnp.float32,
    )
    rank = jnp.sum(jnp.where(named, counts, 0.0), axis=0, keepdims=True).astype(jnp.int32)
    target = destination * cap + rank
    runs = firsts_ref.shape[0] // outs
    for k, out_ref in enumerate(out_refs):
        slots = out_ref.shape[0] // runs
        for run in range(runs):
            first = firsts_ref[k * runs + run]
            slot = first + lax.broadcasted_iota(jnp.int32, (slots, rows), 0)
            one_hot = (slot == target).astype(jnp.float32).astype(jnp.bfloat16)
            out_ref[run * slots : (run + 1) * slots, :] = jnp.dot(
                one_hot, normal_rows, preferred_element_type=jnp.float32
            ).astype(jnp.bfloat16)


def forward_kernel(*refs):
    *block_refs, out_ref = refs
    slots = block_refs[0].shape[0] // 2
    for k, block_ref in enumerate(block_refs):
        out_ref[k * slots : (k + 1) * slots, :] = block_ref[slots:, :]


def collect_kernel(firsts_ref, *refs):
    *block_refs, other_ref, out_ref = refs
    slots = block_refs[0].shape[0] // 2
    for k, block_ref in enumerate(block_refs):
        mine = pl.ds(pl.multiple_of(firsts_ref[2 * k], slots), slots)
        out_ref[mine, :] = block_ref[:slots, :]
        theirs = pl.ds(pl.multiple_of(firsts_ref[2 * k + 1], slots), slots)
        out_ref[theirs, :] = other_ref[k * slots : (k + 1) * slots, :]


def partner(index, k, devices):
    if devices & (devices - 1) == 0:
        return index ^ k
    return (index + k) % devices


def sender(index, k, devices):
    if devices & (devices - 1) == 0:
        return index ^ k
    return (index - k) % devices


def exchange(value, axes, k, devices):
    return lax.ppermute(value, axes, [(i, partner(i, k, devices)) for i in range(devices)])


def local(audio, lengths, conv_kernel, w_qkv, w_out, place, w_adapt):
    frame_count, channels = audio.shape
    seq_devices = lax.axis_size("tm")
    mp_devices = lax.axis_size("mp")
    recs = lengths.shape[1]
    group_frames = frame_count * seq_devices
    width = channels // mp_devices
    pooled_rows = frame_count // STRIDE
    heads = w_qkv.shape[2] // HDE
    where = jnp.concatenate(
        [jnp.stack([lax.axis_index("tm") * frame_count, lax.axis_index("mp")]), lengths[0]]
    )

    if seq_devices == 2:
        ends = jnp.concatenate([audio[:HALO], audio[frame_count - HALO :]], axis=0)
        halo = exchange(ends, "tm", 1, 2)
    else:
        up = [(i, i + 1) for i in range(seq_devices - 1)]
        down = [(j, i) for i, j in up]
        after = lax.ppermute(audio[:HALO], "tm", down)
        before = lax.ppermute(audio[frame_count - HALO :], "tm", up)
        halo = jnp.concatenate([after, before], axis=0)

    smem = pl.BlockSpec(memory_space=pltpu.SMEM)
    vmem = pl.BlockSpec(memory_space=pltpu.VMEM)
    hbm = pl.BlockSpec(memory_space=pltpu.HBM)
    w_three = jnp.transpose(w_qkv, (1, 0, 2))
    taps = conv_kernel.shape[0]

    def tiles(count, *lead):
        return pltpu.VMEM((*lead, count * SUBLANES, LANES), jnp.float32)

    def results(rows):
        return [
            jax.ShapeDtypeStruct((rows, heads * LANES), jnp.bfloat16),
            jax.ShapeDtypeStruct((rows, 2 * heads * LANES), jnp.bfloat16),
            jax.ShapeDtypeStruct((rows // STRIDE, width), jnp.float32),
        ]

    def shared(rows):
        return [
            pltpu.VMEM(conv_kernel.shape, jnp.float32),
            tiles(taps),
            tiles(taps),
            pltpu.VMEM((rows, channels), jnp.bfloat16),
            pltpu.VMEM((rows, channels), jnp.bfloat16),
            pltpu.VMEM(w_three.shape, jnp.bfloat16),
            pltpu.SMEM((recs,), jnp.int32),
            pltpu.SMEM((recs,), jnp.int32),
        ]

    mid = frame_count - 2 * EDGE
    mid_q, mid_kv, mid_mixed = pl.pallas_call(
        interior_kernel,
        out_shape=results(mid),
        in_specs=[smem, hbm, hbm, hbm],
        out_specs=[vmem] * 3,
        scratch_shapes=[
            pltpu.VMEM((mid + 2 * HALO, channels), jnp.bfloat16),
            tiles(mid + 2 * HALO),
            tiles(mid),
            tiles(mid // 2 + 2 * HALO),
            tiles(mid // 2),
            *shared(mid),
            *[pltpu.SemaphoreType.DMA] * 3,
        ],
        compiler_params=pltpu.CompilerParams(vmem_limit_bytes=53 * MIB),
        cost_estimate=pl.CostEstimate(
            flops=60 * mid * channels * w_qkv.shape[2], bytes_accessed=4 * MIB, transcendentals=0
        ),
        name="interior",
    )(where, conv_kernel, audio, w_three)
    edge_q, edge_kv, edge_mixed = pl.pallas_call(
        edge_kernel,
        out_shape=results(2 * EDGE),
        in_specs=[smem, hbm, hbm, vmem, hbm],
        out_specs=[vmem] * 3,
        scratch_shapes=[
            pltpu.VMEM((2 * (EDGE + HALO), channels), jnp.bfloat16),
            tiles(EDGE + 2 * HALO, 2),
            tiles(EDGE, 2),
            tiles(EDGE + 2 * HALO),
            tiles(EDGE),
            *shared(2 * EDGE),
            *[pltpu.SemaphoreType.DMA] * 4,
        ],
        compiler_params=pltpu.CompilerParams(vmem_limit_bytes=44 * MIB),
        cost_estimate=pl.CostEstimate(
            flops=240 * EDGE * channels * w_qkv.shape[2], bytes_accessed=4 * MIB, transcendentals=0
        ),
        name="edges",
    )(
        where,
        conv_kernel,
        audio,
        halo,
        w_three,
    )

    kv_blocks = [mid_kv, edge_kv]
    for k in range(1, seq_devices):
        kv_blocks += [exchange(block, "tm", k, seq_devices) for block in (mid_kv, edge_kv)]
    mp_index = lax.axis_index("mp")
    mp_targets = jnp.stack([partner(mp_index, k, mp_devices) for k in range(mp_devices)])
    mp_senders = jnp.stack([sender(mp_index, k, mp_devices) for k in range(mp_devices)])
    part = (pooled_rows, width)
    own_part, *parts = pl.pallas_call(
        functools.partial(attend_kernel, seq_devices, 256 if seq_devices <= 2 else 64),
        out_shape=[jax.ShapeDtypeStruct(part, jnp.float32)]
        + [jax.ShapeDtypeStruct(part, jnp.bfloat16)] * (mp_devices - 1),
        in_specs=[smem, vmem, vmem, hbm, hbm, hbm] + [vmem] * len(kv_blocks),
        out_specs=[vmem] * mp_devices,
        scratch_shapes=[
            pltpu.VMEM((frame_count, heads * LANES), jnp.bfloat16),
            pltpu.VMEM((group_frames, 2 * heads * LANES), jnp.bfloat16),
            pltpu.VMEM(part, jnp.float32),
            pltpu.VMEM((pooled_rows, heads * LANES), jnp.bfloat16),
            pltpu.VMEM((heads * LANES, channels), jnp.bfloat16),
            pltpu.SemaphoreType.DMA((heads,)),
            pltpu.SemaphoreType.DMA((3,)),
        ],
        compiler_params=pltpu.CompilerParams(
            vmem_limit_bytes=44 * MIB
        ),
        name="attend",
    )(mp_targets, mid_q, edge_q, mid_mixed, edge_mixed, w_out, *kv_blocks)
    others = range(1, mp_devices)
    for k in others:
        own_part += exchange(parts[k - 1], "mp", k, mp_devices).astype(jnp.float32)
    own_part = own_part.astype(jnp.bfloat16)
    pooled = [own_part] + [exchange(own_part, "mp", k, mp_devices) for k in others]

    columns = w_adapt.shape[1]
    projected, squares = pl.pallas_call(
        project_kernel,
        out_shape=[
            jax.ShapeDtypeStruct((pooled_rows, columns), jnp.float32),
            jax.ShapeDtypeStruct((SUBLANES, pooled_rows), jnp.float32),
        ],
        in_specs=[smem] + [vmem] * (mp_devices + 1),
        out_specs=[vmem] * 2,
        scratch_shapes=[pltpu.VMEM((pooled_rows, channels), jnp.bfloat16)],
        compiler_params=pltpu.CompilerParams(vmem_limit_bytes=16 * MIB),
        name="project",
    )(mp_senders, *pooled, w_adapt)
    if mp_devices & (mp_devices - 1) == 0:
        for bit in range(mp_devices.bit_length() - 1):
            squares = squares + exchange(squares, "mp", 1 << bit, mp_devices)
        squares = [squares]
    else:
        squares = [squares] + [exchange(squares, "mp", k, mp_devices) for k in others]

    axes = ("section", "tm")
    sections = lax.axis_size("section")
    device_count = sections * seq_devices
    cap = max(2, (2 * pooled_rows + device_count - 1) // device_count)
    section, core = lax.axis_index("section"), lax.axis_index("tm")
    direct = seq_devices == 2 and sections <= 4
    if direct:

        def slots_of(pairing):
            chosen = [pairing(section, k, sections) * 2 for k in range(sections)]
            return jnp.stack([(chip + c) * cap for chip in chosen for c in (core, 1 - core)])

        firsts = slots_of(partner)
        blocks = [jax.ShapeDtypeStruct((2 * cap, columns), jnp.bfloat16)] * sections
    else:
        firsts = jnp.zeros((1,), jnp.int32)
        blocks = [jax.ShapeDtypeStruct((device_count * cap, columns), jnp.bfloat16)]
    blocks = pl.pallas_call(
        functools.partial(route_kernel, cap, len(blocks)),
        out_shape=blocks,
        in_specs=[smem] + [vmem] * (len(squares) + 2),
        out_specs=[vmem] * len(blocks),
        compiler_params=pltpu.CompilerParams(vmem_limit_bytes=16 * MIB),
        name="route",
    )(firsts, place.T, projected, *squares)
    if not direct:
        return lax.all_to_all(blocks[0], axes, split_axis=0, concat_axis=0, tiled=True)
    arrived = [blocks[0]] + [
        exchange(blocks[k], "section", k, sections) for k in range(1, sections)
    ]
    passed = pl.pallas_call(
        forward_kernel,
        out_shape=jax.ShapeDtypeStruct((sections * cap, columns), jnp.bfloat16),
        in_specs=[vmem] * sections,
        out_specs=vmem,
        compiler_params=pltpu.CompilerParams(vmem_limit_bytes=8 * MIB),
        name="forward",
    )(*arrived)
    return pl.pallas_call(
        collect_kernel,
        out_shape=jax.ShapeDtypeStruct((device_count * cap, columns), jnp.bfloat16),
        in_specs=[smem] + [vmem] * (sections + 1),
        out_specs=vmem,
        compiler_params=pltpu.CompilerParams(vmem_limit_bytes=8 * MIB),
        name="collect",
    )(slots_of(sender), *arrived, exchange(passed, "tm", 1, 2))


def solution(mesh):
    placed = (
        P(("section", "tm"), None),
        P("section", None),
        P(),
        P(None, None, "mp"),
        P("mp", None),
        P(("section", "tm"), None),
        P(None, "mp"),
    )
    return jax.shard_map(
        local, mesh=mesh, in_specs=placed, out_specs=P(("section", "tm"), "mp"), check_vma=False
    )
```

```python
import functools
import math

import jax
import jax.numpy as jnp
from jax import lax
from jax.experimental import pallas as pl
from jax.experimental.pallas import tpu as pltpu
from jax.sharding import PartitionSpec as P

HDE = 96
D = 5120
STRIDE = 4
LANES = 128
SUBLANES = 8
HALO = 16
EDGE = 32
BLOCK = 16
GROUP = 16
MIB = 1 << 20
HIDDEN = -1e30


def conv_blocks(src, dst, taps, blocks, run, firsts, recs, bounds, starts_ref, ends_ref):
    count = taps.shape[0] // SUBLANES
    reach = count // 2
    span = BLOCK + count - 1
    shape = (SUBLANES, LANES)
    upper = lax.broadcasted_iota(jnp.int32, shape, 0) < SUBLANES // 2

    def both(values):
        if len(values) == 1:
            return jnp.full(shape, values[0], jnp.int32)
        return jnp.where(upper, values[0], values[1])

    def convolve(base, inside):
        def frame(k):
            at = (base + k + HALO - reach) * SUBLANES
            return src[pl.ds(pl.multiple_of(at, SUBLANES), SUBLANES), :]

        kernel = [taps[j * SUBLANES : (j + 1) * SUBLANES, :] for j in range(count)]
        totals = [None] * BLOCK
        for k in range(span):
            value = frame(k)
            if inside is not None:
                value = jnp.where(inside(k), value, 0.0)
            for t in range(max(0, k - count + 1), min(BLOCK, k + 1)):
                term = kernel[k - t] * value
                totals[t] = term if totals[t] is None else totals[t] + term
        for t in range(BLOCK):
            at = pl.ds(pl.multiple_of((base + t) * SUBLANES, SUBLANES), SUBLANES)
            half = 0.5 * totals[t]
            value = frame(t + reach) + half * (1.0 + jnp.tanh(half))
            if inside is not None:
                value = jnp.where(inside(t + reach), value, dst[at, :])
            dst[at, :] = value

    def touched(base, length):
        found = jnp.zeros((), jnp.bool_)
        for first in firsts:
            for bound in bounds[:-1]:
                at = bound - first - base
                found = found | ((at > -reach) & (at < length + reach))
        return found

    def masked(base):
        positions = [first + base for first in firsts]
        begin, extra = [], jnp.zeros((), jnp.int32)
        for position in positions:
            first = last = jnp.zeros((), jnp.int32)
            for bound in bounds[:-1]:
                first += (bound <= position).astype(jnp.int32)
                last += (bound <= position + BLOCK - 1).astype(jnp.int32)
            begin.append(first)
            extra = jnp.maximum(extra, last - first)

        def once(turn, carry):
            which = [jnp.minimum(first + turn, recs - 1) for first in begin]
            low = both([starts_ref[r] - p for r, p in zip(which, positions)])
            high = both([ends_ref[r] - p for r, p in zip(which, positions)])
            convolve(base, lambda k: (low <= k - reach) & (high > k - reach))
            return carry

        lax.fori_loop(0, extra + 1, once, 0)

    def blocks_of_run(i, carry):
        base = i * run * BLOCK
        any_touched = touched(base, run * BLOCK)

        @pl.when(jnp.logical_not(any_touched))
        def _():
            for j in range(run):
                convolve(base + j * BLOCK, None)

        @pl.when(any_touched)
        def _():
            def one(j, carry):
                here = base + j * BLOCK
                mine = touched(here, BLOCK)

                @pl.when(mine)
                def _():
                    masked(here)

                @pl.when(jnp.logical_not(mine))
                def _():
                    convolve(here, None)

                return carry

            lax.fori_loop(0, run, one, 0)

        return carry

    lax.fori_loop(0, blocks // run, blocks_of_run, 0)


def shuffle(back):
    row = lax.broadcasted_iota(jnp.int32, (LANES, LANES), 1 if back else 0)
    column = lax.broadcasted_iota(jnp.int32, (LANES, LANES), 0 if back else 1)
    moved = (row // SUBLANES == column % GROUP) & (row % SUBLANES == column // GROUP)
    return moved.astype(jnp.float32).astype(jnp.bfloat16)


def to_tiles(matrix, values, ref, frame):
    stack = jnp.concatenate(values, axis=0)
    at = pl.ds(frame * SUBLANES, GROUP * SUBLANES)
    ref[at, :] = jnp.dot(matrix, stack, preferred_element_type=jnp.float32)


def from_tiles(matrix, ref, frame):
    rows = GROUP * SUBLANES
    low = ref[frame * SUBLANES : frame * SUBLANES + rows, :].astype(jnp.bfloat16)
    moved = jnp.dot(matrix, low, preferred_element_type=jnp.float32)
    return [moved[k * GROUP : (k + 1) * GROUP] for k in range(SUBLANES)]


def blocks_of(value, first, count):
    return [value[:, k * LANES : (k + 1) * LANES] for k in range(first, first + count)]


def recording_bounds(where_ref, starts_ref, ends_ref):
    bounds, total = [], jnp.zeros((), jnp.int32)
    for r in range(where_ref.shape[0] - 2):
        starts_ref[r] = total
        total = total + where_ref[2 + r]
        ends_ref[r] = total
        bounds.append(total)
    return bounds


def spread_taps(taps_ref, full_taps, half_taps):
    count = taps_ref.shape[0]
    blocks = taps_ref.shape[1] // LANES
    for k in range(blocks):
        value = taps_ref[:, k * LANES : (k + 1) * LANES]
        if k < SUBLANES:
            full_taps[pl.ds(k, count, stride=SUBLANES), :] = value
        else:
            for half in range(2):
                at = k - SUBLANES + half * SUBLANES // 2
                half_taps[pl.ds(at, count, stride=SUBLANES), :] = value


def normalise(blocks, mixed, normed, at):
    values = jnp.concatenate(blocks, axis=1)
    mixed[at, :] = values.astype(jnp.bfloat16)
    centred = values - jnp.mean(values, -1, keepdims=True)
    variance = jnp.mean(centred * centred, -1, keepdims=True)
    normed[at, :] = (centred * lax.rsqrt(variance + 1e-05)).astype(jnp.bfloat16)


def pool_rows(rows):
    few = rows // STRIDE
    chosen = (
        lax.broadcasted_iota(jnp.int32, (few, rows), 1) // STRIDE
        == lax.broadcasted_iota(jnp.int32, (few, rows), 0)
    )
    return (chosen.astype(jnp.float32) * (1.0 / STRIDE)).astype(jnp.bfloat16)


def project_heads(normed_rows, w_vmem, position, bounds, at, q_ref, kv_ref):
    recs = len(bounds)
    heads = w_vmem.shape[2] // HDE
    lane = lax.broadcasted_iota(jnp.int32, position.shape, 1)
    mine = jnp.zeros(position.shape, jnp.int32)
    for bound in bounds:
        mine += (position >= bound).astype(jnp.int32)
    same = lane - HDE == mine
    extra_q = jnp.where(same | (lane >= HDE + recs), 0.0, HIDDEN)
    extra_k = jnp.where(same, 1.0, 0.0)
    extra_v = jnp.where(lane == HDE, 1.0, 0.0)
    score_scale = HDE ** (-0.5) * math.log2(math.e)
    for kind, extra in enumerate((extra_q, extra_k, extra_v)):
        result = jnp.dot(normed_rows, w_vmem[kind], preferred_element_type=jnp.float32)
        if kind == 0:
            result = result * score_scale
        for h in range(heads):
            tile, start = divmod(h * HDE, LANES)
            tiles = 1 if start + HDE <= LANES else 2
            head = result[:, tile * LANES : (tile + tiles) * LANES]
            if start:
                head = pltpu.roll(head, tiles * LANES - start, 1)
            head = jnp.where(lane < HDE, head[:, :LANES], extra).astype(jnp.bfloat16)
            if kind == 0:
                q_ref[at, h * LANES : (h + 1) * LANES] = head
            else:
                first = ((kind - 1) * heads + h) * LANES
                kv_ref[at, first : first + LANES] = head


def interior_kernel(
    where_ref,
    taps_hbm,
    audio_ref,
    w_ref,
    q_ref,
    kv_ref,
    pooled_ref,
    audio,
    full_src,
    full_dst,
    half_src,
    half_dst,
    taps_ref,
    full_taps,
    half_taps,
    mixed,
    normed,
    w_vmem,
    starts_ref,
    ends_ref,
    audio_sem,
    taps_sem,
    w_sem,
):
    rows = q_ref.shape[0]
    inner = rows + 2 * HALO
    skip = EDGE - HALO
    half = rows // 2
    load_audio = pltpu.make_async_copy(audio_ref.at[skip : skip + inner], audio, audio_sem)
    load_taps = pltpu.make_async_copy(taps_hbm, taps_ref, taps_sem)
    load_audio.start()
    load_taps.start()
    load_w = pltpu.make_async_copy(w_ref, w_vmem, w_sem)
    load_w.start()
    bounds = recording_bounds(where_ref, starts_ref, ends_ref)
    start = where_ref[0] + EDGE
    forward, back = shuffle(False), shuffle(True)
    load_audio.wait()
    side = SUBLANES // 2
    for row in range(0, inner, GROUP):
        value = audio[row : row + GROUP, : SUBLANES * LANES]
        to_tiles(forward, blocks_of(value, 0, SUBLANES), full_src, row)
    for row in range(0, half + 2 * HALO, GROUP):
        pair = [
            block
            for at in (row, row + half)
            for block in blocks_of(audio[at : at + GROUP, :], SUBLANES, side)
        ]
        to_tiles(forward, pair, half_src, row)
    load_taps.wait()
    spread_taps(taps_ref, full_taps, half_taps)
    recs = len(bounds)
    common = (recs, bounds, starts_ref, ends_ref)
    conv_blocks(full_src, full_dst, full_taps, rows // BLOCK, 4, [start], *common)
    conv_blocks(half_src, half_dst, half_taps, half // BLOCK, 2, [start, start + half], *common)


    for row in range(0, half, GROUP):
        pair = from_tiles(back, half_dst, row)
        for which in range(2):
            at = which * half + row
            blocks = from_tiles(back, full_dst, at) + pair[which * side : (which + 1) * side]
            normalise(blocks, mixed, normed, slice(at, at + GROUP))

    width = pooled_ref.shape[1]
    own_columns = pl.ds(pl.multiple_of(where_ref[1] * width, LANES), width)
    pooled_ref[...] = jnp.dot(
        pool_rows(rows), mixed[:, own_columns], preferred_element_type=jnp.float32
    )
    load_w.wait()
    for which in range(2):
        at = slice(which * half, (which + 1) * half)
        position = start + which * half + lax.broadcasted_iota(jnp.int32, (half, LANES), 0)
        project_heads(normed[at, :], w_vmem, position, bounds, at, q_ref, kv_ref)


def edge_kernel(
    where_ref,
    taps_hbm,
    audio_ref,
    halo_ref,
    w_ref,
    q_ref,
    kv_ref,
    pooled_ref,
    audio,
    full_src,
    full_dst,
    half_src,
    half_dst,
    taps_ref,
    full_taps,
    half_taps,
    mixed,
    normed,
    w_vmem,
    starts_ref,
    ends_ref,
    first_sem,
    last_sem,
    taps_sem,
    w_sem,
):
    frames = audio_ref.shape[0]
    known = EDGE + HALO
    loads = [
        pltpu.make_async_copy(audio_ref.at[:known], audio.at[:known], first_sem),
        pltpu.make_async_copy(audio_ref.at[frames - known :], audio.at[known:], last_sem),
        pltpu.make_async_copy(taps_hbm, taps_ref, taps_sem),
        pltpu.make_async_copy(w_ref, w_vmem, w_sem),
    ]
    for load in loads:
        load.start()
    bounds = recording_bounds(where_ref, starts_ref, ends_ref)
    forward, back = shuffle(False), shuffle(True)
    starts = [where_ref[0], where_ref[0] + frames - EDGE]
    length = EDGE + 2 * HALO
    has_before = (starts[0] > 0).astype(jnp.float32)
    has_after = (starts[0] + frames < bounds[-1]).astype(jnp.float32)
    before = (halo_ref[HALO:, :].astype(jnp.float32) * has_before).astype(jnp.bfloat16)
    after = (halo_ref[:HALO, :].astype(jnp.float32) * has_after).astype(jnp.bfloat16)
    for load in loads[:3]:
        load.wait()
    side = SUBLANES // 2
    for row in range(0, length, GROUP):
        first = before if row == 0 else audio[row - HALO : row - HALO + GROUP, :]
        last = after if row == known else audio[known + row : known + row + GROUP, :]
        for which, value in enumerate((first, last)):
            to_tiles(forward, blocks_of(value, 0, SUBLANES), full_src.at[which], row)
        pair = blocks_of(first, SUBLANES, side) + blocks_of(last, SUBLANES, side)
        to_tiles(forward, pair, half_src, row)
    spread_taps(taps_ref, full_taps, half_taps)
    recs = len(bounds)
    common = (recs, bounds, starts_ref, ends_ref)
    for which in range(2):
        conv_blocks(
            full_src.at[which],
            full_dst.at[which],
            full_taps,
            EDGE // BLOCK,
            2,
            [starts[which]],
            *common,
        )
    conv_blocks(half_src, half_dst, half_taps, EDGE // BLOCK, 2, starts, *common)
    for row in range(0, EDGE, GROUP):
        pair = from_tiles(back, half_dst, row)
        for which in range(2):
            blocks = from_tiles(back, full_dst.at[which], row)
            blocks += pair[which * side : (which + 1) * side]
            at = which * EDGE + row
            normalise(blocks, mixed, normed, slice(at, at + GROUP))
    width = pooled_ref.shape[1]
    own_columns = pl.ds(pl.multiple_of(where_ref[1] * width, LANES), width)
    pooled_ref[...] = jnp.dot(
        pool_rows(2 * EDGE), mixed[:, own_columns], preferred_element_type=jnp.float32
    )
    loads[3].wait()
    row = lax.broadcasted_iota(jnp.int32, (2 * EDGE, LANES), 0)
    position = jnp.where(row < EDGE, starts[0] + row, starts[1] - EDGE + row)
    project_heads(normed[...], w_vmem, position, bounds, slice(None), q_ref, kv_ref)


def attend_kernel(count, rows, targets_ref, mid_q, edge_q, w_ref, *refs):
    kv_refs, out_refs = refs[: 2 * count], refs[2 * count : -5]
    queries, kv, pooled, w_vmem, w_sem = refs[-5:]
    frames = queries.shape[0]
    heads = queries.shape[1] // LANES
    width = out_refs[0].shape[1]
    loads = [
        pltpu.make_async_copy(
            w_ref.at[h * HDE : (h + 1) * HDE], w_vmem.at[h * LANES : h * LANES + HDE], w_sem.at[h]
        )
        for h in range(heads)
    ]
    for load in loads:
        load.start()
    for h in range(heads):
        w_vmem[h * LANES + HDE : (h + 1) * LANES, :] = jnp.zeros(
            (LANES - HDE, w_vmem.shape[1]), jnp.bfloat16
        )
    queries[:EDGE, :] = edge_q[:EDGE, :]
    queries[EDGE : frames - EDGE, :] = mid_q[...]
    queries[frames - EDGE :, :] = edge_q[EDGE:, :]
    at = 0
    for ref in kv_refs:
        kv[at : at + ref.shape[0], :] = ref[...]
        at += ref.shape[0]
    few = rows // STRIDE
    pool = pool_rows(rows)

    def step(i, carry):
        at = pl.ds(pl.multiple_of(i * rows, rows), rows)
        for h in range(heads):
            lanes = slice(h * LANES, (h + 1) * LANES)
            scores = lax.dot_general(
                queries[at, lanes],
                kv[:, lanes],
                (((1,), (1,)), ((), ())),
                preferred_element_type=jnp.float32,
            )
            peak = jnp.max(scores, axis=1, keepdims=True)
            weights = jnp.exp2(scores - peak).astype(jnp.bfloat16)
            values = kv[:, (heads + h) * LANES : (heads + h + 1) * LANES]
            out = jnp.dot(weights, values, preferred_element_type=jnp.float32)
            attended = (out * (1.0 / out[:, HDE : HDE + 1])).astype(jnp.bfloat16)
            pooled[pl.ds(pl.multiple_of(i * few, few), few), lanes] = jnp.dot(
                pool, attended, preferred_element_type=jnp.float32
            ).astype(jnp.bfloat16)
        return carry

    lax.fori_loop(0, frames // rows, step, 0)
    for load in loads:
        load.wait()
    for k, out_ref in enumerate(out_refs):
        columns = pl.ds(pl.multiple_of(targets_ref[k] * width, LANES), width)
        total = jnp.dot(pooled[...], w_vmem[:, columns], preferred_element_type=jnp.float32)
        out_ref[...] = total.astype(out_ref.dtype)


def project_kernel(targets_ref, *refs):
    *part_refs, w_ref, out_ref, squares_ref, pooled = refs
    width = part_refs[0].shape[1]
    for k, part_ref in enumerate(part_refs):
        at = pl.ds(pl.multiple_of(targets_ref[k] * width, LANES), width)
        pooled[:, at] = part_ref[...]
    total = jnp.dot(pooled[...], w_ref[...], preferred_element_type=jnp.float32)
    out_ref[...] = total
    rows = total.shape[0]
    squares = jnp.sum(total * total, axis=1, keepdims=True)
    squares_ref[...] = jnp.transpose(jnp.broadcast_to(squares, (rows, rows)))[:SUBLANES]


def route_kernel(cap, outs, firsts_ref, place_ref, rows_ref, *refs):
    square_refs, out_refs = refs[:-outs], refs[-outs:]
    rows = rows_ref.shape[0]
    devices = firsts_ref.shape[0] if len(out_refs) > 1 else out_refs[0].shape[0] // cap
    squares = square_refs[0][...]
    for ref in square_refs[1:]:
        squares += ref[...]
    scale = lax.rsqrt(squares[:1] / D + 1e-05)
    scale = jnp.transpose(jnp.broadcast_to(scale, (rows, rows)))[:, :1]
    normal_rows = (rows_ref[...] * scale).astype(jnp.bfloat16)
    destination = place_ref[...]
    named = lax.broadcasted_iota(jnp.int32, (devices, rows), 0) == destination
    earlier = lax.broadcasted_iota(jnp.int32, (rows, rows), 0) < lax.broadcasted_iota(
        jnp.int32, (rows, rows), 1
    )
    counts = jnp.dot(
        named.astype(jnp.float32).astype(jnp.bfloat16),
        earlier.astype(jnp.float32).astype(jnp.bfloat16),
        preferred_element_type=jnp.float32,
    )
    rank = jnp.sum(jnp.where(named, counts, 0.0), axis=0, keepdims=True).astype(jnp.int32)
    target = destination * cap + rank
    runs = firsts_ref.shape[0] // outs
    for k, out_ref in enumerate(out_refs):
        slots = out_ref.shape[0] // runs
        for run in range(runs):
            first = firsts_ref[k * runs + run]
            slot = first + lax.broadcasted_iota(jnp.int32, (slots, rows), 0)
            one_hot = (slot == target).astype(jnp.float32).astype(jnp.bfloat16)
            out_ref[run * slots : (run + 1) * slots, :] = jnp.dot(
                one_hot, normal_rows, preferred_element_type=jnp.float32
            ).astype(jnp.bfloat16)


def forward_kernel(*refs):
    *block_refs, out_ref = refs
    slots = block_refs[0].shape[0] // 2
    for k, block_ref in enumerate(block_refs):
        out_ref[k * slots : (k + 1) * slots, :] = block_ref[slots:, :]


def collect_kernel(firsts_ref, *refs):
    *block_refs, other_ref, out_ref = refs
    slots = block_refs[0].shape[0] // 2
    for k, block_ref in enumerate(block_refs):
        mine = pl.ds(pl.multiple_of(firsts_ref[2 * k], slots), slots)
        out_ref[mine, :] = block_ref[:slots, :]
        theirs = pl.ds(pl.multiple_of(firsts_ref[2 * k + 1], slots), slots)
        out_ref[theirs, :] = other_ref[k * slots : (k + 1) * slots, :]


def partner(index, k, devices):
    if devices & (devices - 1) == 0:
        return index ^ k
    return (index + k) % devices


def sender(index, k, devices):
    if devices & (devices - 1) == 0:
        return index ^ k
    return (index - k) % devices


def exchange(value, axes, k, devices):
    return lax.ppermute(value, axes, [(i, partner(i, k, devices)) for i in range(devices)])


def local(audio, lengths, conv_kernel, w_qkv, w_out, place, w_adapt):
    frame_count, channels = audio.shape
    seq_devices = lax.axis_size("tm")
    mp_devices = lax.axis_size("mp")
    recs = lengths.shape[1]
    group_frames = frame_count * seq_devices
    width = channels // mp_devices
    pooled_rows = frame_count // STRIDE
    heads = w_qkv.shape[2] // HDE
    where = jnp.concatenate(
        [jnp.stack([lax.axis_index("tm") * frame_count, lax.axis_index("mp")]), lengths[0]]
    )

    if seq_devices == 2:
        ends = jnp.concatenate([audio[:HALO], audio[frame_count - HALO :]], axis=0)
        halo = exchange(ends, "tm", 1, 2)
    else:
        up = [(i, i + 1) for i in range(seq_devices - 1)]
        down = [(j, i) for i, j in up]
        after = lax.ppermute(audio[:HALO], "tm", down)
        before = lax.ppermute(audio[frame_count - HALO :], "tm", up)
        halo = jnp.concatenate([after, before], axis=0)

    smem = pl.BlockSpec(memory_space=pltpu.SMEM)
    vmem = pl.BlockSpec(memory_space=pltpu.VMEM)
    hbm = pl.BlockSpec(memory_space=pltpu.HBM)
    w_three = jnp.transpose(w_qkv, (1, 0, 2))
    taps = conv_kernel.shape[0]

    def tiles(count, *lead):
        return pltpu.VMEM((*lead, count * SUBLANES, LANES), jnp.float32)

    def results(rows):
        return [
            jax.ShapeDtypeStruct((rows, heads * LANES), jnp.bfloat16),
            jax.ShapeDtypeStruct((rows, 2 * heads * LANES), jnp.bfloat16),
            jax.ShapeDtypeStruct((rows // STRIDE, width), jnp.float32),
        ]

    def shared(rows):
        return [
            pltpu.VMEM(conv_kernel.shape, jnp.float32),
            tiles(taps),
            tiles(taps),
            pltpu.VMEM((rows, channels), jnp.bfloat16),
            pltpu.VMEM((rows, channels), jnp.bfloat16),
            pltpu.VMEM(w_three.shape, jnp.bfloat16),
            pltpu.SMEM((recs,), jnp.int32),
            pltpu.SMEM((recs,), jnp.int32),
        ]

    mid = frame_count - 2 * EDGE
    mid_q, mid_kv, mid_mixed = pl.pallas_call(
        interior_kernel,
        out_shape=results(mid),
        in_specs=[smem, hbm, hbm, hbm],
        out_specs=[vmem] * 3,
        scratch_shapes=[
            pltpu.VMEM((mid + 2 * HALO, channels), jnp.bfloat16),
            tiles(mid + 2 * HALO),
            tiles(mid),
            tiles(mid // 2 + 2 * HALO),
            tiles(mid // 2),
            *shared(mid),
            *[pltpu.SemaphoreType.DMA] * 3,
        ],
        compiler_params=pltpu.CompilerParams(vmem_limit_bytes=53 * MIB),
        cost_estimate=pl.CostEstimate(
            flops=60 * mid * channels * w_qkv.shape[2], bytes_accessed=4 * MIB, transcendentals=0
        ),
        name="interior",
    )(where, conv_kernel, audio, w_three)
    edge_q, edge_kv, edge_mixed = pl.pallas_call(
        edge_kernel,
        out_shape=results(2 * EDGE),
        in_specs=[smem, hbm, hbm, vmem, hbm],
        out_specs=[vmem] * 3,
        scratch_shapes=[
            pltpu.VMEM((2 * (EDGE + HALO), channels), jnp.bfloat16),
            tiles(EDGE + 2 * HALO, 2),
            tiles(EDGE, 2),
            tiles(EDGE + 2 * HALO),
            tiles(EDGE),
            *shared(2 * EDGE),
            *[pltpu.SemaphoreType.DMA] * 4,
        ],
        compiler_params=pltpu.CompilerParams(vmem_limit_bytes=44 * MIB),
        cost_estimate=pl.CostEstimate(
            flops=240 * EDGE * channels * w_qkv.shape[2], bytes_accessed=4 * MIB, transcendentals=0
        ),
        name="edges",
    )(
        where,
        conv_kernel,
        audio,
        halo,
        w_three,
    )

    kv_blocks = [mid_kv, edge_kv]
    for k in range(1, seq_devices):
        kv_blocks += [exchange(block, "tm", k, seq_devices) for block in (mid_kv, edge_kv)]
    mp_index = lax.axis_index("mp")
    mp_targets = jnp.stack([partner(mp_index, k, mp_devices) for k in range(mp_devices)])
    mp_senders = jnp.stack([sender(mp_index, k, mp_devices) for k in range(mp_devices)])
    part = (pooled_rows, width)
    own_part, *parts = pl.pallas_call(
        functools.partial(attend_kernel, seq_devices, 256 if seq_devices <= 2 else 64),
        out_shape=[jax.ShapeDtypeStruct(part, jnp.float32)]
        + [jax.ShapeDtypeStruct(part, jnp.bfloat16)] * (mp_devices - 1),
        in_specs=[smem, vmem, vmem, hbm] + [vmem] * len(kv_blocks),
        out_specs=[vmem] * mp_devices,
        scratch_shapes=[
            pltpu.VMEM((frame_count, heads * LANES), jnp.bfloat16),
            pltpu.VMEM((group_frames, 2 * heads * LANES), jnp.bfloat16),
            pltpu.VMEM((pooled_rows, heads * LANES), jnp.bfloat16),
            pltpu.VMEM((heads * LANES, channels), jnp.bfloat16),
            pltpu.SemaphoreType.DMA((heads,)),
        ],
        compiler_params=pltpu.CompilerParams(
            vmem_limit_bytes=44 * MIB
        ),
        name="attend",
    )(mp_targets, mid_q, edge_q, w_out, *kv_blocks)
    cut = EDGE // STRIDE
    own_part += jnp.concatenate([edge_mixed[:cut], mid_mixed, edge_mixed[cut:]], axis=0)
    others = range(1, mp_devices)
    for k in others:
        own_part += exchange(parts[k - 1], "mp", k, mp_devices).astype(jnp.float32)
    own_part = own_part.astype(jnp.bfloat16)
    pooled = [own_part] + [exchange(own_part, "mp", k, mp_devices) for k in others]

    columns = w_adapt.shape[1]
    projected, squares = pl.pallas_call(
        project_kernel,
        out_shape=[
            jax.ShapeDtypeStruct((pooled_rows, columns), jnp.float32),
            jax.ShapeDtypeStruct((SUBLANES, pooled_rows), jnp.float32),
        ],
        in_specs=[smem] + [vmem] * (mp_devices + 1),
        out_specs=[vmem] * 2,
        scratch_shapes=[pltpu.VMEM((pooled_rows, channels), jnp.bfloat16)],
        compiler_params=pltpu.CompilerParams(vmem_limit_bytes=16 * MIB),
        name="project",
    )(mp_senders, *pooled, w_adapt)
    squares = [squares] + [exchange(squares, "mp", k, mp_devices) for k in others]

    axes = ("section", "tm")
    sections = lax.axis_size("section")
    device_count = sections * seq_devices
    cap = max(2, (2 * pooled_rows + device_count - 1) // device_count)
    section, core = lax.axis_index("section"), lax.axis_index("tm")
    direct = seq_devices == 2 and sections <= 4
    if direct:

        def slots_of(pairing):
            chosen = [pairing(section, k, sections) * 2 for k in range(sections)]
            return jnp.stack([(chip + c) * cap for chip in chosen for c in (core, 1 - core)])

        firsts = slots_of(partner)
        blocks = [jax.ShapeDtypeStruct((2 * cap, columns), jnp.bfloat16)] * sections
    else:
        firsts = jnp.zeros((1,), jnp.int32)
        blocks = [jax.ShapeDtypeStruct((device_count * cap, columns), jnp.bfloat16)]
    blocks = pl.pallas_call(
        functools.partial(route_kernel, cap, len(blocks)),
        out_shape=blocks,
        in_specs=[smem] + [vmem] * (mp_devices + 2),
        out_specs=[vmem] * len(blocks),
        compiler_params=pltpu.CompilerParams(vmem_limit_bytes=16 * MIB),
        name="route",
    )(firsts, place.T, projected, *squares)
    if not direct:
        return lax.all_to_all(blocks[0], axes, split_axis=0, concat_axis=0, tiled=True)
    arrived = [blocks[0]] + [
        exchange(blocks[k], "section", k, sections) for k in range(1, sections)
    ]
    passed = pl.pallas_call(
        forward_kernel,
        out_shape=jax.ShapeDtypeStruct((sections * cap, columns), jnp.bfloat16),
        in_specs=[vmem] * sections,
        out_specs=vmem,
        compiler_params=pltpu.CompilerParams(vmem_limit_bytes=8 * MIB),
        name="forward",
    )(*arrived)
    return pl.pallas_call(
        collect_kernel,
        out_shape=jax.ShapeDtypeStruct((device_count * cap, columns), jnp.bfloat16),
        in_specs=[smem] + [vmem] * (sections + 1),
        out_specs=vmem,
        compiler_params=pltpu.CompilerParams(vmem_limit_bytes=8 * MIB),
        name="collect",
    )(slots_of(sender), *arrived, exchange(passed, "tm", 1, 2))


def solution(mesh):
    placed = (
        P(("section", "tm"), None),
        P("section", None),
        P(),
        P(None, None, "mp"),
        P("mp", None),
        P(("section", "tm"), None),
        P(None, "mp"),
    )
    return jax.shard_map(
        local, mesh=mesh, in_specs=placed, out_specs=P(("section", "tm"), "mp"), check_vma=False
    )
```

```python
import functools
import math

import jax
import jax.numpy as jnp
from jax import lax
from jax.experimental import pallas as pl
from jax.experimental.pallas import tpu as pltpu
from jax.sharding import PartitionSpec as P

HDE = 96
D = 5120
STRIDE = 4
LANES = 128
SUBLANES = 8
HALO = 16
EDGE = 32
BLOCK = 16
GROUP = 16
MIB = 1 << 20
HIDDEN = -1e30


def conv_blocks(src, dst, taps, blocks, run, firsts, recs, bounds, starts_ref, ends_ref):
    count = taps.shape[0] // SUBLANES
    reach = count // 2
    span = BLOCK + count - 1
    shape = (SUBLANES, LANES)
    upper = lax.broadcasted_iota(jnp.int32, shape, 0) < SUBLANES // 2

    def both(values):
        if len(values) == 1:
            return jnp.full(shape, values[0], jnp.int32)
        return jnp.where(upper, values[0], values[1])

    def convolve(base, inside):
        def frame(k):
            at = (base + k + HALO - reach) * SUBLANES
            return src[pl.ds(pl.multiple_of(at, SUBLANES), SUBLANES), :]

        kernel = [taps[j * SUBLANES : (j + 1) * SUBLANES, :] for j in range(count)]
        totals = [None] * BLOCK
        for k in range(span):
            value = frame(k)
            if inside is not None:
                value = jnp.where(inside(k), value, 0.0)
            for t in range(max(0, k - count + 1), min(BLOCK, k + 1)):
                term = kernel[k - t] * value
                totals[t] = term if totals[t] is None else totals[t] + term
        for t in range(BLOCK):
            at = pl.ds(pl.multiple_of((base + t) * SUBLANES, SUBLANES), SUBLANES)
            half = 0.5 * totals[t]
            value = frame(t + reach) + half * (1.0 + jnp.tanh(half))
            if inside is not None:
                value = jnp.where(inside(t + reach), value, dst[at, :])
            dst[at, :] = value

    def touched(base, length):
        found = jnp.zeros((), jnp.bool_)
        for first in firsts:
            for bound in bounds[:-1]:
                at = bound - first - base
                found = found | ((at > -reach) & (at < length + reach))
        return found

    def masked(base):
        positions = [first + base for first in firsts]
        begin, extra = [], jnp.zeros((), jnp.int32)
        for position in positions:
            first = last = jnp.zeros((), jnp.int32)
            for bound in bounds[:-1]:
                first += (bound <= position).astype(jnp.int32)
                last += (bound <= position + BLOCK - 1).astype(jnp.int32)
            begin.append(first)
            extra = jnp.maximum(extra, last - first)

        def once(turn, carry):
            which = [jnp.minimum(first + turn, recs - 1) for first in begin]
            low = both([starts_ref[r] - p for r, p in zip(which, positions)])
            high = both([ends_ref[r] - p for r, p in zip(which, positions)])
            convolve(base, lambda k: (low <= k - reach) & (high > k - reach))
            return carry

        lax.fori_loop(0, extra + 1, once, 0)

    def blocks_of_run(i, carry):
        base = i * run * BLOCK
        any_touched = touched(base, run * BLOCK)

        @pl.when(jnp.logical_not(any_touched))
        def _():
            for j in range(run):
                convolve(base + j * BLOCK, None)

        @pl.when(any_touched)
        def _():
            def one(j, carry):
                here = base + j * BLOCK
                mine = touched(here, BLOCK)

                @pl.when(mine)
                def _():
                    masked(here)

                @pl.when(jnp.logical_not(mine))
                def _():
                    convolve(here, None)

                return carry

            lax.fori_loop(0, run, one, 0)

        return carry

    lax.fori_loop(0, blocks // run, blocks_of_run, 0)


def shuffle(back):
    row = lax.broadcasted_iota(jnp.int32, (LANES, LANES), 1 if back else 0)
    column = lax.broadcasted_iota(jnp.int32, (LANES, LANES), 0 if back else 1)
    moved = (row // SUBLANES == column % GROUP) & (row % SUBLANES == column // GROUP)
    return moved.astype(jnp.float32).astype(jnp.bfloat16)


def to_tiles(matrix, values, ref, frame):
    stack = jnp.concatenate(values, axis=0)
    at = pl.ds(frame * SUBLANES, GROUP * SUBLANES)
    ref[at, :] = jnp.dot(matrix, stack, preferred_element_type=jnp.float32)


def from_tiles(matrix, ref, frame):
    rows = GROUP * SUBLANES
    low = ref[frame * SUBLANES : frame * SUBLANES + rows, :].astype(jnp.bfloat16)
    moved = jnp.dot(matrix, low, preferred_element_type=jnp.float32)
    return [moved[k * GROUP : (k + 1) * GROUP] for k in range(SUBLANES)]


def blocks_of(value, first, count):
    return [value[:, k * LANES : (k + 1) * LANES] for k in range(first, first + count)]


def recording_bounds(where_ref, starts_ref, ends_ref):
    bounds, total = [], jnp.zeros((), jnp.int32)
    for r in range(where_ref.shape[0] - 2):
        starts_ref[r] = total
        total = total + where_ref[2 + r]
        ends_ref[r] = total
        bounds.append(total)
    return bounds


def spread_taps(taps_ref, full_taps, half_taps):
    count = taps_ref.shape[0]
    blocks = taps_ref.shape[1] // LANES
    for k in range(blocks):
        value = taps_ref[:, k * LANES : (k + 1) * LANES]
        if k < SUBLANES:
            full_taps[pl.ds(k, count, stride=SUBLANES), :] = value
        else:
            for half in range(2):
                at = k - SUBLANES + half * SUBLANES // 2
                half_taps[pl.ds(at, count, stride=SUBLANES), :] = value


def normalise(blocks, mixed, normed, at):
    values = jnp.concatenate(blocks, axis=1)
    mixed[at, :] = values.astype(jnp.bfloat16)
    centred = values - jnp.mean(values, -1, keepdims=True)
    variance = jnp.mean(centred * centred, -1, keepdims=True)
    normed[at, :] = (centred * lax.rsqrt(variance + 1e-05)).astype(jnp.bfloat16)


def pool_rows(rows):
    few = rows // STRIDE
    chosen = (
        lax.broadcasted_iota(jnp.int32, (few, rows), 1) // STRIDE
        == lax.broadcasted_iota(jnp.int32, (few, rows), 0)
    )
    return (chosen.astype(jnp.float32) * (1.0 / STRIDE)).astype(jnp.bfloat16)


def project_heads(normed_rows, w_vmem, position, bounds, at, q_ref, kv_ref):
    recs = len(bounds)
    heads = w_vmem.shape[2] // HDE
    lane = lax.broadcasted_iota(jnp.int32, position.shape, 1)
    mine = jnp.zeros(position.shape, jnp.int32)
    for bound in bounds:
        mine += (position >= bound).astype(jnp.int32)
    same = lane - HDE == mine
    extra_q = jnp.where(same | (lane >= HDE + recs), 0.0, HIDDEN)
    extra_k = jnp.where(same, 1.0, 0.0)
    extra_v = jnp.where(lane == HDE, 1.0, 0.0)
    score_scale = HDE ** (-0.5) * math.log2(math.e)
    for kind, extra in enumerate((extra_q, extra_k, extra_v)):
        result = jnp.dot(normed_rows, w_vmem[kind], preferred_element_type=jnp.float32)
        if kind == 0:
            result = result * score_scale
        for h in range(heads):
            tile, start = divmod(h * HDE, LANES)
            tiles = 1 if start + HDE <= LANES else 2
            head = result[:, tile * LANES : (tile + tiles) * LANES]
            if start:
                head = pltpu.roll(head, tiles * LANES - start, 1)
            head = jnp.where(lane < HDE, head[:, :LANES], extra).astype(jnp.bfloat16)
            if kind == 0:
                q_ref[at, h * LANES : (h + 1) * LANES] = head
            else:
                first = ((kind - 1) * heads + h) * LANES
                kv_ref[at, first : first + LANES] = head


def interior_kernel(
    where_ref,
    taps_hbm,
    audio_ref,
    w_ref,
    q_ref,
    kv_ref,
    pooled_ref,
    audio,
    full_src,
    full_dst,
    half_src,
    half_dst,
    taps_ref,
    full_taps,
    half_taps,
    mixed,
    normed,
    w_vmem,
    starts_ref,
    ends_ref,
    audio_sem,
    taps_sem,
    w_sem,
):
    rows = q_ref.shape[0]
    inner = rows + 2 * HALO
    skip = EDGE - HALO
    half = rows // 2
    load_audio = pltpu.make_async_copy(audio_ref.at[skip : skip + inner], audio, audio_sem)
    load_taps = pltpu.make_async_copy(taps_hbm, taps_ref, taps_sem)
    load_audio.start()
    load_taps.start()
    load_w = pltpu.make_async_copy(w_ref, w_vmem, w_sem)
    load_w.start()
    bounds = recording_bounds(where_ref, starts_ref, ends_ref)
    start = where_ref[0] + EDGE
    forward, back = shuffle(False), shuffle(True)
    load_audio.wait()
    side = SUBLANES // 2
    for row in range(0, inner, GROUP):
        value = audio[row : row + GROUP, : SUBLANES * LANES]
        to_tiles(forward, blocks_of(value, 0, SUBLANES), full_src, row)
    for row in range(0, half + 2 * HALO, GROUP):
        pair = [
            block
            for at in (row, row + half)
            for block in blocks_of(audio[at : at + GROUP, :], SUBLANES, side)
        ]
        to_tiles(forward, pair, half_src, row)
    load_taps.wait()
    spread_taps(taps_ref, full_taps, half_taps)
    recs = len(bounds)
    common = (recs, bounds, starts_ref, ends_ref)
    conv_blocks(full_src, full_dst, full_taps, rows // BLOCK, 4, [start], *common)
    conv_blocks(half_src, half_dst, half_taps, half // BLOCK, 2, [start, start + half], *common)


    for row in range(0, half, GROUP):
        pair = from_tiles(back, half_dst, row)
        for which in range(2):
            at = which * half + row
            blocks = from_tiles(back, full_dst, at) + pair[which * side : (which + 1) * side]
            normalise(blocks, mixed, normed, slice(at, at + GROUP))

    width = pooled_ref.shape[1]
    own_columns = pl.ds(pl.multiple_of(where_ref[1] * width, LANES), width)
    pooled_ref[...] = jnp.dot(
        pool_rows(rows), mixed[:, own_columns], preferred_element_type=jnp.float32
    )
    load_w.wait()
    for which in range(2):
        at = slice(which * half, (which + 1) * half)
        position = start + which * half + lax.broadcasted_iota(jnp.int32, (half, LANES), 0)
        project_heads(normed[at, :], w_vmem, position, bounds, at, q_ref, kv_ref)


def edge_kernel(
    where_ref,
    taps_hbm,
    audio_ref,
    halo_ref,
    w_ref,
    q_ref,
    kv_ref,
    pooled_ref,
    audio,
    full_src,
    full_dst,
    half_src,
    half_dst,
    taps_ref,
    full_taps,
    half_taps,
    mixed,
    normed,
    w_vmem,
    starts_ref,
    ends_ref,
    first_sem,
    last_sem,
    taps_sem,
    w_sem,
):
    frames = audio_ref.shape[0]
    known = EDGE + HALO
    loads = [
        pltpu.make_async_copy(audio_ref.at[:known], audio.at[:known], first_sem),
        pltpu.make_async_copy(audio_ref.at[frames - known :], audio.at[known:], last_sem),
        pltpu.make_async_copy(taps_hbm, taps_ref, taps_sem),
        pltpu.make_async_copy(w_ref, w_vmem, w_sem),
    ]
    for load in loads:
        load.start()
    bounds = recording_bounds(where_ref, starts_ref, ends_ref)
    forward, back = shuffle(False), shuffle(True)
    starts = [where_ref[0], where_ref[0] + frames - EDGE]
    length = EDGE + 2 * HALO
    has_before = (starts[0] > 0).astype(jnp.float32)
    has_after = (starts[0] + frames < bounds[-1]).astype(jnp.float32)
    before = (halo_ref[HALO:, :].astype(jnp.float32) * has_before).astype(jnp.bfloat16)
    after = (halo_ref[:HALO, :].astype(jnp.float32) * has_after).astype(jnp.bfloat16)
    for load in loads[:3]:
        load.wait()
    side = SUBLANES // 2
    for row in range(0, length, GROUP):
        first = before if row == 0 else audio[row - HALO : row - HALO + GROUP, :]
        last = after if row == known else audio[known + row : known + row + GROUP, :]
        for which, value in enumerate((first, last)):
            to_tiles(forward, blocks_of(value, 0, SUBLANES), full_src.at[which], row)
        pair = blocks_of(first, SUBLANES, side) + blocks_of(last, SUBLANES, side)
        to_tiles(forward, pair, half_src, row)
    spread_taps(taps_ref, full_taps, half_taps)
    recs = len(bounds)
    common = (recs, bounds, starts_ref, ends_ref)
    for which in range(2):
        conv_blocks(
            full_src.at[which],
            full_dst.at[which],
            full_taps,
            EDGE // BLOCK,
            2,
            [starts[which]],
            *common,
        )
    conv_blocks(half_src, half_dst, half_taps, EDGE // BLOCK, 2, starts, *common)
    for row in range(0, EDGE, GROUP):
        pair = from_tiles(back, half_dst, row)
        for which in range(2):
            blocks = from_tiles(back, full_dst.at[which], row)
            blocks += pair[which * side : (which + 1) * side]
            at = which * EDGE + row
            normalise(blocks, mixed, normed, slice(at, at + GROUP))
    width = pooled_ref.shape[1]
    own_columns = pl.ds(pl.multiple_of(where_ref[1] * width, LANES), width)
    pooled_ref[...] = jnp.dot(
        pool_rows(2 * EDGE), mixed[:, own_columns], preferred_element_type=jnp.float32
    )
    loads[3].wait()
    row = lax.broadcasted_iota(jnp.int32, (2 * EDGE, LANES), 0)
    position = jnp.where(row < EDGE, starts[0] + row, starts[1] - EDGE + row)
    project_heads(normed[...], w_vmem, position, bounds, slice(None), q_ref, kv_ref)


def attend_kernel(count, rows, targets_ref, mid_q, edge_q, w_ref, *refs):
    kv_refs, out_refs = refs[: 2 * count], refs[2 * count : -5]
    queries, kv, pooled, w_vmem, w_sem = refs[-5:]
    frames = queries.shape[0]
    heads = queries.shape[1] // LANES
    width = out_refs[0].shape[1]
    loads = [
        pltpu.make_async_copy(
            w_ref.at[h * HDE : (h + 1) * HDE], w_vmem.at[h * LANES : h * LANES + HDE], w_sem.at[h]
        )
        for h in range(heads)
    ]
    for load in loads:
        load.start()
    for h in range(heads):
        w_vmem[h * LANES + HDE : (h + 1) * LANES, :] = jnp.zeros(
            (LANES - HDE, w_vmem.shape[1]), jnp.bfloat16
        )
    queries[:EDGE, :] = edge_q[:EDGE, :]
    queries[EDGE : frames - EDGE, :] = mid_q[...]
    queries[frames - EDGE :, :] = edge_q[EDGE:, :]
    at = 0
    for ref in kv_refs:
        kv[at : at + ref.shape[0], :] = ref[...]
        at += ref.shape[0]
    few = rows // STRIDE
    pool = pool_rows(rows)

    def step(i, carry):
        at = pl.ds(pl.multiple_of(i * rows, rows), rows)
        for h in range(heads):
            lanes = slice(h * LANES, (h + 1) * LANES)
            scores = lax.dot_general(
                queries[at, lanes],
                kv[:, lanes],
                (((1,), (1,)), ((), ())),
                preferred_element_type=jnp.float32,
            )
            peak = jnp.max(scores, axis=1, keepdims=True)
            weights = jnp.exp2(scores - peak).astype(jnp.bfloat16)
            values = kv[:, (heads + h) * LANES : (heads + h + 1) * LANES]
            out = jnp.dot(weights, values, preferred_element_type=jnp.float32)
            attended = (out * (1.0 / out[:, HDE : HDE + 1])).astype(jnp.bfloat16)
            pooled[pl.ds(pl.multiple_of(i * few, few), few), lanes] = jnp.dot(
                pool, attended, preferred_element_type=jnp.float32
            ).astype(jnp.bfloat16)
        return carry

    lax.fori_loop(0, frames // rows, step, 0)
    for load in loads:
        load.wait()
    for k, out_ref in enumerate(out_refs):
        columns = pl.ds(pl.multiple_of(targets_ref[k] * width, LANES), width)
        total = jnp.dot(pooled[...], w_vmem[:, columns], preferred_element_type=jnp.float32)
        out_ref[...] = total.astype(out_ref.dtype)


def sum_kernel(mid_ref, edge_ref, own_ref, *refs):
    *part_refs, out_ref = refs
    total = own_ref[...]
    for part_ref in part_refs:
        total += part_ref[...].astype(jnp.float32)
    cut = EDGE // STRIDE
    mixed = jnp.concatenate([edge_ref[:cut, :], mid_ref[...], edge_ref[cut:, :]], axis=0)
    out_ref[...] = (total + mixed).astype(jnp.bfloat16)


def project_kernel(targets_ref, *refs):
    *part_refs, w_ref, out_ref, squares_ref, pooled = refs
    width = part_refs[0].shape[1]
    for k, part_ref in enumerate(part_refs):
        at = pl.ds(pl.multiple_of(targets_ref[k] * width, LANES), width)
        pooled[:, at] = part_ref[...]
    total = jnp.dot(pooled[...], w_ref[...], preferred_element_type=jnp.float32)
    out_ref[...] = total
    rows = total.shape[0]
    squares = jnp.sum(total * total, axis=1, keepdims=True)
    squares_ref[...] = jnp.transpose(jnp.broadcast_to(squares, (rows, rows)))[:SUBLANES]


def route_kernel(cap, outs, firsts_ref, place_ref, rows_ref, *refs):
    square_refs, out_refs = refs[:-outs], refs[-outs:]
    rows = rows_ref.shape[0]
    devices = firsts_ref.shape[0] if len(out_refs) > 1 else out_refs[0].shape[0] // cap
    squares = square_refs[0][...]
    for ref in square_refs[1:]:
        squares += ref[...]
    scale = lax.rsqrt(squares[:1] / D + 1e-05)
    scale = jnp.transpose(jnp.broadcast_to(scale, (rows, rows)))[:, :1]
    normal_rows = (rows_ref[...] * scale).astype(jnp.bfloat16)
    destination = place_ref[...]
    named = lax.broadcasted_iota(jnp.int32, (devices, rows), 0) == destination
    earlier = lax.broadcasted_iota(jnp.int32, (rows, rows), 0) < lax.broadcasted_iota(
        jnp.int32, (rows, rows), 1
    )
    counts = jnp.dot(
        named.astype(jnp.float32).astype(jnp.bfloat16),
        earlier.astype(jnp.float32).astype(jnp.bfloat16),
        preferred_element_type=jnp.float32,
    )
    rank = jnp.sum(jnp.where(named, counts, 0.0), axis=0, keepdims=True).astype(jnp.int32)
    target = destination * cap + rank
    runs = firsts_ref.shape[0] // outs
    for k, out_ref in enumerate(out_refs):
        slots = out_ref.shape[0] // runs
        for run in range(runs):
            first = firsts_ref[k * runs + run]
            slot = first + lax.broadcasted_iota(jnp.int32, (slots, rows), 0)
            one_hot = (slot == target).astype(jnp.float32).astype(jnp.bfloat16)
            out_ref[run * slots : (run + 1) * slots, :] = jnp.dot(
                one_hot, normal_rows, preferred_element_type=jnp.float32
            ).astype(jnp.bfloat16)


def forward_kernel(*refs):
    *block_refs, out_ref = refs
    slots = block_refs[0].shape[0] // 2
    for k, block_ref in enumerate(block_refs):
        out_ref[k * slots : (k + 1) * slots, :] = block_ref[slots:, :]


def collect_kernel(firsts_ref, *refs):
    *block_refs, other_ref, out_ref = refs
    slots = block_refs[0].shape[0] // 2
    for k, block_ref in enumerate(block_refs):
        mine = pl.ds(pl.multiple_of(firsts_ref[2 * k], slots), slots)
        out_ref[mine, :] = block_ref[:slots, :]
        theirs = pl.ds(pl.multiple_of(firsts_ref[2 * k + 1], slots), slots)
        out_ref[theirs, :] = other_ref[k * slots : (k + 1) * slots, :]


def partner(index, k, devices):
    if devices & (devices - 1) == 0:
        return index ^ k
    return (index + k) % devices


def sender(index, k, devices):
    if devices & (devices - 1) == 0:
        return index ^ k
    return (index - k) % devices


def exchange(value, axes, k, devices):
    return lax.ppermute(value, axes, [(i, partner(i, k, devices)) for i in range(devices)])


def local(audio, lengths, conv_kernel, w_qkv, w_out, place, w_adapt):
    frame_count, channels = audio.shape
    seq_devices = lax.axis_size("tm")
    mp_devices = lax.axis_size("mp")
    recs = lengths.shape[1]
    group_frames = frame_count * seq_devices
    width = channels // mp_devices
    pooled_rows = frame_count // STRIDE
    heads = w_qkv.shape[2] // HDE
    where = jnp.concatenate(
        [jnp.stack([lax.axis_index("tm") * frame_count, lax.axis_index("mp")]), lengths[0]]
    )

    if seq_devices == 2:
        ends = jnp.concatenate([audio[:HALO], audio[frame_count - HALO :]], axis=0)
        halo = exchange(ends, "tm", 1, 2)
    else:
        up = [(i, i + 1) for i in range(seq_devices - 1)]
        down = [(j, i) for i, j in up]
        after = lax.ppermute(audio[:HALO], "tm", down)
        before = lax.ppermute(audio[frame_count - HALO :], "tm", up)
        halo = jnp.concatenate([after, before], axis=0)

    smem = pl.BlockSpec(memory_space=pltpu.SMEM)
    vmem = pl.BlockSpec(memory_space=pltpu.VMEM)
    hbm = pl.BlockSpec(memory_space=pltpu.HBM)
    w_three = jnp.transpose(w_qkv, (1, 0, 2))
    taps = conv_kernel.shape[0]

    def tiles(count, *lead):
        return pltpu.VMEM((*lead, count * SUBLANES, LANES), jnp.float32)

    def results(rows):
        return [
            jax.ShapeDtypeStruct((rows, heads * LANES), jnp.bfloat16),
            jax.ShapeDtypeStruct((rows, 2 * heads * LANES), jnp.bfloat16),
            jax.ShapeDtypeStruct((rows // STRIDE, width), jnp.float32),
        ]

    def shared(rows):
        return [
            pltpu.VMEM(conv_kernel.shape, jnp.float32),
            tiles(taps),
            tiles(taps),
            pltpu.VMEM((rows, channels), jnp.bfloat16),
            pltpu.VMEM((rows, channels), jnp.bfloat16),
            pltpu.VMEM(w_three.shape, jnp.bfloat16),
            pltpu.SMEM((recs,), jnp.int32),
            pltpu.SMEM((recs,), jnp.int32),
        ]

    mid = frame_count - 2 * EDGE
    mid_q, mid_kv, mid_mixed = pl.pallas_call(
        interior_kernel,
        out_shape=results(mid),
        in_specs=[smem, hbm, hbm, hbm],
        out_specs=[vmem] * 3,
        scratch_shapes=[
            pltpu.VMEM((mid + 2 * HALO, channels), jnp.bfloat16),
            tiles(mid + 2 * HALO),
            tiles(mid),
            tiles(mid // 2 + 2 * HALO),
            tiles(mid // 2),
            *shared(mid),
            *[pltpu.SemaphoreType.DMA] * 3,
        ],
        compiler_params=pltpu.CompilerParams(vmem_limit_bytes=53 * MIB),
        cost_estimate=pl.CostEstimate(
            flops=60 * mid * channels * w_qkv.shape[2], bytes_accessed=4 * MIB, transcendentals=0
        ),
        name="interior",
    )(where, conv_kernel, audio, w_three)
    edge_q, edge_kv, edge_mixed = pl.pallas_call(
        edge_kernel,
        out_shape=results(2 * EDGE),
        in_specs=[smem, hbm, hbm, vmem, hbm],
        out_specs=[vmem] * 3,
        scratch_shapes=[
            pltpu.VMEM((2 * (EDGE + HALO), channels), jnp.bfloat16),
            tiles(EDGE + 2 * HALO, 2),
            tiles(EDGE, 2),
            tiles(EDGE + 2 * HALO),
            tiles(EDGE),
            *shared(2 * EDGE),
            *[pltpu.SemaphoreType.DMA] * 4,
        ],
        compiler_params=pltpu.CompilerParams(vmem_limit_bytes=44 * MIB),
        cost_estimate=pl.CostEstimate(
            flops=240 * EDGE * channels * w_qkv.shape[2], bytes_accessed=4 * MIB, transcendentals=0
        ),
        name="edges",
    )(
        where,
        conv_kernel,
        audio,
        halo,
        w_three,
    )

    kv_blocks = [mid_kv, edge_kv]
    for k in range(1, seq_devices):
        kv_blocks += [exchange(block, "tm", k, seq_devices) for block in (mid_kv, edge_kv)]
    mp_index = lax.axis_index("mp")
    mp_targets = jnp.stack([partner(mp_index, k, mp_devices) for k in range(mp_devices)])
    mp_senders = jnp.stack([sender(mp_index, k, mp_devices) for k in range(mp_devices)])
    part = (pooled_rows, width)
    own_part, *parts = pl.pallas_call(
        functools.partial(attend_kernel, seq_devices, 256 if seq_devices <= 2 else 64),
        out_shape=[jax.ShapeDtypeStruct(part, jnp.float32)]
        + [jax.ShapeDtypeStruct(part, jnp.bfloat16)] * (mp_devices - 1),
        in_specs=[smem, vmem, vmem, hbm] + [vmem] * len(kv_blocks),
        out_specs=[vmem] * mp_devices,
        scratch_shapes=[
            pltpu.VMEM((frame_count, heads * LANES), jnp.bfloat16),
            pltpu.VMEM((group_frames, 2 * heads * LANES), jnp.bfloat16),
            pltpu.VMEM((pooled_rows, heads * LANES), jnp.bfloat16),
            pltpu.VMEM((heads * LANES, channels), jnp.bfloat16),
            pltpu.SemaphoreType.DMA((heads,)),
        ],
        compiler_params=pltpu.CompilerParams(
            vmem_limit_bytes=44 * MIB
        ),
        name="attend",
    )(mp_targets, mid_q, edge_q, w_out, *kv_blocks)
    others = range(1, mp_devices)
    own_part = pl.pallas_call(
        sum_kernel,
        out_shape=jax.ShapeDtypeStruct(part, jnp.bfloat16),
        in_specs=[vmem] * (mp_devices + 2),
        out_specs=vmem,
        compiler_params=pltpu.CompilerParams(vmem_limit_bytes=8 * MIB),
        name="sum_heads",
    )(
        mid_mixed,
        edge_mixed,
        own_part,
        *[exchange(parts[k - 1], "mp", k, mp_devices) for k in others],
    )
    pooled = [own_part] + [exchange(own_part, "mp", k, mp_devices) for k in others]

    columns = w_adapt.shape[1]
    projected, squares = pl.pallas_call(
        project_kernel,
        out_shape=[
            jax.ShapeDtypeStruct((pooled_rows, columns), jnp.float32),
            jax.ShapeDtypeStruct((SUBLANES, pooled_rows), jnp.float32),
        ],
        in_specs=[smem] + [vmem] * (mp_devices + 1),
        out_specs=[vmem] * 2,
        scratch_shapes=[pltpu.VMEM((pooled_rows, channels), jnp.bfloat16)],
        compiler_params=pltpu.CompilerParams(vmem_limit_bytes=16 * MIB),
        name="project",
    )(mp_senders, *pooled, w_adapt)
    squares = [squares] + [exchange(squares, "mp", k, mp_devices) for k in others]

    axes = ("section", "tm")
    sections = lax.axis_size("section")
    device_count = sections * seq_devices
    cap = max(2, (2 * pooled_rows + device_count - 1) // device_count)
    section, core = lax.axis_index("section"), lax.axis_index("tm")
    direct = seq_devices == 2 and sections <= 4
    if direct:

        def slots_of(pairing):
            chosen = [pairing(section, k, sections) * 2 for k in range(sections)]
            return jnp.stack([(chip + c) * cap for chip in chosen for c in (core, 1 - core)])

        firsts = slots_of(partner)
        blocks = [jax.ShapeDtypeStruct((2 * cap, columns), jnp.bfloat16)] * sections
    else:
        firsts = jnp.zeros((1,), jnp.int32)
        blocks = [jax.ShapeDtypeStruct((device_count * cap, columns), jnp.bfloat16)]
    blocks = pl.pallas_call(
        functools.partial(route_kernel, cap, len(blocks)),
        out_shape=blocks,
        in_specs=[smem] + [vmem] * (mp_devices + 2),
        out_specs=[vmem] * len(blocks),
        compiler_params=pltpu.CompilerParams(vmem_limit_bytes=16 * MIB),
        name="route",
    )(firsts, place.T, projected, *squares)
    if not direct:
        return lax.all_to_all(blocks[0], axes, split_axis=0, concat_axis=0, tiled=True)
    arrived = [blocks[0]] + [
        exchange(blocks[k], "section", k, sections) for k in range(1, sections)
    ]
    passed = pl.pallas_call(
        forward_kernel,
        out_shape=jax.ShapeDtypeStruct((sections * cap, columns), jnp.bfloat16),
        in_specs=[vmem] * sections,
        out_specs=vmem,
        compiler_params=pltpu.CompilerParams(vmem_limit_bytes=8 * MIB),
        name="forward",
    )(*arrived)
    return pl.pallas_call(
        collect_kernel,
        out_shape=jax.ShapeDtypeStruct((device_count * cap, columns), jnp.bfloat16),
        in_specs=[smem] + [vmem] * (sections + 1),
        out_specs=vmem,
        compiler_params=pltpu.CompilerParams(vmem_limit_bytes=8 * MIB),
        name="collect",
    )(slots_of(sender), *arrived, exchange(passed, "tm", 1, 2))


def solution(mesh):
    placed = (
        P(("section", "tm"), None),
        P("section", None),
        P(),
        P(None, None, "mp"),
        P("mp", None),
        P(("section", "tm"), None),
        P(None, "mp"),
    )
    return jax.shard_map(
        local, mesh=mesh, in_specs=placed, out_specs=P(("section", "tm"), "mp"), check_vma=False
    )
```
